32 devices in a mesh: groups: 2 (over y), space: 4 (over z), ens: 2 (over x), chan: 2 (over core).
Axes of the slice: x: 2, y: 2, z: 4, core: 2. Of those that a mesh axis runs over, the one named last changes fastest.
Arguments:
- fields: bfloat16 [4, 8, 768, 256], P(('groups', 'ens'), 'space', None, 'chan'), parts along dimension 0, may hold values from -6 to 6
- cotangent: bfloat16 [4, 8, 768, 256], P(('groups', 'ens'), 'space', None, 'chan'), parts along dimension 0, may hold values from -6 to 6
- band_rows: int32 [8], P('groups'), parts along dimension 0, may hold values from 1 to 2, 6 in all
- tap_shift: int32 [6, 9], replicated, may hold values from -8 to 8
- quad_weight: float32 [6], replicated, may hold values from 1.5 to 6
- legendre: bfloat16 [368, 6, 384], P('space'), may hold values from -0.3125 to 0.3125
- spectral_filter: bfloat16 [2, 384, 256], P(None, None, 'chan'), may hold values from -4 to 4
- tap_weight: bfloat16 [9, 256], P(None, 'chan'), may hold values from -2 to 2
Outputs:
- output: bfloat16 [4, 8, 768, 256], P(('groups', 'ens'), 'space', None, 'chan'), parts along dimension 0
- input_grad: bfloat16 [4, 8, 768, 256], P(('groups', 'ens'), 'space', None, 'chan'), parts along dimension 0
- filter_grad: float32 [4, 384, 256], P('groups', None, 'chan'), parts along dimension 0
- tap_grad: float32 [18, 256], P('groups', 'chan'), parts along dimension 0
The draws below stay inside these ranges and needn't reach their ends.
There are 2 independent parts, one for each index of `groups`. The reference program is written for one: setup_inputs(seed, part) draws one part's arguments, and reference() takes and returns one part's arrays. A program takes and returns all parts, laid end to end along the dimension named above; an argument that names none is the same for every part. Nothing has to cross between parts.
Inputs may be any that keep to these rules, and one draw needn't show every extreme that they name: `band_rows`: entry b is the number of live latitude rows of device b of the space axis, held in its first slots; the entries sum to 6 and some device holds 2.
All inputs are finite; a program needn't handle non-finite values.
Results may differ from the reference program's by a relative error of at most 0.0084.
Values may be sent and summed in bfloat16 or wider, within the bound.
No kernel may reach another device: no remote copies, remote signals or barrier semaphores. Data moves between devices by JAX's collectives and lax.ppermute only.
A program may use at most 256 MiB of HBM per device.

```python
import math
import jax
import jax.numpy as jnp
import numpy as np
from jax import lax

C = 256
LON = 768
M = 368
L = 384
TAPS = 9
ROWS_CAP = 2
LATS = 6
SLOTS = 8
ENS = 2
N_SPACE = 4


def with_ends(values, stream_key, low, top_value):
    longest = values.shape.index(max(values.shape))
    spots = []
    for shift in (0, 1):
        where = [jax.random.randint(jax.random.fold_in(stream_key, axis), (), 0, length) for axis, length in enumerate(values.shape)]
        where[longest] = (where[longest] + shift) % values.shape[longest]
        spots.append(tuple(where))
    return values.at[spots[0]].set(low).at[spots[1]].set(top_value)


def block_scale(key, extent, cuts, smallest, top_value):
    gain, own = 1.0, jax.random.fold_in(key, 6)
    for dim, blocks in cuts:
        draws = jnp.exp(jax.random.uniform(jax.random.fold_in(own, dim), (blocks,), jnp.float32, smallest / len(cuts), top_value / len(cuts)))
        gain = gain * jnp.repeat(draws, extent[dim] // blocks).reshape([-1 if axis == dim else 1 for axis in range(len(extent))])
    return gain


def profile(count, total, most, slope):
    weights = [(1 << 20) // math.isqrt(standing ** slope) + 1 for standing in range(2, count + 1)]
    rest, given = total - most - (count - 1), [1] * (count - 1)
    while rest > 0:
        candidates = [i for i in range(count - 1) if given[i] < most]
        mass, remaining = sum([weights[i] for i in candidates]), rest
        for i in candidates:
            addition = min(most - given[i], max(1, remaining * weights[i] // mass), rest)
            given[i] = given[i] + addition
            rest = rest - addition
    return np.array([most] + given)


def uneven_parts(rng, count, total, most, skew):
    if count == 2:
        one = jax.random.randint(rng, (), max(1, total - most), min(most, total - 1) + 1)
        return jnp.stack([one, total - one])
    tallies = jnp.asarray(profile(count, total, most, skew), jnp.int32)
    pairs = (count - 1) // 2
    source_of, sink = tallies[1:1 + 2 * pairs:2], tallies[2:2 + 2 * pairs:2]
    slack = jnp.minimum(source_of - 1, most - sink)
    shifted = jax.random.randint(jax.random.fold_in(rng, 1), (pairs,), 0, 1 << 20) % (slack + 1)
    tallies = tallies.at[1:1 + 2 * pairs:2].set(source_of - shifted).at[2:2 + 2 * pairs:2].set(sink + shifted)
    return tallies[jax.random.permutation(jax.random.fold_in(rng, 2), count)]


def scatter_about(own_key, dims, scale, most, cuts=(), kind=jnp.bfloat16):
    entries = jax.random.normal(own_key, dims, jnp.float32) * scale
    if len(cuts) > 0:
        entries = block_scale(own_key, dims, cuts, -0.22, 0.18) * entries
    return jnp.clip(entries, min=-most, max=most).astype(kind)


def setup_inputs(seed: int = 0, part: int = 0) -> dict:
    keys = jax.random.split(jax.random.key(seed), 9)
    part_splits = jax.random.split(jax.random.fold_in(keys[8], part), 9)
    fields = scatter_about(part_splits[0], (ENS, SLOTS, LON, C), 1.0, 6.0, ((0, 2), (1, 4), (3, 2)))
    cotangent = scatter_about(part_splits[1], (ENS, SLOTS, LON, C), 1.0, 6.0, ((0, 2), (1, 4), (3, 2)))
    band_rows = uneven_parts(part_splits[2], N_SPACE, LATS, ROWS_CAP, 2).astype(jnp.int32)
    tap_shift = with_ends(jax.random.randint(keys[3], (LATS, TAPS), -8, 9), jax.random.fold_in(keys[3], 1), -8, 8).astype(jnp.int32)
    quad_weight = jnp.clip(jnp.exp(jax.random.uniform(keys[4], (LATS,), jnp.float32, math.log(1.5), math.log(6.0))), 1.5, 6.0)
    legendre = scatter_about(keys[5], (M, LATS, L), L ** -0.5, 0.3125, ((0, 4),))
    spectral_filter = scatter_about(keys[6], (2, L, C), 1.0, 4.0, ((2, 2),))
    tap_weight = scatter_about(keys[7], (TAPS, C), 0.35, 2.0, ((1, 2),))
    return {"fields": fields, "cotangent": cotangent, "band_rows": band_rows, "tap_shift": tap_shift, "quad_weight": quad_weight, "legendre": legendre, "spectral_filter": spectral_filter, "tap_weight": tap_weight}


def gelu_value(values):
    return 0.5 * values * (1.0 + jax.scipy.special.erf(values * 0.7071067811865476))

def gelu_slope(values):
    return 0.5 * (1.0 + jax.scipy.special.erf(values * 0.7071067811865476)) + values * jnp.exp(-0.5 * values * values) * 0.3989422804014327

def fourier_tables(lon_count, mode_count):
    lon_ids = jnp.arange(lon_count, dtype=jnp.int32)
    mode_ids = jnp.arange(mode_count, dtype=jnp.int32)
    phase = (lon_ids[:, None] * mode_ids[None, :] % lon_count).astype(jnp.float32) * (2.0 * math.pi / lon_count)
    factor = 1.0 / math.sqrt(lon_count)
    forward = jnp.stack([jnp.cos(phase) * factor, -jnp.sin(phase) * factor], axis=1)
    weights = jnp.where(mode_ids == 0, 1.0, 2.0).astype(jnp.float32)
    inverse = jnp.transpose(forward, (1, 2, 0)) * weights[None, :, None]
    return (forward.astype(jnp.bfloat16), inverse.astype(jnp.bfloat16))

def rounded_field(values):
    return lax.optimization_barrier(values.astype(jnp.bfloat16)).astype(jnp.float32)

def reference(fields, cotangent, band_rows, tap_shift, quad_weight, legendre, spectral_filter, tap_weight):
    lat_count = LATS
    lon_count = LON
    chan_count = fields.shape[3]
    slot_total = N_SPACE * ROWS_CAP
    starts = jnp.cumsum(band_rows) - band_rows
    slot_ids = jnp.arange(slot_total, dtype=jnp.int32)
    owner = slot_ids // ROWS_CAP
    within = slot_ids % ROWS_CAP
    alive = within < band_rows[owner]
    target = jnp.where(alive, starts[owner] + within, lat_count).astype(jnp.int32)
    slot_of_lat = jnp.zeros((lat_count,), jnp.int32).at[target].set(slot_ids, mode='drop')
    x_live = jnp.take(fields, slot_of_lat, axis=1)
    dy_live = jnp.take(cotangent, slot_of_lat, axis=1)
    forward_tab, inverse_tab = fourier_tables(lon_count, M)
    forward_transform_fn = forward_tab.astype(jnp.float32)
    inverse_transform_fn = inverse_tab.astype(jnp.float32)
    plain_f = legendre.astype(jnp.float32)
    weighted_f = rounded_field(quad_weight[None, :, None].astype(jnp.float32) * plain_f)
    filter_f = spectral_filter.astype(jnp.float32)
    filter_re = filter_f[0][:, None, :]
    filter_im = filter_f[1][:, None, :]
    taps_f = tap_weight.astype(jnp.float32)
    lon_ids = jnp.arange(lon_count, dtype=jnp.int32)
    member_count = fields.shape[0]

    def member(running, inputs):
        x_one, dy_one = inputs
        x_f = x_one.astype(jnp.float32)
        activation_field = rounded_field(gelu_value(x_f))
        output_gradient_field = dy_one.astype(jnp.float32)
        harmonic_coefficients = rounded_field(jnp.einsum('qfb,fhr->hqrb', activation_field, forward_transform_fn))
        spectra = jnp.einsum('kgmc,mgl->klmc', harmonic_coefficients, weighted_f)
        filtered = rounded_field(jnp.stack([spectra[0] * filter_re - spectra[1] * filter_im, spectra[0] * filter_im + spectra[1] * filter_re]))
        synthesis_field = rounded_field(jnp.einsum('klmc,mgl->kgmc', filtered, plain_f))
        spectral_branch_output = jnp.einsum('bdsj,bsx->dxj', synthesis_field, inverse_transform_fn)
        zero_row = jnp.zeros((1, lon_count, chan_count), jnp.float32)
        padded = jnp.concatenate([zero_row, activation_field, zero_row], axis=0)
        disco_out = jnp.zeros((lat_count, lon_count, chan_count), jnp.float32)
        spread = []
        tap_terms = []
        for offset in range(3):
            source = padded[offset:offset + lat_count]
            spread_one = jnp.zeros((lat_count, lon_count, chan_count), jnp.float32)
            for column in range(3):
                tap_index = offset * 3 + column
                shift_col = tap_shift[:, tap_index][:, None]
                index = jnp.broadcast_to(((lon_ids[None, :] + shift_col) % lon_count)[:, :, None], source.shape)
                moved = jnp.take_along_axis(source, index, axis=1)
                disco_out = disco_out + moved * taps_f[tap_index]
                tap_terms.append(lax.optimization_barrier(jnp.sum(moved * output_gradient_field, axis=(0, 1))))
                index_back = jnp.broadcast_to(((lon_ids[None, :] - shift_col) % lon_count)[:, :, None], source.shape)
                spread_one = spread_one + jnp.take_along_axis(output_gradient_field, index_back, axis=1) * taps_f[tap_index]
            spread.append(spread_one)
        output = (x_f + spectral_branch_output + disco_out).astype(jnp.bfloat16)
        synthesis_gradient = rounded_field(jnp.einsum('uqx,znq->zunx', output_gradient_field, inverse_transform_fn))
        grad_filtered = jnp.einsum('kgmc,mgl->klmc', synthesis_gradient, plain_f)
        filter_part = jnp.stack([lax.optimization_barrier(jnp.sum(grad_filtered[0] * spectra[0] + grad_filtered[1] * spectra[1], axis=1)), lax.optimization_barrier(jnp.sum(grad_filtered[1] * spectra[0] - grad_filtered[0] * spectra[1], axis=1))])
        grad_spectra = rounded_field(jnp.stack([grad_filtered[0] * filter_re + grad_filtered[1] * filter_im, grad_filtered[1] * filter_re - grad_filtered[0] * filter_im]))
        coefficient_gradient = rounded_field(jnp.einsum('klmc,mgl->kgmc', grad_spectra, weighted_f))
        spectral_branch_gradient = jnp.einsum('ofsx,wos->fwx', coefficient_gradient, forward_transform_fn)
        grad_disco = spread[1] + jnp.concatenate([spread[0][1:], zero_row], axis=0) + jnp.concatenate([zero_row, spread[2][:-1]], axis=0)
        input_grad = (output_gradient_field + (spectral_branch_gradient + grad_disco) * gelu_slope(x_f)).astype(jnp.bfloat16)
        running = (running[0] + filter_part, running[1] + jnp.stack(tap_terms))
        return (running, (output, input_grad))
    start_sums = (jnp.zeros((2, L, chan_count), jnp.float32), jnp.zeros((TAPS, chan_count), jnp.float32))
    sums, outs = lax.scan(member, start_sums, (x_live, dy_live))
    output = jnp.zeros(fields.shape, jnp.bfloat16).at[:, slot_of_lat].set(outs[0])
    input_grad = jnp.zeros(fields.shape, jnp.bfloat16).at[:, slot_of_lat].set(outs[1])
    return (output, input_grad, sums[0] / member_count, sums[1] / (member_count * lat_count))
```

```python
import functools
import math

import jax
import jax.numpy as jnp
import ml_dtypes
import numpy as np
from jax import lax
from jax.experimental import pallas as pl
from jax.experimental.pallas import tpu as pltpu
from jax.sharding import PartitionSpec as P

F32 = jnp.float32
BF16 = jnp.bfloat16
VMEM = pl.BlockSpec(memory_space=pltpu.VMEM)
SMEM = pl.BlockSpec(memory_space=pltpu.SMEM)
REACH = 8
TAP_ROWS = 16


def gelu_value(values):
    return 0.5 * values * (1.0 + lax.erf(values * 0.7071067811865476))


def gelu_slope(values):
    return (
        0.5 * (1.0 + lax.erf(values * 0.7071067811865476))
        + values * jnp.exp(-0.5 * values * values) * 0.3989422804014327
    )


def round_up(count, step):
    return -(-count // step) * step


def fourier_table(lon_count, blocks, local_modes, padded_modes):
    lon_ids = np.arange(lon_count)
    mode_ids = np.arange(blocks * local_modes)
    phase = (mode_ids[:, None] * lon_ids[None, :] % lon_count) * (2.0 * math.pi / lon_count)
    factor = 1.0 / math.sqrt(lon_count)
    both = np.stack([np.cos(phase), -np.sin(phase)]) * factor
    both = both.reshape(2, blocks, local_modes, lon_count).transpose(1, 0, 2, 3)
    both = np.pad(both, ((0, 0), (0, 0), (0, padded_modes - local_modes), (0, 0)))
    return both.reshape(blocks, 2 * padded_modes, lon_count).astype(ml_dtypes.bfloat16)


def lat_pairs(lat_count):
    return [(a, b) for a in range(lat_count) for b in range(a, lat_count)]


def first_row_of(rows_ref, block, blocks):
    total = jnp.int32(0)
    for other in range(blocks):
        total = total + jnp.where(other < block, rows_ref[other], 0)
    return total


def call(kernel, out_shape, in_specs, args, scratch=(), limit=32, flops=0, moved=0):
    leaves = jax.tree.leaves(out_shape)
    return pl.pallas_call(
        kernel,
        out_shape=out_shape,
        in_specs=in_specs,
        out_specs=jax.tree.map(lambda _: VMEM, out_shape),
        scratch_shapes=list(scratch),
        compiler_params=pltpu.CompilerParams(vmem_limit_bytes=limit * 1024 * 1024),
        cost_estimate=pl.CostEstimate(
            flops=flops,
            bytes_accessed=moved + sum(math.prod(leaf.shape) * leaf.dtype.itemsize for leaf in leaves),
            transcendentals=0,
        ),
    )(*args)


def forward_kernel(blocks, rows_ref, x_ref, dy_ref, table_ref, act_ref, down_ref, up_ref, *outs):
    slots, lon_count, chans = x_ref.shape
    me = lax.axis_index("space")
    step = 64 if lon_count % 64 == 0 else lon_count

    def activate(i, carry):
        part = pl.ds(pl.multiple_of(i * step, step), step)
        for slot in range(slots):
            act_ref[slot, part, :] = gelu_value(x_ref[slot, part, :].astype(F32)).astype(BF16)
        return carry

    lax.fori_loop(0, lon_count // step, activate, 0)
    last = rows_ref[me] - 1
    down_ref[0] = act_ref[0]
    down_ref[1] = dy_ref[0]
    up_ref[0] = act_ref[last]
    up_ref[1] = dy_ref[last]
    source = jnp.concatenate(
        [dy_ref[slot] for slot in range(slots)] + [act_ref[slot] for slot in range(slots)], axis=-1
    )
    for shift in range(blocks):
        block = lax.rem(me + shift, blocks)
        sums = jnp.dot(table_ref[block], source, preferred_element_type=F32).astype(BF16)
        for field in range(2):
            for slot in range(slots):
                at = (field * slots + slot) * chans
                outs[shift][field, slot] = sums[:, at : at + chans]


def prepare_kernel(local_modes, leg_ref, filter_ref, mixer_ref, back_ref, pairs_ref):
    lat_count, padded_modes, _ = leg_ref.shape
    pairs = lat_pairs(lat_count)
    used = len(pairs) * padded_modes
    mode = lax.axis_index("space") * local_modes + lax.broadcasted_iota(
        jnp.int32, (padded_modes, 1), 0
    )
    twice = jnp.where(mode == 0, 1.0, 2.0)
    for index, (a, b) in enumerate(pairs):
        at = index * padded_modes
        pairs_ref[at : at + padded_modes, :] = (
            leg_ref[a].astype(F32) * leg_ref[b].astype(F32) * twice
        ).astype(BF16)
    if pairs_ref.shape[0] > used:
        pairs_ref[used:, :] = jnp.zeros((pairs_ref.shape[0] - used, pairs_ref.shape[1]), BF16)
    both = jnp.concatenate([filter_ref[0], filter_ref[1]], axis=-1)
    mixer_ref[...] = jnp.dot(pairs_ref[...], both, preferred_element_type=F32)

    def turn(i, carry):
        part = pl.ds(pl.multiple_of(i * 128, 128), 128)
        back_ref[:, part] = pairs_ref[part, :].astype(F32).T.astype(BF16)
        return carry

    lax.fori_loop(0, pairs_ref.shape[0] // 128, turn, 0)


def mix_kernel(blocks, lat_count, rows_ref, quad_ref, mixer_ref, back_ref, *refs):
    ins, outs, sums = refs[:blocks], refs[blocks : 2 * blocks], refs[2 * blocks : 3 * blocks]
    coeff, grad, synth, grad_coeff, products, gradient = refs[3 * blocks :]
    slots = ins[0].shape[1]
    padded_modes, chans = coeff.shape[2:]
    me = lax.axis_index("space")
    pairs = lat_pairs(lat_count)
    for shift in range(blocks):
        block = lax.rem(me + (blocks - shift), blocks)
        start = first_row_of(rows_ref, block, blocks)
        for slot in range(slots):
            lat = jnp.minimum(start + slot, lat_count - 1)

            @pl.when(slot < rows_ref[block])
            def _():
                weight = quad_ref[lat]
                for part in range(2):
                    rows = slice(part * padded_modes, (part + 1) * padded_modes)
                    grad[lat, part] = ins[shift][0, slot, rows, :].astype(F32)
                    coeff[lat, part] = ins[shift][1, slot, rows, :].astype(F32) * weight

    def mix(i, carry):
        rows = pl.ds(pl.multiple_of(i * 8, 8), 8)
        a0 = [coeff[lat, 0, rows, :] for lat in range(lat_count)]
        a1 = [coeff[lat, 1, rows, :] for lat in range(lat_count)]
        b0 = [grad[lat, 0, rows, :] for lat in range(lat_count)]
        b1 = [grad[lat, 1, rows, :] for lat in range(lat_count)]
        zero = jnp.zeros((8, chans), F32)
        y0, y1, z0, z1 = ([zero] * lat_count for _ in range(4))
        for index, (a, b) in enumerate(pairs):
            at = pl.ds(pl.multiple_of(index * padded_modes + i * 8, 8), 8)
            real = mixer_ref[at, :chans]
            imag = mixer_ref[at, chans:]
            h0 = h1 = zero
            for p, q in [(a, b)] if a == b else [(a, b), (b, a)]:
                y0[p] = y0[p] + real * a0[q] - imag * a1[q]
                y1[p] = y1[p] + imag * a0[q] + real * a1[q]
                z0[q] = z0[q] + real * b0[p] + imag * b1[p]
                z1[q] = z1[q] + real * b1[p] - imag * b0[p]
                h0 = h0 + b0[p] * a0[q] + b1[p] * a1[q]
                h1 = h1 + b1[p] * a0[q] - b0[p] * a1[q]
            products[at, :chans] = h0
            products[at, chans:] = h1
        for lat in range(lat_count):
            synth[lat, 0, rows, :] = y0[lat]
            synth[lat, 1, rows, :] = y1[lat]
            grad_coeff[lat, 0, rows, :] = z0[lat] * quad_ref[lat]
            grad_coeff[lat, 1, rows, :] = z1[lat] * quad_ref[lat]
        return carry

    lax.fori_loop(0, padded_modes // 8, mix, 0)
    used = len(pairs) * padded_modes
    if products.shape[0] > used:
        products[used:, :] = jnp.zeros((products.shape[0] - used, products.shape[1]), F32)
    gradient[...] = jnp.dot(
        back_ref[...], products[...].astype(BF16), preferred_element_type=F32
    )
    share = gradient.shape[0] // blocks
    for shift in range(blocks):
        block = lax.rem(me + shift, blocks)
        part = gradient[pl.ds(pl.multiple_of(block * share, share), share), :]
        sums[shift][...] = jnp.concatenate([part[:, :chans], part[:, chans:]], axis=0).astype(BF16)
        start = first_row_of(rows_ref, block, blocks)
        for slot in range(slots):
            lat = jnp.minimum(start + slot, lat_count - 1)
            for half in range(2):
                rows = slice(half * padded_modes, (half + 1) * padded_modes)
                outs[shift][0, slot, rows, :] = synth[lat, half].astype(BF16)
                outs[shift][1, slot, rows, :] = grad_coeff[lat, half].astype(BF16)


def disco_kernel(
    blocks, lat_count, rows_ref, shift_ref, x_ref, dy_ref, act_ref, low_ref, high_ref, taps_ref,
    base_ref, slope_ref, base_grad_ref, tap_ref, acts, grads,
):
    slots, lon_count, chans = x_ref.shape
    taps = taps_ref.shape[0]
    me = lax.axis_index("space")
    live = rows_ref[me]
    start = first_row_of(rows_ref, me, blocks)

    def wrapped(target, row, value):
        target[row, REACH : REACH + lon_count, :] = value
        target[row, :REACH, :] = value[lon_count - REACH :, :]
        target[row, REACH + lon_count :, :] = value[:REACH, :]

    wrapped(acts, 0, low_ref[0].astype(F32))
    wrapped(grads, 0, low_ref[1].astype(F32))
    wrapped(acts, slots + 1, high_ref[0].astype(F32))
    wrapped(grads, slots + 1, high_ref[1].astype(F32))
    for slot in range(slots):
        alive = jnp.where(slot < live, 1.0, 0.0)
        wrapped(acts, slot + 1, act_ref[slot].astype(F32))
        wrapped(grads, slot + 1, dy_ref[slot].astype(F32) * alive)
    weights = taps_ref[...].astype(F32)
    step = 32 if lon_count % 32 == 0 else lon_count
    totals = [jnp.zeros((8, chans), F32)] * taps
    for slot in range(slots):
        below = jnp.where(slot + 1 < live, slot + 2, slots + 1)
        rows = [slot, slot + 1, below]
        lat = jnp.clip(start + slot, 0, lat_count - 1)
        lats = [jnp.maximum(lat - 1, 0), lat, jnp.minimum(lat + 1, lat_count - 1)]
        ahead = [REACH + shift_ref[lat, t] for t in range(taps)]
        behind = [REACH - shift_ref[lats[2 - t // 3], t] for t in range(taps)]

        def taps_of(i, totals):
            at = pl.multiple_of(i * step, step)
            part = pl.ds(at, step)
            x = x_ref[slot, part, :].astype(F32)
            dy = grads[slot + 1, pl.ds(pl.multiple_of(REACH + at, 8), step), :]
            out = x
            back = jnp.zeros((step, chans), F32)
            fresh = []
            for t in range(taps):
                moved = acts[rows[t // 3], pl.ds(at + ahead[t], step), :]
                out = out + moved * weights[t : t + 1, :]
                fresh.append(totals[t] + jnp.sum((moved * dy).reshape(step // 8, 8, chans), axis=0))
                back = back + grads[rows[2 - t // 3], pl.ds(at + behind[t], step), :] * weights[
                    t : t + 1, :
                ]
            slope = gelu_slope(x)
            base_ref[slot, part, :] = out
            slope_ref[slot, part, :] = slope
            base_grad_ref[slot, part, :] = dy + back * slope
            return tuple(fresh)

        totals = list(lax.fori_loop(0, lon_count // step, taps_of, tuple(totals)))
    lines = [jnp.sum(total, axis=0, keepdims=True) for total in totals]
    lines.append(jnp.zeros((tap_ref.shape[0] - taps, chans), F32))
    tap_ref[...] = jnp.concatenate(lines, axis=0)


def sum_kernel(tap_ref, *refs):
    parts, out_ref = refs[:-1], refs[-1]
    count = parts[0].shape[0]
    total = parts[0][...].astype(F32)
    for part in parts[1:]:
        total = total + part[...].astype(F32)
    out_ref[:count, :] = total
    out_ref[count:, :] = tap_ref[...]


def member_kernel(lat_count, *refs):
    members = len(refs) - 2
    parts, out_ref, held = refs[:members], refs[-2], refs[-1]
    me = lax.axis_index("ens")
    for shift in range(members):
        held[lax.rem(me + (members - shift), members)] = parts[shift][...]
    total = held[0]
    for member in range(1, members):
        total = total + held[member]
    total = total / members
    count = total.shape[0] - TAP_ROWS
    out_ref[:count, :] = total[:count, :].astype(BF16)
    taps = total[count:, :] / lat_count
    high = taps.astype(BF16)
    out_ref[count : count + TAP_ROWS, :] = high
    out_ref[count + TAP_ROWS :, :] = (taps - high.astype(F32)).astype(BF16)


def spread_kernel(*refs):
    blocks = len(refs) - 3
    parts, filter_ref, tap_ref, held = refs[:blocks], refs[-3], refs[-2], refs[-1]
    me = lax.axis_index("space")
    degrees = filter_ref.shape[1]
    share = degrees // blocks
    for shift in range(blocks):
        block = lax.rem(me + (blocks - shift), blocks)
        part = parts[shift][...].astype(F32)
        rows = pl.ds(pl.multiple_of(block * share, share), share)
        filter_ref[0, rows, :] = part[:share, :]
        filter_ref[1, rows, :] = part[share : 2 * share, :]
        held[block] = part[2 * share : 2 * share + TAP_ROWS, :] + part[2 * share + TAP_ROWS :, :]
    total = held[0]
    for block in range(1, blocks):
        total = total + held[block]
    tap_ref[...] = total[: tap_ref.shape[0], :]


def finish_kernel(
    blocks, rows_ref, table_ref, base_ref, slope_ref, base_grad_ref, *refs
):
    ins, out_ref, grad_ref, source = refs[:blocks], refs[blocks], refs[blocks + 1], refs[blocks + 2]
    slots, lon_count, chans = base_ref.shape
    me = lax.axis_index("space")
    live = rows_ref[me]
    depth = ins[0].shape[2]
    for shift in range(blocks):
        block = lax.rem(me + (blocks - shift), blocks)
        rows = pl.ds(pl.multiple_of(block * depth, depth), depth)
        for field in range(2):
            for slot in range(slots):
                at = (field * slots + slot) * chans
                source[rows, at : at + chans] = ins[shift][field, slot]
    sums = jnp.dot(table_ref[...], source[...], preferred_element_type=F32)
    for slot in range(slots):
        at = slot * chans
        out = base_ref[slot] + sums[:, at : at + chans]
        at = (slots + slot) * chans
        grad = base_grad_ref[slot] + sums[:, at : at + chans] * slope_ref[slot]
        alive = slot < live
        out_ref[slot] = jnp.where(alive, out, 0.0).astype(BF16)
        grad_ref[slot] = jnp.where(alive, grad, 0.0).astype(BF16)


def shifted(values, axis, shift):
    count = lax.axis_size(axis)
    return lax.ppermute(values, axis, [(i, (i + shift) % count) for i in range(count)])


def body(
    fields, cotangent, band_rows, tap_shift, quad_weight, legendre, spectral_filter, tap_weight
):
    blocks = lax.axis_size("space")
    members = lax.axis_size("ens")
    _, slots, lon_count, chans = fields.shape
    local_modes, lat_count, degrees = legendre.shape
    padded_modes = round_up(local_modes, 16)
    depth = 2 * padded_modes
    pairs = len(lat_pairs(lat_count))
    pair_rows = round_up(pairs * padded_modes, 128)
    share = 2 * degrees // blocks
    big = 32 if pair_rows <= 4096 else 60
    shape = jax.ShapeDtypeStruct
    table = fourier_table(lon_count, blocks, local_modes, padded_modes)
    table_in = jnp.asarray(table)
    table_out = jnp.asarray(np.ascontiguousarray(table.reshape(blocks * depth, lon_count).T))
    x, dy = fields[0], cotangent[0]
    field = shape((slots, lon_count, chans), F32)
    coded = shape((2, slots, depth, chans), BF16)
    rim = shape((2, lon_count, chans), BF16)

    act, down, up, *coded_parts = call(
        functools.partial(forward_kernel, blocks),
        [shape(x.shape, BF16), rim, rim] + [coded] * blocks,
        [SMEM, VMEM, VMEM, VMEM],
        (band_rows, x, dy, table_in),
        flops=2 * blocks * depth * lon_count * 2 * slots * chans,
    )
    got = [coded_parts[0]] + [shifted(coded_parts[s], "space", s) for s in range(1, blocks)]
    low = lax.ppermute(up, "space", [(i, i + 1) for i in range(blocks - 1)])
    high = lax.ppermute(down, "space", [(i + 1, i) for i in range(blocks - 1)])

    leg_rows = jnp.pad(
        jnp.transpose(legendre, (1, 0, 2)), ((0, 0), (0, padded_modes - local_modes), (0, 0))
    )
    mixer, back = call(
        functools.partial(prepare_kernel, local_modes),
        [shape((pair_rows, 2 * chans), F32), shape((degrees, pair_rows), BF16)],
        [VMEM, VMEM],
        (leg_rows, spectral_filter),
        scratch=[pltpu.VMEM((pair_rows, degrees), BF16)],
        limit=big,
        flops=2 * pair_rows * degrees * 2 * chans,
    )
    base, slope, base_grad, tap_part = call(
        functools.partial(disco_kernel, blocks, lat_count),
        [field, field, field, shape((TAP_ROWS, chans), F32)],
        [SMEM, SMEM] + [VMEM] * 6,
        (band_rows, tap_shift, x, dy, act, low, high, tap_weight),
        scratch=[pltpu.VMEM((slots + 2, lon_count + 2 * REACH, chans), F32)] * 2,
        flops=60 * slots * lon_count * chans,
    )
    spectral = pltpu.VMEM((lat_count, 2, padded_modes, chans), F32)
    mixed = call(
        functools.partial(mix_kernel, blocks, lat_count),
        [coded] * blocks + [shape((share, chans), BF16)] * blocks,
        [SMEM, SMEM] + [VMEM] * (2 + blocks),
        (band_rows, quad_weight, mixer, back, *got),
        scratch=[spectral] * 4
        + [pltpu.VMEM((pair_rows, 2 * chans), F32), pltpu.VMEM((degrees, 2 * chans), F32)],
        limit=big,
        flops=2 * degrees * pair_rows * 2 * chans,
    )
    back_parts, sum_parts = mixed[:blocks], mixed[blocks:]
    summed = [sum_parts[0]] + [shifted(sum_parts[s], "space", s) for s in range(1, blocks)]
    returned = [back_parts[0]] + [shifted(back_parts[s], "space", s) for s in range(1, blocks)]
    own = call(
        sum_kernel,
        shape((share + TAP_ROWS, chans), F32),
        [VMEM] * (1 + blocks),
        (tap_part, *summed),
    )
    by_member = [own] + [shifted(own, "ens", s) for s in range(1, members)]
    final = call(
        functools.partial(member_kernel, lat_count),
        shape((share + 2 * TAP_ROWS, chans), BF16),
        [VMEM] * members,
        by_member,
        scratch=[pltpu.VMEM((members, share + TAP_ROWS, chans), F32)],
    )
    spread = [final] + [shifted(final, "space", s) for s in range(1, blocks)]
    output, input_grad = call(
        functools.partial(finish_kernel, blocks),
        [shape(x.shape, BF16)] * 2,
        [SMEM] + [VMEM] * (4 + blocks),
        (band_rows, table_out, base, slope, base_grad, *returned),
        scratch=[pltpu.VMEM((blocks * depth, 2 * slots * chans), BF16)],
        flops=2 * blocks * depth * lon_count * 2 * slots * chans,
    )
    filter_grad, tap_grad = call(
        spread_kernel,
        [shape((2, degrees, chans), F32), shape((tap_weight.shape[0], chans), F32)],
        [VMEM] * blocks,
        spread,
        scratch=[pltpu.VMEM((blocks, TAP_ROWS, chans), F32)],
    )
    return (output[None], input_grad[None], filter_grad, tap_grad)


def solution(mesh):
    in_specs = (
        P(("groups", "ens"), "space", None, "chan"),
        P(("groups", "ens"), "space", None, "chan"),
        P("groups"),
        P(),
        P(),
        P("space", None, None),
        P(None, None, "chan"),
        P(None, "chan"),
    )
    out_specs = (
        P(("groups", "ens"), "space", None, "chan"),
        P(("groups", "ens"), "space", None, "chan"),
        P("groups", None, "chan"),
        P("groups", "chan"),
    )
    return jax.shard_map(body, mesh=mesh, in_specs=in_specs, out_specs=out_specs, check_vma=False)
```

```python
import functools
import math

import jax
import jax.numpy as jnp
import ml_dtypes
import numpy as np
from jax import lax
from jax.experimental import pallas as pl
from jax.experimental.pallas import tpu as pltpu
from jax.sharding import PartitionSpec as P

F32 = jnp.float32
BF16 = jnp.bfloat16
VMEM = pl.BlockSpec(memory_space=pltpu.VMEM)
SMEM = pl.BlockSpec(memory_space=pltpu.SMEM)
HBM = pl.BlockSpec(memory_space=pltpu.HBM)
REACH = 8
TAP_ROWS = 16


def gelu_value(values):
    return 0.5 * values * (1.0 + lax.erf(values * 0.7071067811865476))


def gelu_slope(values):
    return (
        0.5 * (1.0 + lax.erf(values * 0.7071067811865476))
        + values * jnp.exp(-0.5 * values * values) * 0.3989422804014327
    )


def round_up(count, step):
    return -(-count // step) * step


def fourier_table(lon_count, blocks, local_modes, padded_modes):
    lon_ids = np.arange(lon_count)
    mode_ids = np.arange(blocks * local_modes)
    phase = (mode_ids[:, None] * lon_ids[None, :] % lon_count) * (2.0 * math.pi / lon_count)
    factor = 1.0 / math.sqrt(lon_count)
    both = np.stack([np.cos(phase), -np.sin(phase)]) * factor
    both = both.reshape(2, blocks, local_modes, lon_count).transpose(1, 0, 2, 3)
    both = np.pad(both, ((0, 0), (0, 0), (0, padded_modes - local_modes), (0, 0)))
    return both.reshape(blocks, 2 * padded_modes, lon_count).astype(ml_dtypes.bfloat16)


def lat_pairs(lat_count):
    return [(a, b) for a in range(lat_count) for b in range(a, lat_count)]


def first_row_of(rows_ref, block, blocks):
    total = jnp.int32(0)
    for other in range(blocks):
        total = total + jnp.where(other < block, rows_ref[other], 0)
    return total


def call(kernel, out_shape, in_specs, args, scratch=(), limit=32, flops=0, moved=1024):
    return pl.pallas_call(
        kernel,
        out_shape=out_shape,
        in_specs=in_specs,
        out_specs=jax.tree.map(lambda _: VMEM, out_shape),
        scratch_shapes=list(scratch),
        compiler_params=pltpu.CompilerParams(vmem_limit_bytes=limit * 1024 * 1024),
        cost_estimate=pl.CostEstimate(flops=flops, bytes_accessed=moved, transcendentals=0),
    )(*args)


def forward_kernel(
    blocks, rows_ref, x_hbm, dy_hbm, table_hbm, act_ref, *refs
):
    outs, (down_ref, up_ref, x_ref, dy_ref, table_ref, sems) = refs[:blocks], refs[blocks:]
    slots, lon_count, chans = x_ref.shape
    me = lax.axis_index("space")
    step = 64 if lon_count % 64 == 0 else lon_count
    loads = [
        pltpu.make_async_copy(source, target, sems.at[i])
        for i, (source, target) in enumerate(
            [(x_hbm, x_ref), (dy_hbm, dy_ref), (table_hbm, table_ref)]
        )
    ]
    for load in loads:
        load.start()
    loads[0].wait()

    def activate(i, carry):
        part = pl.ds(pl.multiple_of(i * step, step), step)
        for slot in range(slots):
            act_ref[slot, part, :] = gelu_value(x_ref[slot, part, :].astype(F32)).astype(BF16)
        return carry

    lax.fori_loop(0, lon_count // step, activate, 0)
    loads[1].wait()
    last = rows_ref[me] - 1
    down_ref[0] = act_ref[0]
    down_ref[1] = dy_ref[0]
    up_ref[0] = act_ref[last]
    up_ref[1] = dy_ref[last]
    source = jnp.concatenate(
        [dy_ref[slot] for slot in range(slots)] + [act_ref[slot] for slot in range(slots)], axis=-1
    )
    loads[2].wait()
    for shift in range(blocks):
        block = jnp.bitwise_xor(me, shift)
        sums = jnp.dot(table_ref[block], source, preferred_element_type=F32).astype(BF16)
        for field in range(2):
            for slot in range(slots):
                at = (field * slots + slot) * chans
                outs[shift][field, slot] = sums[:, at : at + chans]


def prepare_kernel(local_modes, leg_ref, filter_ref, mixer_ref, back_ref, pairs_ref):
    lat_count, padded_modes, _ = leg_ref.shape
    pairs = lat_pairs(lat_count)
    used = len(pairs) * padded_modes
    mode = lax.axis_index("space") * local_modes + lax.broadcasted_iota(
        jnp.int32, (padded_modes, 1), 0
    )
    twice = jnp.where(mode == 0, 1.0, 2.0)
    for index, (a, b) in enumerate(pairs):
        at = index * padded_modes
        pairs_ref[at : at + padded_modes, :] = (
            leg_ref[a].astype(F32) * leg_ref[b].astype(F32) * twice
        ).astype(BF16)
    if pairs_ref.shape[0] > used:
        pairs_ref[used:, :] = jnp.zeros((pairs_ref.shape[0] - used, pairs_ref.shape[1]), BF16)
    both = jnp.concatenate([filter_ref[0], filter_ref[1]], axis=-1)
    mixer_ref[...] = jnp.dot(pairs_ref[...], both, preferred_element_type=F32)

    def turn(i, carry):
        part = pl.ds(pl.multiple_of(i * 128, 128), 128)
        back_ref[:, part] = pairs_ref[part, :].astype(F32).T.astype(BF16)
        return carry

    lax.fori_loop(0, pairs_ref.shape[0] // 128, turn, 0)


def mix_kernel(blocks, lat_count, rows_ref, quad_ref, mixer_ref, back_ref, *refs):
    ins, outs = refs[:blocks], refs[blocks : 2 * blocks]
    keep_ref, send_ref, coeff, grad, synth, grad_coeff, products, gradient = refs[2 * blocks :]
    slots = ins[0].shape[1]
    padded_modes, chans = coeff.shape[2:]
    me = lax.axis_index("space")
    pairs = lat_pairs(lat_count)
    for shift in range(blocks):
        block = jnp.bitwise_xor(me, shift)
        start = first_row_of(rows_ref, block, blocks)
        for slot in range(slots):
            lat = jnp.minimum(start + slot, lat_count - 1)

            @pl.when(slot < rows_ref[block])
            def _():
                weight = quad_ref[lat]
                for part in range(2):
                    rows = slice(part * padded_modes, (part + 1) * padded_modes)
                    grad[lat, part] = ins[shift][0, slot, rows, :].astype(F32)
                    coeff[lat, part] = ins[shift][1, slot, rows, :].astype(F32) * weight

    def mix(i, carry):
        rows = pl.ds(pl.multiple_of(i * 8, 8), 8)
        a0 = [coeff[lat, 0, rows, :] for lat in range(lat_count)]
        a1 = [coeff[lat, 1, rows, :] for lat in range(lat_count)]
        b0 = [grad[lat, 0, rows, :] for lat in range(lat_count)]
        b1 = [grad[lat, 1, rows, :] for lat in range(lat_count)]
        zero = jnp.zeros((8, chans), F32)
        y0, y1, z0, z1 = ([zero] * lat_count for _ in range(4))
        for index, (a, b) in enumerate(pairs):
            at = pl.ds(pl.multiple_of(index * padded_modes + i * 8, 8), 8)
            real = mixer_ref[at, :chans]
            imag = mixer_ref[at, chans:]
            h0 = h1 = zero
            for p, q in [(a, b)] if a == b else [(a, b), (b, a)]:
                y0[p] = y0[p] + real * a0[q] - imag * a1[q]
                y1[p] = y1[p] + imag * a0[q] + real * a1[q]
                z0[q] = z0[q] + real * b0[p] + imag * b1[p]
                z1[q] = z1[q] + real * b1[p] - imag * b0[p]
                h0 = h0 + b0[p] * a0[q] + b1[p] * a1[q]
                h1 = h1 + b1[p] * a0[q] - b0[p] * a1[q]
            products[at, :chans] = h0
            products[at, chans:] = h1
        for lat in range(lat_count):
            synth[lat, 0, rows, :] = y0[lat]
            synth[lat, 1, rows, :] = y1[lat]
            grad_coeff[lat, 0, rows, :] = z0[lat] * quad_ref[lat]
            grad_coeff[lat, 1, rows, :] = z1[lat] * quad_ref[lat]
        return carry

    lax.fori_loop(0, padded_modes // 8, mix, 0)
    used = len(pairs) * padded_modes
    if products.shape[0] > used:
        products[used:, :] = jnp.zeros((products.shape[0] - used, products.shape[1]), F32)
    gradient[...] = jnp.dot(
        back_ref[...], products[...].astype(BF16), preferred_element_type=F32
    )
    half = gradient.shape[0] // 2
    upper = jnp.where(jnp.bitwise_and(me, blocks // 2) != 0, 1, 0)
    for target, which in ((keep_ref, upper), (send_ref, 1 - upper)):
        part = gradient[pl.ds(pl.multiple_of(which * half, half), half), :]
        both = jnp.concatenate([part[:, :chans], part[:, chans:]], axis=0)
        target[...] = both.astype(target.dtype)
    for shift in range(blocks):
        block = jnp.bitwise_xor(me, shift)
        start = first_row_of(rows_ref, block, blocks)
        for slot in range(slots):
            lat = jnp.minimum(start + slot, lat_count - 1)
            for half in range(2):
                rows = slice(half * padded_modes, (half + 1) * padded_modes)
                outs[shift][0, slot, rows, :] = synth[lat, half].astype(BF16)
                outs[shift][1, slot, rows, :] = grad_coeff[lat, half].astype(BF16)


def disco_kernel(
    blocks, lat_count, rows_ref, shift_ref, x_ref, dy_ref, act_ref, low_ref, high_ref, taps_ref,
    base_ref, slope_ref, base_grad_ref, tap_ref, acts, grads,
):
    slots, lon_count, chans = x_ref.shape
    taps = taps_ref.shape[0]
    me = lax.axis_index("space")
    live = rows_ref[me]
    start = first_row_of(rows_ref, me, blocks)

    def wrapped(target, row, value):
        target[row, REACH : REACH + lon_count, :] = value
        target[row, :REACH, :] = value[lon_count - REACH :, :]
        target[row, REACH + lon_count :, :] = value[:REACH, :]

    wrapped(acts, 0, low_ref[0].astype(F32))
    wrapped(grads, 0, low_ref[1].astype(F32))
    wrapped(acts, slots + 1, high_ref[0].astype(F32))
    wrapped(grads, slots + 1, high_ref[1].astype(F32))
    for slot in range(slots):
        alive = jnp.where(slot < live, 1.0, 0.0)
        wrapped(acts, slot + 1, act_ref[slot].astype(F32))
        wrapped(grads, slot + 1, dy_ref[slot].astype(F32) * alive)
    weights = taps_ref[...].astype(F32)
    step = 32 if lon_count % 32 == 0 else lon_count
    totals = [jnp.zeros((8, chans), F32)] * taps
    for slot in range(slots):
        below = jnp.where(slot + 1 < live, slot + 2, slots + 1)
        rows = [slot, slot + 1, below]
        lat = jnp.clip(start + slot, 0, lat_count - 1)
        lats = [jnp.maximum(lat - 1, 0), lat, jnp.minimum(lat + 1, lat_count - 1)]
        ahead = [REACH + shift_ref[lat, t] for t in range(taps)]
        behind = [REACH - shift_ref[lats[2 - t // 3], t] for t in range(taps)]

        def taps_of(i, totals):
            at = pl.multiple_of(i * step, step)
            part = pl.ds(at, step)
            x = x_ref[slot, part, :].astype(F32)
            dy = grads[slot + 1, pl.ds(pl.multiple_of(REACH + at, 8), step), :]
            out = x
            back = jnp.zeros((step, chans), F32)
            fresh = []
            for t in range(taps):
                moved = acts[rows[t // 3], pl.ds(at + ahead[t], step), :]
                out = out + moved * weights[t : t + 1, :]
                fresh.append(totals[t] + jnp.sum((moved * dy).reshape(step // 8, 8, chans), axis=0))
                back = back + grads[rows[2 - t // 3], pl.ds(at + behind[t], step), :] * weights[
                    t : t + 1, :
                ]
            slope = gelu_slope(x)
            base_ref[slot, part, :] = out
            slope_ref[slot, part, :] = slope
            base_grad_ref[slot, part, :] = dy + back * slope
            return tuple(fresh)

        totals = list(lax.fori_loop(0, lon_count // step, taps_of, tuple(totals)))
    lines = [jnp.sum(total, axis=0, keepdims=True) for total in totals]
    lines.append(jnp.zeros((tap_ref.shape[0] - taps, chans), F32))
    tap_ref[...] = jnp.concatenate(lines, axis=0)


def split_taps(taps, out_ref, count):
    high = taps.astype(BF16)
    out_ref[count : count + TAP_ROWS, :] = high
    out_ref[count + TAP_ROWS :, :] = (taps - high.astype(F32)).astype(BF16)


def joined_taps(rows):
    return rows[-2 * TAP_ROWS : -TAP_ROWS, :] + rows[-TAP_ROWS:, :]


def halve_kernel(distance, kept_ref, got_ref, keep_ref, send_ref, total):
    total[...] = kept_ref[...] + got_ref[...].astype(F32)
    rows = total.shape[0] // 2
    half = rows // 2
    upper = jnp.where(jnp.bitwise_and(lax.axis_index("space"), distance) != 0, half, 0)
    for target, at in ((keep_ref, upper), (send_ref, half - upper)):
        both = [
            total[pl.ds(pl.multiple_of(part * rows + at, 8), half), :] for part in range(2)
        ]
        target[...] = jnp.concatenate(both, axis=0).astype(target.dtype)


def own_kernel(kept_ref, got_ref, tap_ref, out_ref):
    count = kept_ref.shape[0]
    out_ref[:count, :] = (kept_ref[...] + got_ref[...].astype(F32)).astype(BF16)
    split_taps(tap_ref[...], out_ref, count)


def member_kernel(lat_count, *refs):
    members = len(refs) - 2
    parts, out_ref, held = refs[:members], refs[-2], refs[-1]
    me = lax.axis_index("ens")
    count = out_ref.shape[0] - 2 * TAP_ROWS
    for shift in range(members):
        at = lax.rem(me + (members - shift), members)
        part = parts[shift][...].astype(F32)
        held[at, :count, :] = part[:count, :]
        held[at, count:, :] = joined_taps(part)
    total = held[0]
    for member in range(1, members):
        total = total + held[member]
    total = total / members
    out_ref[:count, :] = total[:count, :].astype(BF16)
    split_taps(total[count:, :] / lat_count, out_ref, count)


def spread_kernel(*refs):
    parts, (filter_ref, tap_ref, held) = refs[:-3], refs[-3:]
    me = lax.axis_index("space")
    blocks = len(parts)
    share = filter_ref.shape[1] // blocks
    for shift in range(blocks):
        block = jnp.bitwise_xor(me, shift)
        part = parts[shift][...].astype(F32)
        at = pl.ds(pl.multiple_of(block * share, share), share)
        filter_ref[0, at, :] = part[:share, :]
        filter_ref[1, at, :] = part[share : 2 * share, :]
        held[block] = joined_taps(part)
    total = held[0]
    for block in range(1, blocks):
        total = total + held[block]
    tap_ref[...] = total[: tap_ref.shape[0], :]


def finish_kernel(
    blocks, rows_ref, table_ref, base_ref, slope_ref, base_grad_ref, *refs
):
    ins, out_ref, grad_ref, source = refs[:blocks], refs[blocks], refs[blocks + 1], refs[blocks + 2]
    slots, lon_count, chans = base_ref.shape
    me = lax.axis_index("space")
    live = rows_ref[me]
    depth = ins[0].shape[2]
    for shift in range(blocks):
        block = jnp.bitwise_xor(me, shift)
        rows = pl.ds(pl.multiple_of(block * depth, depth), depth)
        for field in range(2):
            for slot in range(slots):
                at = (field * slots + slot) * chans
                source[rows, at : at + chans] = ins[shift][field, slot]
    sums = jnp.dot(table_ref[...], source[...], preferred_element_type=F32)
    for slot in range(slots):
        at = slot * chans
        out = base_ref[slot] + sums[:, at : at + chans]
        at = (slots + slot) * chans
        grad = base_grad_ref[slot] + sums[:, at : at + chans] * slope_ref[slot]
        alive = slot < live
        out_ref[slot] = jnp.where(alive, out, 0.0).astype(BF16)
        grad_ref[slot] = jnp.where(alive, grad, 0.0).astype(BF16)


def shifted(values, axis, shift):
    count = lax.axis_size(axis)
    return lax.ppermute(values, axis, [(i, (i + shift) % count) for i in range(count)])


def crossed(values, distance):
    count = lax.axis_size("space")
    return lax.ppermute(values, "space", [(i, i ^ distance) for i in range(count)])


def crossed_all(parts, distances):
    return {s: crossed(parts[s], s) for s in distances}


def body(
    fields, cotangent, band_rows, tap_shift, quad_weight, legendre, spectral_filter, tap_weight
):
    blocks = lax.axis_size("space")
    members = lax.axis_size("ens")
    _, slots, lon_count, chans = fields.shape
    local_modes, lat_count, degrees = legendre.shape
    padded_modes = round_up(local_modes, 16)
    depth = 2 * padded_modes
    pairs = len(lat_pairs(lat_count))
    pair_rows = round_up(pairs * padded_modes, 128)
    share = 2 * degrees // blocks
    big = 32 if pair_rows <= 4096 else 60
    shape = jax.ShapeDtypeStruct
    table = fourier_table(lon_count, blocks, local_modes, padded_modes)
    table_in = jnp.asarray(table)
    table_out = jnp.asarray(np.ascontiguousarray(table.reshape(blocks * depth, lon_count).T))
    x, dy = fields[0], cotangent[0]
    field = shape((slots, lon_count, chans), F32)
    coded = shape((2, slots, depth, chans), BF16)
    rim = shape((2, lon_count, chans), BF16)

    act, *coded_parts, down, up = call(
        functools.partial(forward_kernel, blocks),
        [shape(x.shape, BF16)] + [coded] * blocks + [rim] * 2,
        [SMEM, HBM, HBM, HBM],
        (band_rows, x, dy, table_in),
        scratch=[
            pltpu.VMEM(x.shape, BF16),
            pltpu.VMEM(dy.shape, BF16),
            pltpu.VMEM(table.shape, BF16),
            pltpu.SemaphoreType.DMA((3,)),
        ],
        limit=60,
        flops=2 * blocks * depth * lon_count * 2 * slots * chans,
    )
    far = list(range(blocks - 1, 0, -1))
    got = [coded_parts[0], *reversed(crossed_all(coded_parts, far).values())]
    leg_rows = jnp.pad(
        jnp.transpose(legendre, (1, 0, 2)), ((0, 0), (0, padded_modes - local_modes), (0, 0))
    )
    mixer, back = call(
        functools.partial(prepare_kernel, local_modes),
        [shape((pair_rows, 2 * chans), F32), shape((degrees, pair_rows), BF16)],
        [VMEM, VMEM],
        (leg_rows, spectral_filter),
        scratch=[pltpu.VMEM((pair_rows, degrees), BF16)],
        limit=big,
        flops=2 * pair_rows * degrees * 2 * chans,
        moved=8 * pair_rows * chans,
    )
    down, up, got, mixer = lax.optimization_barrier((down, up, got, mixer))
    low = lax.ppermute(up, "space", [(i, i + 1) for i in range(blocks - 1)])
    high = lax.ppermute(down, "space", [(i + 1, i) for i in range(blocks - 1)])
    spectral = pltpu.VMEM((lat_count, 2, padded_modes, chans), F32)
    mixed = call(
        functools.partial(mix_kernel, blocks, lat_count),
        [coded] * blocks + [shape((degrees, chans), F32), shape((degrees, chans), BF16)],
        [SMEM, SMEM] + [VMEM] * (2 + blocks),
        (band_rows, quad_weight, mixer, back, *got),
        scratch=[spectral] * 4
        + [pltpu.VMEM((pair_rows, 2 * chans), F32), pltpu.VMEM((degrees, 2 * chans), F32)],
        limit=big,
        flops=2 * degrees * pair_rows * 2 * chans,
    )
    back_parts, keep, send = mixed[:blocks], mixed[blocks], mixed[blocks + 1]
    distance = blocks // 2
    got_sums = crossed(send, distance)
    near = crossed(back_parts[1], 1)
    far_parts, got_sums = lax.optimization_barrier((list(back_parts[2:]), got_sums))
    returned = [back_parts[0], near]
    returned += reversed(crossed_all([None, None, *far_parts], far[:-1]).values())
    base, slope, base_grad, tap_part = call(
        functools.partial(disco_kernel, blocks, lat_count),
        [field, field, field, shape((TAP_ROWS, chans), F32)],
        [SMEM, SMEM] + [VMEM] * 6,
        (band_rows, tap_shift, x, dy, act, low, high, tap_weight),
        scratch=[pltpu.VMEM((slots + 2, lon_count + 2 * REACH, chans), F32)] * 2,
    )
    while distance > 1:
        distance //= 2
        rows = keep.shape[0] // 2
        keep, send = call(
            functools.partial(halve_kernel, distance),
            [shape((rows, chans), F32), shape((rows, chans), BF16)],
            [VMEM, VMEM],
            (keep, got_sums),
            scratch=[pltpu.VMEM(keep.shape, F32)],
        )
        got_sums = crossed(send, distance)
    got_sums, returned[1] = lax.optimization_barrier((got_sums, returned[1]))
    own = call(
        own_kernel,
        shape((share + 2 * TAP_ROWS, chans), BF16),
        [VMEM] * 3,
        (keep, got_sums, tap_part),
    )
    by_member = [own] + [shifted(own, "ens", s) for s in range(1, members)]
    final = call(
        functools.partial(member_kernel, lat_count),
        shape((share + 2 * TAP_ROWS, chans), BF16),
        [VMEM] * members,
        by_member,
        scratch=[pltpu.VMEM((members, share + TAP_ROWS, chans), F32)],
    )
    spread = [final] + [crossed(final, s) for s in range(1, blocks)]
    output, input_grad = call(
        functools.partial(finish_kernel, blocks),
        [shape(x.shape, BF16)] * 2,
        [SMEM] + [VMEM] * (4 + blocks),
        (band_rows, table_out, base, slope, base_grad, *returned),
        scratch=[pltpu.VMEM((blocks * depth, 2 * slots * chans), BF16)],
        flops=2 * blocks * depth * lon_count * 2 * slots * chans,
    )
    filter_grad, tap_grad = call(
        spread_kernel,
        [shape((2, degrees, chans), F32), shape((tap_weight.shape[0], chans), F32)],
        [VMEM] * blocks,
        spread,
        scratch=[pltpu.VMEM((blocks, TAP_ROWS, chans), F32)],
    )
    return (output[None], input_grad[None], filter_grad, tap_grad)


def solution(mesh):
    in_specs = (
        P(("groups", "ens"), "space", None, "chan"),
        P(("groups", "ens"), "space", None, "chan"),
        P("groups"),
        P(),
        P(),
        P("space", None, None),
        P(None, None, "chan"),
        P(None, "chan"),
    )
    out_specs = (
        P(("groups", "ens"), "space", None, "chan"),
        P(("groups", "ens"), "space", None, "chan"),
        P("groups", None, "chan"),
        P("groups", "chan"),
    )
    return jax.shard_map(body, mesh=mesh, in_specs=in_specs, out_specs=out_specs, check_vma=False)
```

```python
import functools
import math

import jax
import jax.numpy as jnp
import ml_dtypes
import numpy as np
from jax import lax
from jax.experimental import pallas as pl
from jax.experimental.pallas import tpu as pltpu
from jax.sharding import PartitionSpec as P

F32 = jnp.float32
BF16 = jnp.bfloat16
VMEM = pl.BlockSpec(memory_space=pltpu.VMEM)
SMEM = pl.BlockSpec(memory_space=pltpu.SMEM)
HBM = pl.BlockSpec(memory_space=pltpu.HBM)
REACH = 8
TAP_ROWS = 16


def gelu_value(values):
    return 0.5 * values * (1.0 + lax.erf(values * 0.7071067811865476))


def gelu_slope(values):
    return (
        0.5 * (1.0 + lax.erf(values * 0.7071067811865476))
        + values * jnp.exp(-0.5 * values * values) * 0.3989422804014327
    )


def round_up(count, step):
    return -(-count // step) * step


def fourier_table(lon_count, blocks, local_modes, depth):
    lon_ids = np.arange(lon_count)
    mode_ids = np.arange(blocks * local_modes)
    phase = (mode_ids[:, None] * lon_ids[None, :] % lon_count) * (2.0 * math.pi / lon_count)
    factor = 1.0 / math.sqrt(lon_count)
    both = np.stack([np.cos(phase), -np.sin(phase)]) * factor
    both = both.reshape(2, blocks, local_modes, lon_count).transpose(1, 0, 2, 3)
    both = both.reshape(blocks, 2 * local_modes, lon_count)
    both = np.pad(both, ((0, 0), (0, depth - 2 * local_modes), (0, 0)))
    return both.astype(ml_dtypes.bfloat16)


def lat_pairs(lat_count):
    return [(a, b) for a in range(lat_count) for b in range(a, lat_count)]


def first_row_of(rows_ref, block, blocks):
    total = jnp.int32(0)
    for other in range(blocks):
        total = total + jnp.where(other < block, rows_ref[other], 0)
    return total


def call(kernel, out_shape, in_specs, args, scratch=(), limit=32, flops=0, moved=1024):
    return pl.pallas_call(
        kernel,
        out_shape=out_shape,
        in_specs=in_specs,
        out_specs=jax.tree.map(lambda _: VMEM, out_shape),
        scratch_shapes=list(scratch),
        compiler_params=pltpu.CompilerParams(vmem_limit_bytes=limit * 1024 * 1024),
        cost_estimate=pl.CostEstimate(flops=flops, bytes_accessed=moved, transcendentals=0),
    )(*args)


def activate(x_ref, act_ref):
    slots, lon_count, _ = x_ref.shape
    step = 64 if lon_count % 64 == 0 else lon_count

    def run(i, carry):
        part = pl.ds(pl.multiple_of(i * step, step), step)
        for slot in range(slots):
            act_ref[slot, part, :] = gelu_value(x_ref[slot, part, :].astype(F32)).astype(BF16)
        return carry

    lax.fori_loop(0, lon_count // step, run, 0)


def forward_kernel(blocks, x_hbm, dy_hbm, table_hbm, *refs):
    outs, (x_ref, dy_ref, table_ref, act_ref, sems) = refs[:blocks], refs[blocks:]
    slots, _, chans = x_ref.shape
    me = lax.axis_index("space")
    loads = [
        pltpu.make_async_copy(source, target, sems.at[i])
        for i, (source, target) in enumerate(
            [(x_hbm, x_ref), (dy_hbm, dy_ref), (table_hbm, table_ref)]
        )
    ]
    for load in loads:
        load.start()
    loads[0].wait()
    activate(x_ref, act_ref)
    loads[1].wait()
    source = jnp.concatenate(
        [dy_ref[slot] for slot in range(slots)] + [act_ref[slot] for slot in range(slots)], axis=-1
    )
    loads[2].wait()
    for shift in range(blocks):
        block = jnp.bitwise_xor(me, shift)
        sums = jnp.dot(table_ref[block], source, preferred_element_type=F32)
        columns = [sums[:, at * chans : (at + 1) * chans] for at in range(2 * slots)]
        outs[shift][...] = jnp.concatenate(columns, axis=0).astype(BF16)


def prepare_kernel(
    local_modes, rows_ref, leg_ref, filter_ref, x_ref, dy_ref,
    mixer_ref, back_ref, act_ref, first_rim, second_rim, pairs_ref,
):
    me = lax.axis_index("space")
    activate(x_ref, act_ref)
    last = rows_ref[me] - 1
    odd = jnp.bitwise_and(me, 1)
    for rim_ref, row in ((first_rim, last * (1 - odd)), (second_rim, last * odd)):
        rim_ref[0] = act_ref[row]
        rim_ref[1] = dy_ref[row]
    lat_count, padded_modes, _ = leg_ref.shape
    pairs = lat_pairs(lat_count)
    used = len(pairs) * padded_modes
    mode = me * local_modes + lax.broadcasted_iota(
        jnp.int32, (padded_modes, 1), 0
    )
    twice = jnp.where(mode == 0, 1.0, 2.0)
    for index, (a, b) in enumerate(pairs):
        at = index * padded_modes
        pairs_ref[at : at + padded_modes, :] = (
            leg_ref[a].astype(F32) * leg_ref[b].astype(F32) * twice
        ).astype(BF16)
    if pairs_ref.shape[0] > used:
        pairs_ref[used:, :] = jnp.zeros((pairs_ref.shape[0] - used, pairs_ref.shape[1]), BF16)
    both = jnp.concatenate([filter_ref[0], filter_ref[1]], axis=-1)
    mixer_ref[...] = jnp.dot(pairs_ref[...], both, preferred_element_type=F32)

    def turn(i, carry):
        part = pl.ds(pl.multiple_of(i * 128, 128), 128)
        back_ref[:, part] = pairs_ref[part, :].astype(F32).T.astype(BF16)
        return carry

    lax.fori_loop(0, pairs_ref.shape[0] // 128, turn, 0)


def mix_kernel(blocks, slots, lat_count, local_modes, rows_ref, quad_ref, mixer_ref, back_ref, *refs):
    ins, outs = refs[:blocks], refs[blocks : 2 * blocks]
    keep_ref, send_ref, coeff, grad, synth, grad_coeff, products, gradient, wide = refs[2 * blocks :]
    padded_modes, chans = coeff.shape[2:]
    me = lax.axis_index("space")
    pairs = lat_pairs(lat_count)
    depth = wide.shape[1] // (2 * slots)
    padding = padded_modes - local_modes
    if padding > 0:
        zeros = jnp.zeros((padding, chans), F32)
        for lat in range(lat_count):
            for part in range(2):
                coeff[lat, part, local_modes:, :] = zeros
                grad[lat, part, local_modes:, :] = zeros

    def rows_at(field, slot, part):
        at = (field * slots + slot) * depth + part * local_modes
        return slice(at, at + local_modes)

    for shift in range(blocks):
        block = jnp.bitwise_xor(me, shift)
        start = first_row_of(rows_ref, block, blocks)
        wide[shift] = ins[shift][...].astype(F32)
        for slot in range(slots):
            lat = jnp.minimum(start + slot, lat_count - 1)

            @pl.when(slot < rows_ref[block])
            def _():
                weight = quad_ref[lat]
                for part in range(2):
                    grad[lat, part, :local_modes, :] = wide[shift, rows_at(0, slot, part), :]
                    coeff[lat, part, :local_modes, :] = (
                        wide[shift, rows_at(1, slot, part), :] * weight
                    )

    def mix(i, carry):
        rows = pl.ds(pl.multiple_of(i * 8, 8), 8)
        a0 = [coeff[lat, 0, rows, :] for lat in range(lat_count)]
        a1 = [coeff[lat, 1, rows, :] for lat in range(lat_count)]
        b0 = [grad[lat, 0, rows, :] for lat in range(lat_count)]
        b1 = [grad[lat, 1, rows, :] for lat in range(lat_count)]
        zero = jnp.zeros((8, chans), F32)
        y0, y1, z0, z1 = ([zero] * lat_count for _ in range(4))
        for index, (a, b) in enumerate(pairs):
            at = pl.ds(pl.multiple_of(index * padded_modes + i * 8, 8), 8)
            real = mixer_ref[at, :chans]
            imag = mixer_ref[at, chans:]
            h0 = h1 = zero
            for p, q in [(a, b)] if a == b else [(a, b), (b, a)]:
                y0[p] = y0[p] + real * a0[q] - imag * a1[q]
                y1[p] = y1[p] + imag * a0[q] + real * a1[q]
                z0[q] = z0[q] + real * b0[p] + imag * b1[p]
                z1[q] = z1[q] + real * b1[p] - imag * b0[p]
                h0 = h0 + b0[p] * a0[q] + b1[p] * a1[q]
                h1 = h1 + b1[p] * a0[q] - b0[p] * a1[q]
            products[at, :chans] = h0
            products[at, chans:] = h1
        for lat in range(lat_count):
            synth[lat, 0, rows, :] = y0[lat]
            synth[lat, 1, rows, :] = y1[lat]
            grad_coeff[lat, 0, rows, :] = z0[lat] * quad_ref[lat]
            grad_coeff[lat, 1, rows, :] = z1[lat] * quad_ref[lat]
        return carry

    lax.fori_loop(0, padded_modes // 8, mix, 0)
    used = len(pairs) * padded_modes
    if products.shape[0] > used:
        products[used:, :] = jnp.zeros((products.shape[0] - used, products.shape[1]), F32)
    gradient[...] = jnp.dot(
        back_ref[...], products[...].astype(BF16), preferred_element_type=F32
    )
    half = gradient.shape[0] // 2
    upper = jnp.bitwise_and(me, 1)
    for target, which in ((keep_ref, upper), (send_ref, 1 - upper)):
        part = gradient[pl.ds(pl.multiple_of(which * half, half), half), :]
        both = jnp.concatenate([part[:, :chans], part[:, chans:]], axis=0)
        target[...] = both.astype(target.dtype)
    for shift in range(blocks):
        block = jnp.bitwise_xor(me, shift)
        start = first_row_of(rows_ref, block, blocks)
        for slot in range(slots):
            lat = jnp.minimum(start + slot, lat_count - 1)
            for part in range(2):
                wide[shift, rows_at(0, slot, part), :] = synth[lat, part, :local_modes, :]
                wide[shift, rows_at(1, slot, part), :] = grad_coeff[lat, part, :local_modes, :]
        outs[shift][...] = wide[shift].astype(BF16)


def disco_kernel(
    blocks, lat_count, rows_ref, shift_ref, x_ref, dy_ref, act_ref, first_rim, second_rim, taps_ref,
    base_ref, slope_ref, base_grad_ref, tap_ref, acts, grads,
):
    slots, lon_count, chans = x_ref.shape
    taps = taps_ref.shape[0]
    me = lax.axis_index("space")
    live = rows_ref[me]
    start = first_row_of(rows_ref, me, blocks)

    def wrapped(target, row, value):
        target[row, REACH : REACH + lon_count, :] = value
        target[row, :REACH, :] = value[lon_count - REACH :, :]
        target[row, REACH + lon_count :, :] = value[:REACH, :]

    odd = jnp.bitwise_and(me, 1)
    for rim_ref, row in ((first_rim, (slots + 1) * (1 - odd)), (second_rim, (slots + 1) * odd)):
        wrapped(acts, row, rim_ref[0].astype(F32))
        wrapped(grads, row, rim_ref[1].astype(F32))
    for slot in range(slots):
        alive = jnp.where(slot < live, 1.0, 0.0)
        wrapped(acts, slot + 1, act_ref[slot].astype(F32))
        wrapped(grads, slot + 1, dy_ref[slot].astype(F32) * alive)
    weights = taps_ref[...].astype(F32)
    step = 32 if lon_count % 32 == 0 else lon_count
    totals = [jnp.zeros((8, chans), F32)] * taps
    for slot in range(slots):
        below = jnp.where(slot + 1 < live, slot + 2, slots + 1)
        rows = [slot, slot + 1, below]
        lat = jnp.clip(start + slot, 0, lat_count - 1)
        lats = [jnp.maximum(lat - 1, 0), lat, jnp.minimum(lat + 1, lat_count - 1)]
        ahead = [REACH + shift_ref[lat, t] for t in range(taps)]
        behind = [REACH - shift_ref[lats[2 - t // 3], t] for t in range(taps)]

        def taps_of(i, totals):
            at = pl.multiple_of(i * step, step)
            part = pl.ds(at, step)
            x = x_ref[slot, part, :].astype(F32)
            dy = grads[slot + 1, pl.ds(pl.multiple_of(REACH + at, 8), step), :]
            out = x
            back = jnp.zeros((step, chans), F32)
            fresh = []
            for t in range(taps):
                moved = acts[rows[t // 3], pl.ds(at + ahead[t], step), :]
                out = out + moved * weights[t : t + 1, :]
                fresh.append(totals[t] + jnp.sum((moved * dy).reshape(step // 8, 8, chans), axis=0))
                back = back + grads[rows[2 - t // 3], pl.ds(at + behind[t], step), :] * weights[
                    t : t + 1, :
                ]
            slope = gelu_slope(x)
            base_ref[slot, part, :] = out
            slope_ref[slot, part, :] = slope
            base_grad_ref[slot, part, :] = dy + back * slope
            return tuple(fresh)

        totals = list(lax.fori_loop(0, lon_count // step, taps_of, tuple(totals)))
    lines = [jnp.sum(total, axis=0, keepdims=True) for total in totals]
    lines.append(jnp.zeros((tap_ref.shape[0] - taps, chans), F32))
    tap_ref[...] = jnp.concatenate(lines, axis=0)


def split_taps(taps, out_ref, count):
    high = taps.astype(BF16)
    out_ref[count : count + TAP_ROWS, :] = high
    out_ref[count + TAP_ROWS :, :] = (taps - high.astype(F32)).astype(BF16)


def joined_taps(rows):
    return rows[-2 * TAP_ROWS : -TAP_ROWS, :] + rows[-TAP_ROWS:, :]


def halve_kernel(distance, kept_ref, got_ref, keep_ref, send_ref, total):
    total[...] = kept_ref[...] + got_ref[...].astype(F32)
    rows = total.shape[0] // 2
    half = rows // 2
    upper = jnp.where(jnp.bitwise_and(lax.axis_index("space"), distance) != 0, half, 0)
    for target, at in ((keep_ref, upper), (send_ref, half - upper)):
        both = [
            total[pl.ds(pl.multiple_of(part * rows + at, 8), half), :] for part in range(2)
        ]
        target[...] = jnp.concatenate(both, axis=0).astype(target.dtype)


def own_kernel(kept_ref, got_ref, tap_ref, out_ref):
    count = kept_ref.shape[0]
    out_ref[:count, :] = (kept_ref[...] + got_ref[...].astype(F32)).astype(BF16)
    split_taps(tap_ref[...], out_ref, count)


def member_kernel(lat_count, *refs):
    members = len(refs) - 2
    parts, out_ref, held = refs[:members], refs[-2], refs[-1]
    me = lax.axis_index("ens")
    count = out_ref.shape[0] - 2 * TAP_ROWS
    for shift in range(members):
        at = lax.rem(me + (members - shift), members)
        part = parts[shift][...].astype(F32)
        held[at, :count, :] = part[:count, :]
        held[at, count:, :] = joined_taps(part)
    total = held[0]
    for member in range(1, members):
        total = total + held[member]
    total = total / members
    out_ref[:count, :] = total[:count, :].astype(BF16)
    split_taps(total[count:, :] / lat_count, out_ref, count)


def mirrored(block, blocks):
    place = jnp.int32(0)
    bits = blocks.bit_length() - 1
    for bit in range(bits):
        place = place + (jnp.bitwise_and(block, 1 << bit) >> bit) * (1 << (bits - 1 - bit))
    return place


def spread_kernel(*refs):
    parts, (filter_ref, tap_ref, held) = refs[:-3], refs[-3:]
    me = lax.axis_index("space")
    blocks = len(parts)
    share = filter_ref.shape[1] // blocks
    for shift in range(blocks):
        block = jnp.bitwise_xor(me, shift)
        part = parts[shift][...].astype(F32)
        at = pl.ds(pl.multiple_of(mirrored(block, blocks) * share, share), share)
        filter_ref[0, at, :] = part[:share, :]
        filter_ref[1, at, :] = part[share : 2 * share, :]
        held[block] = joined_taps(part)
    total = held[0]
    for block in range(1, blocks):
        total = total + held[block]
    tap_ref[...] = total[: tap_ref.shape[0], :]


def finish_kernel(
    blocks, rows_ref, table_ref, base_ref, slope_ref, base_grad_ref, *refs
):
    ins, out_ref, grad_ref, source = refs[:blocks], refs[blocks], refs[blocks + 1], refs[blocks + 2]
    slots, lon_count, chans = base_ref.shape
    me = lax.axis_index("space")
    live = rows_ref[me]
    depth = source.shape[0] // blocks
    for shift in range(blocks):
        block = jnp.bitwise_xor(me, shift)
        rows = pl.ds(pl.multiple_of(block * depth, 8), depth)
        part = ins[shift][...].astype(F32)
        for at in range(2 * slots):
            source[rows, at * chans : (at + 1) * chans] = part[at * depth : (at + 1) * depth, :]
    sums = jnp.dot(table_ref[...], source[...].astype(BF16), preferred_element_type=F32)
    for slot in range(slots):
        at = slot * chans
        out = base_ref[slot] + sums[:, at : at + chans]
        at = (slots + slot) * chans
        grad = base_grad_ref[slot] + sums[:, at : at + chans] * slope_ref[slot]
        alive = slot < live
        out_ref[slot] = jnp.where(alive, out, 0.0).astype(BF16)
        grad_ref[slot] = jnp.where(alive, grad, 0.0).astype(BF16)


def shifted(values, axis, shift):
    count = lax.axis_size(axis)
    return lax.ppermute(values, axis, [(i, (i + shift) % count) for i in range(count)])


def crossed(values, distance):
    count = lax.axis_size("space")
    return lax.ppermute(values, "space", [(i, i ^ distance) for i in range(count)])


def crossed_all(parts, distances):
    return {s: crossed(parts[s], s) for s in distances}


def body(
    fields, cotangent, band_rows, tap_shift, quad_weight, legendre, spectral_filter, tap_weight
):
    blocks = lax.axis_size("space")
    members = lax.axis_size("ens")
    _, slots, lon_count, chans = fields.shape
    local_modes, lat_count, degrees = legendre.shape
    padded_modes = round_up(local_modes, 16)
    depth = round_up(2 * local_modes, 8)
    pairs = len(lat_pairs(lat_count))
    pair_rows = round_up(pairs * padded_modes, 128)
    share = 2 * degrees // blocks
    big = 32 if pair_rows <= 4096 else 60
    shape = jax.ShapeDtypeStruct
    table = fourier_table(lon_count, blocks, local_modes, depth)
    table_in = jnp.asarray(table)
    table_out = jnp.asarray(np.ascontiguousarray(table.reshape(blocks * depth, lon_count).T))
    x, dy = fields[0], cotangent[0]
    field = shape((slots, lon_count, chans), F32)
    coded = shape((2 * slots * depth, chans), BF16)
    rim = shape((2, lon_count, chans), BF16)

    coded_parts = call(
        functools.partial(forward_kernel, blocks),
        [coded] * blocks,
        [HBM] * 3,
        (x, dy, table_in),
        scratch=[
            pltpu.VMEM(x.shape, BF16),
            pltpu.VMEM(dy.shape, BF16),
            pltpu.VMEM(table.shape, BF16),
            pltpu.VMEM(x.shape, BF16),
            pltpu.SemaphoreType.DMA((3,)),
        ],
        limit=60,
        flops=2 * blocks * depth * lon_count * 2 * slots * chans,
    )
    far = list(range(blocks - 1, 0, -1))
    got = [coded_parts[0], *reversed(crossed_all(coded_parts, far).values())]
    leg_rows = jnp.pad(
        jnp.transpose(legendre, (1, 0, 2)), ((0, 0), (0, padded_modes - local_modes), (0, 0))
    )
    mixer, back, act, first_rim, second_rim = call(
        functools.partial(prepare_kernel, local_modes),
        [shape((pair_rows, 2 * chans), F32), shape((degrees, pair_rows), BF16)]
        + [shape(x.shape, BF16), rim, rim],
        [SMEM] + [VMEM] * 4,
        (band_rows, leg_rows, spectral_filter, x, dy),
        scratch=[pltpu.VMEM((pair_rows, degrees), BF16)],
        limit=big,
        flops=2 * pair_rows * degrees * 2 * chans,
        moved=8 * pair_rows * chans,
    )
    first_rim, second_rim, got[-1] = lax.optimization_barrier((first_rim, second_rim, got[-1]))
    first_rim = crossed(first_rim, 1)
    inner = [(i, i ^ 1) for i in range(blocks)]
    inner = [(i + 1, j + 1) for i, j in inner if max(i, j) + 1 < blocks]
    second_rim = lax.ppermute(second_rim, "space", inner)
    spectral = pltpu.VMEM((lat_count, 2, padded_modes, chans), F32)
    mixed = call(
        functools.partial(mix_kernel, blocks, slots, lat_count, local_modes),
        [coded] * blocks + [shape((degrees, chans), F32), shape((degrees, chans), BF16)],
        [SMEM, SMEM] + [VMEM] * (2 + blocks),
        (band_rows, quad_weight, mixer, back, *got),
        scratch=[spectral] * 4
        + [pltpu.VMEM((pair_rows, 2 * chans), F32), pltpu.VMEM((degrees, 2 * chans), F32)]
        + [pltpu.VMEM((blocks, *coded.shape), F32)],
        limit=big,
        flops=20 * degrees * pair_rows * 2 * chans,
    )
    back_parts, keep, send = mixed[:blocks], mixed[blocks], mixed[blocks + 1]
    distance = 1
    got_sums = crossed(send, distance)
    base, slope, base_grad, tap_part = call(
        functools.partial(disco_kernel, blocks, lat_count),
        [field, field, field, shape((TAP_ROWS, chans), F32)],
        [SMEM, SMEM] + [VMEM] * 6,
        (band_rows, tap_shift, x, dy, act, first_rim, second_rim, tap_weight),
        scratch=[pltpu.VMEM((slots + 2, lon_count + 2 * REACH, chans), F32)] * 2,
    )
    while 2 * distance < blocks:
        distance *= 2
        rows = keep.shape[0] // 2
        keep, send = call(
            functools.partial(halve_kernel, distance),
            [shape((rows, chans), F32), shape((rows, chans), BF16)],
            [VMEM, VMEM],
            (keep, got_sums),
            scratch=[pltpu.VMEM(keep.shape, F32)],
        )
        got_sums = crossed(send, distance)
    back_parts, keep = lax.optimization_barrier((back_parts, keep))
    returned = [back_parts[0], *reversed(crossed_all(back_parts, far).values())]
    own = call(
        own_kernel,
        shape((share + 2 * TAP_ROWS, chans), BF16),
        [VMEM] * 3,
        (keep, got_sums, tap_part),
    )
    by_member = [own] + [shifted(own, "ens", s) for s in range(1, members)]
    final = call(
        functools.partial(member_kernel, lat_count),
        shape((share + 2 * TAP_ROWS, chans), BF16),
        [VMEM] * members,
        by_member,
        flops=1200000000,
        scratch=[pltpu.VMEM((members, share + TAP_ROWS, chans), F32)],
    )
    spread = [final] + [crossed(final, s) for s in range(1, blocks)]
    output, input_grad = call(
        functools.partial(finish_kernel, blocks),
        [shape(x.shape, BF16)] * 2,
        [SMEM] + [VMEM] * (4 + blocks),
        (band_rows, table_out, base, slope, base_grad, *returned),
        scratch=[pltpu.VMEM((blocks * depth, 2 * slots * chans), F32)],
        flops=2 * blocks * depth * lon_count * 2 * slots * chans,
    )
    filter_grad, tap_grad = call(
        spread_kernel,
        [shape((2, degrees, chans), F32), shape((tap_weight.shape[0], chans), F32)],
        [VMEM] * blocks,
        spread,
        scratch=[pltpu.VMEM((blocks, TAP_ROWS, chans), F32)],
    )
    return (output[None], input_grad[None], filter_grad, tap_grad)


def solution(mesh):
    in_specs = (
        P(("groups", "ens"), "space", None, "chan"),
        P(("groups", "ens"), "space", None, "chan"),
        P("groups"),
        P(),
        P(),
        P("space", None, None),
        P(None, None, "chan"),
        P(None, "chan"),
    )
    out_specs = (
        P(("groups", "ens"), "space", None, "chan"),
        P(("groups", "ens"), "space", None, "chan"),
        P("groups", None, "chan"),
        P("groups", "chan"),
    )
    return jax.shard_map(body, mesh=mesh, in_specs=in_specs, out_specs=out_specs, check_vma=False)
```

```python
import functools
import math

import jax
import jax.numpy as jnp
import ml_dtypes
import numpy as np
from jax import lax
from jax.experimental import pallas as pl
from jax.experimental.pallas import tpu as pltpu
from jax.sharding import PartitionSpec as P

F32 = jnp.float32
BF16 = jnp.bfloat16
VMEM = pl.BlockSpec(memory_space=pltpu.VMEM)
SMEM = pl.BlockSpec(memory_space=pltpu.SMEM)
HBM = pl.BlockSpec(memory_space=pltpu.HBM)
REACH = 8
TAP_ROWS = 16


def gelu_value(values):
    return 0.5 * values * (1.0 + lax.erf(values * 0.7071067811865476))


def gelu_slope(values):
    return (
        0.5 * (1.0 + lax.erf(values * 0.7071067811865476))
        + values * jnp.exp(-0.5 * values * values) * 0.3989422804014327
    )


def round_up(count, step):
    return -(-count // step) * step


def fourier_table(lon_count, blocks, local_modes, depth):
    lon_ids = np.arange(lon_count)
    mode_ids = np.arange(blocks * local_modes)
    phase = (mode_ids[:, None] * lon_ids[None, :] % lon_count) * (2.0 * math.pi / lon_count)
    factor = 1.0 / math.sqrt(lon_count)
    both = np.stack([np.cos(phase), -np.sin(phase)]) * factor
    both = both.reshape(2, blocks, local_modes, lon_count).transpose(1, 0, 2, 3)
    both = both.reshape(blocks, 2 * local_modes, lon_count)
    both = np.pad(both, ((0, 0), (0, depth - 2 * local_modes), (0, 0)))
    return both.astype(ml_dtypes.bfloat16)


def lat_pairs(lat_count):
    return [(a, b) for a in range(lat_count) for b in range(a, lat_count)]


def first_row_of(rows_ref, block, blocks):
    total = jnp.int32(0)
    for other in range(blocks):
        total = total + jnp.where(other < block, rows_ref[other], 0)
    return total


def call(kernel, out_shape, in_specs, args, scratch=(), limit=32, flops=0, moved=1024):
    return pl.pallas_call(
        kernel,
        out_shape=out_shape,
        in_specs=in_specs,
        out_specs=jax.tree.map(lambda _: VMEM, out_shape),
        scratch_shapes=list(scratch),
        compiler_params=pltpu.CompilerParams(vmem_limit_bytes=limit * 1024 * 1024),
        cost_estimate=pl.CostEstimate(flops=flops, bytes_accessed=moved, transcendentals=0),
    )(*args)


def activate(x_ref, act_ref):
    slots, lon_count, _ = x_ref.shape
    step = 64 if lon_count % 64 == 0 else lon_count

    def run(i, carry):
        part = pl.ds(pl.multiple_of(i * step, step), step)
        for slot in range(slots):
            act_ref[slot, part, :] = gelu_value(x_ref[slot, part, :].astype(F32)).astype(BF16)
        return carry

    lax.fori_loop(0, lon_count // step, run, 0)


def forward_kernel(blocks, x_hbm, dy_hbm, table_hbm, *refs):
    outs, (x_ref, dy_ref, table_ref, act_ref, sems) = refs[:blocks], refs[blocks:]
    slots, _, chans = x_ref.shape
    me = lax.axis_index("space")
    loads = [
        pltpu.make_async_copy(source, target, sems.at[i])
        for i, (source, target) in enumerate(
            [(x_hbm, x_ref), (dy_hbm, dy_ref), (table_hbm, table_ref)]
        )
    ]
    for load in loads:
        load.start()
    loads[0].wait()
    activate(x_ref, act_ref)
    loads[1].wait()
    source = jnp.concatenate(
        [dy_ref[slot] for slot in range(slots)] + [act_ref[slot] for slot in range(slots)], axis=-1
    )
    loads[2].wait()
    for shift in range(blocks):
        block = jnp.bitwise_xor(me, shift)
        sums = jnp.dot(table_ref[block], source, preferred_element_type=F32)
        columns = [sums[:, at * chans : (at + 1) * chans] for at in range(2 * slots)]
        outs[shift][...] = jnp.concatenate(columns, axis=0).astype(BF16)


def wrapped(target, row, value):
    lon_count = value.shape[0]
    target[row, REACH : REACH + lon_count, :] = value
    target[row, :REACH, :] = value[lon_count - REACH :, :]
    target[row, REACH + lon_count :, :] = value[:REACH, :]


def folded(values):
    return jnp.sum(values.reshape(values.shape[0] // 8, 8, values.shape[1]), axis=0)


def prepare_kernel(
    local_modes, blocks, rows_ref, shift_ref, leg_ref, filter_ref, x_ref, dy_ref, taps_ref,
    mixer_ref, back_ref, first_rim, second_rim, base_ref, slope_ref, base_grad_ref, tap_ref,
    pairs_ref, act_ref, acts, grads,
):
    me = lax.axis_index("space")
    activate(x_ref, act_ref)
    last = rows_ref[me] - 1
    odd = jnp.bitwise_and(me, 1)
    for rim_ref, row in ((first_rim, last * (1 - odd)), (second_rim, last * odd)):
        rim_ref[0] = act_ref[row]
        rim_ref[1] = dy_ref[row]
    pair_products(local_modes, leg_ref, filter_ref, mixer_ref, back_ref, pairs_ref)
    disco_inner(
        blocks, rows_ref, shift_ref, x_ref, dy_ref, act_ref, taps_ref,
        base_ref, slope_ref, base_grad_ref, tap_ref, acts, grads,
    )


def pair_products(local_modes, leg_ref, filter_ref, mixer_ref, back_ref, pairs_ref):
    me = lax.axis_index("space")
    lat_count, padded_modes, _ = leg_ref.shape
    pairs = lat_pairs(lat_count)
    used = len(pairs) * padded_modes
    mode = me * local_modes + lax.broadcasted_iota(
        jnp.int32, (padded_modes, 1), 0
    )
    twice = jnp.where(mode == 0, 1.0, 2.0)
    for index, (a, b) in enumerate(pairs):
        at = index * padded_modes
        pairs_ref[at : at + padded_modes, :] = (
            leg_ref[a].astype(F32) * leg_ref[b].astype(F32) * twice
        ).astype(BF16)
    if pairs_ref.shape[0] > used:
        pairs_ref[used:, :] = jnp.zeros((pairs_ref.shape[0] - used, pairs_ref.shape[1]), BF16)
    both = jnp.concatenate([filter_ref[0], filter_ref[1]], axis=-1)
    mixer_ref[...] = jnp.dot(pairs_ref[...], both, preferred_element_type=F32)

    def turn(i, carry):
        part = pl.ds(pl.multiple_of(i * 128, 128), 128)
        back_ref[:, part] = pairs_ref[part, :].astype(F32).T.astype(BF16)
        return carry

    lax.fori_loop(0, pairs_ref.shape[0] // 128, turn, 0)


def mix_kernel(blocks, slots, lat_count, local_modes, rows_ref, quad_ref, mixer_ref, back_ref, *refs):
    ins, outs = refs[:blocks], refs[blocks : 2 * blocks]
    keep_ref, send_ref, coeff, grad, synth, grad_coeff, products, gradient, wide = refs[2 * blocks :]
    padded_modes, chans = coeff.shape[2:]
    me = lax.axis_index("space")
    pairs = lat_pairs(lat_count)
    depth = wide.shape[1] // (2 * slots)
    padding = padded_modes - local_modes
    if padding > 0:
        zeros = jnp.zeros((padding, chans), F32)
        for lat in range(lat_count):
            for part in range(2):
                coeff[lat, part, local_modes:, :] = zeros
                grad[lat, part, local_modes:, :] = zeros

    def rows_at(field, slot, part):
        at = (field * slots + slot) * depth + part * local_modes
        return slice(at, at + local_modes)

    for shift in range(blocks):
        block = jnp.bitwise_xor(me, shift)
        start = first_row_of(rows_ref, block, blocks)
        wide[shift] = ins[shift][...].astype(F32)
        for slot in range(slots):
            lat = jnp.minimum(start + slot, lat_count - 1)

            @pl.when(slot < rows_ref[block])
            def _():
                weight = quad_ref[lat]
                for part in range(2):
                    grad[lat, part, :local_modes, :] = wide[shift, rows_at(0, slot, part), :]
                    coeff[lat, part, :local_modes, :] = (
                        wide[shift, rows_at(1, slot, part), :] * weight
                    )

    def mix(i, carry):
        rows = pl.ds(pl.multiple_of(i * 8, 8), 8)
        a0 = [coeff[lat, 0, rows, :] for lat in range(lat_count)]
        a1 = [coeff[lat, 1, rows, :] for lat in range(lat_count)]
        b0 = [grad[lat, 0, rows, :] for lat in range(lat_count)]
        b1 = [grad[lat, 1, rows, :] for lat in range(lat_count)]
        zero = jnp.zeros((8, chans), F32)
        y0, y1, z0, z1 = ([zero] * lat_count for _ in range(4))
        for index, (a, b) in enumerate(pairs):
            at = pl.ds(pl.multiple_of(index * padded_modes + i * 8, 8), 8)
            real = mixer_ref[at, :chans]
            imag = mixer_ref[at, chans:]
            h0 = h1 = zero
            for p, q in [(a, b)] if a == b else [(a, b), (b, a)]:
                y0[p] = y0[p] + real * a0[q] - imag * a1[q]
                y1[p] = y1[p] + imag * a0[q] + real * a1[q]
                z0[q] = z0[q] + real * b0[p] + imag * b1[p]
                z1[q] = z1[q] + real * b1[p] - imag * b0[p]
                h0 = h0 + b0[p] * a0[q] + b1[p] * a1[q]
                h1 = h1 + b1[p] * a0[q] - b0[p] * a1[q]
            products[at, :chans] = h0
            products[at, chans:] = h1
        for lat in range(lat_count):
            synth[lat, 0, rows, :] = y0[lat]
            synth[lat, 1, rows, :] = y1[lat]
            grad_coeff[lat, 0, rows, :] = z0[lat] * quad_ref[lat]
            grad_coeff[lat, 1, rows, :] = z1[lat] * quad_ref[lat]
        return carry

    lax.fori_loop(0, padded_modes // 8, mix, 0)
    used = len(pairs) * padded_modes
    if products.shape[0] > used:
        products[used:, :] = jnp.zeros((products.shape[0] - used, products.shape[1]), F32)
    gradient[...] = jnp.dot(
        back_ref[...], products[...].astype(BF16), preferred_element_type=F32
    )
    half = gradient.shape[0] // 2
    upper = jnp.bitwise_and(me, 1)
    for target, which in ((keep_ref, upper), (send_ref, 1 - upper)):
        part = gradient[pl.ds(pl.multiple_of(which * half, half), half), :]
        both = jnp.concatenate([part[:, :chans], part[:, chans:]], axis=0)
        target[...] = both.astype(target.dtype)
    for shift in range(blocks):
        block = jnp.bitwise_xor(me, shift)
        start = first_row_of(rows_ref, block, blocks)
        for slot in range(slots):
            lat = jnp.minimum(start + slot, lat_count - 1)
            for part in range(2):
                wide[shift, rows_at(0, slot, part), :] = synth[lat, part, :local_modes, :]
                wide[shift, rows_at(1, slot, part), :] = grad_coeff[lat, part, :local_modes, :]
        outs[shift][...] = wide[shift].astype(BF16)


def disco_inner(
    blocks, rows_ref, shift_ref, x_ref, dy_ref, act_ref, taps_ref,
    base_ref, slope_ref, base_grad_ref, tap_ref, acts, grads,
):
    slots, lon_count, chans = x_ref.shape
    taps = taps_ref.shape[0]
    me = lax.axis_index("space")
    live = rows_ref[me]
    start = first_row_of(rows_ref, me, blocks)
    for slot in range(slots):
        alive = jnp.where(slot < live, 1.0, 0.0)
        wrapped(acts, slot, act_ref[slot].astype(F32))
        wrapped(grads, slot, dy_ref[slot].astype(F32) * alive)
    acts[slots] = jnp.zeros(acts.shape[1:], F32)
    grads[slots] = jnp.zeros(grads.shape[1:], F32)
    weights = taps_ref[...].astype(F32)
    step = 32 if lon_count % 32 == 0 else lon_count
    totals = [jnp.zeros((8, chans), F32)] * taps
    top = shift_ref.shape[0] - 1
    for slot in range(slots):
        below = jnp.where(slot + 1 < live, slot + 1, slots)
        sources = [(1, slot)]
        if slot > 0:
            sources.append((0, slot - 1))
        if slot + 1 < slots:
            sources.append((2, below))
        lat = jnp.clip(start + slot, 0, top)
        ahead, behind = [], []
        for offset, row in sources:
            other = jnp.clip(lat + offset - 1, 0, top)
            for column in range(3):
                t = 3 * offset + column
                ahead.append((t, row, REACH + shift_ref[lat, t]))
                t = 3 * (2 - offset) + column
                behind.append((t, row, REACH - shift_ref[other, t]))

        def inner(i, totals):
            at = pl.multiple_of(i * step, step)
            part = pl.ds(at, step)
            x = x_ref[slot, part, :].astype(F32)
            dy = grads[slot, pl.ds(pl.multiple_of(REACH + at, 8), step), :]
            out = x
            back = jnp.zeros((step, chans), F32)
            fresh = list(totals)
            for t, row, first in ahead:
                moved = acts[row, pl.ds(at + first, step), :]
                out = out + moved * weights[t : t + 1, :]
                fresh[t] = fresh[t] + folded(moved * dy)
            for t, row, first in behind:
                back = back + grads[row, pl.ds(at + first, step), :] * weights[t : t + 1, :]
            slope = gelu_slope(x)
            base_ref[slot, part, :] = out
            slope_ref[slot, part, :] = slope
            base_grad_ref[slot, part, :] = dy + back * slope
            return tuple(fresh)

        totals = list(lax.fori_loop(0, lon_count // step, inner, tuple(totals)))
    lines = [jnp.sum(total, axis=0, keepdims=True) for total in totals]
    lines.append(jnp.zeros((tap_ref.shape[0] - taps, chans), F32))
    tap_ref[...] = jnp.concatenate(lines, axis=0)


def rim_kernel(
    blocks, rows_ref, shift_ref, dy_ref, first_rim, second_rim, taps_ref, inner_ref,
    rim_ref, rim_grad_ref, tap_ref, acts, grads,
):
    _, lon_count, chans = dy_ref.shape
    me = lax.axis_index("space")
    live = rows_ref[me]
    start = first_row_of(rows_ref, me, blocks)
    odd = jnp.bitwise_and(me, 1)
    for source, row in ((first_rim, 1 - odd), (second_rim, odd)):
        wrapped(acts, row, source[0].astype(F32))
        wrapped(grads, row, source[1].astype(F32))
    weights = taps_ref[...].astype(F32)
    step = 32 if lon_count % 32 == 0 else lon_count
    top = shift_ref.shape[0] - 1
    lines = [jnp.zeros((1, chans), F32)] * tap_ref.shape[0]
    for side in range(2):
        slot = 0 if side == 0 else live - 1
        lat = jnp.clip(start + slot, 0, top)
        other = jnp.clip(lat + 2 * side - 1, 0, top)
        ahead = [(t, REACH + shift_ref[lat, t]) for t in range(6 * side, 6 * side + 3)]
        behind = [(t, REACH - shift_ref[other, t]) for t in range(6 - 6 * side, 9 - 6 * side)]

        def rim(i, totals):
            at = pl.multiple_of(i * step, step)
            part = pl.ds(at, step)
            dy = dy_ref[slot, part, :].astype(F32)
            out = back = jnp.zeros((step, chans), F32)
            fresh = []
            for total, (t, first) in zip(totals, ahead):
                moved = acts[side, pl.ds(at + first, step), :]
                out = out + moved * weights[t : t + 1, :]
                fresh.append(total + folded(moved * dy))
            for t, first in behind:
                back = back + grads[side, pl.ds(at + first, step), :] * weights[t : t + 1, :]
            rim_ref[side, part, :] = out
            rim_grad_ref[side, part, :] = back
            return tuple(fresh)

        totals = lax.fori_loop(0, lon_count // step, rim, (jnp.zeros((8, chans), F32),) * 3)
        for (t, _), total in zip(ahead, totals):
            lines[t] = jnp.sum(total, axis=0, keepdims=True)
    tap_ref[...] = inner_ref[...] + jnp.concatenate(lines, axis=0)


def split_taps(taps, out_ref, count):
    high = taps.astype(BF16)
    out_ref[count : count + TAP_ROWS, :] = high
    out_ref[count + TAP_ROWS :, :] = (taps - high.astype(F32)).astype(BF16)


def joined_taps(rows):
    return rows[-2 * TAP_ROWS : -TAP_ROWS, :] + rows[-TAP_ROWS:, :]


def split_taps(taps, out_ref, count):
    high = taps.astype(BF16)
    out_ref[count : count + TAP_ROWS, :] = high
    out_ref[count + TAP_ROWS :, :] = (taps - high.astype(F32)).astype(BF16)


def joined_taps(ref):
    rows = ref[ref.shape[0] - 2 * TAP_ROWS :, :].astype(F32)
    return rows[:TAP_ROWS, :] + rows[TAP_ROWS:, :]


def added(first_ref, second_ref):
    return first_ref[...].astype(F32) + second_ref[...].astype(F32)


def half_kernel(kept_ref, got_ref, tap_ref, out_ref):
    out_ref[: kept_ref.shape[0], :] = added(kept_ref, got_ref).astype(BF16)
    split_taps(tap_ref[...], out_ref, kept_ref.shape[0])


def add_kernel(scale, tap_scale, own_ref, other_ref, out_ref):
    count = own_ref.shape[0] - 2 * TAP_ROWS
    out_ref[:count, :] = (added(own_ref, other_ref)[:count, :] / scale).astype(BF16)
    split_taps((joined_taps(own_ref) + joined_taps(other_ref)) / tap_scale, out_ref, count)


def spread_kernel(own_ref, other_ref, filter_ref, tap_ref):
    half = filter_ref.shape[1] // 2
    upper = jnp.bitwise_and(lax.axis_index("space"), 1)
    for ref, which in ((own_ref, upper), (other_ref, 1 - upper)):
        at = pl.ds(pl.multiple_of(which * half, half), half)
        rows = ref[: 2 * half, :].astype(F32)
        filter_ref[0, at, :] = rows[:half, :]
        filter_ref[1, at, :] = rows[half:, :]
    tap_ref[...] = (joined_taps(own_ref) + joined_taps(other_ref))[: tap_ref.shape[0], :]


def finish_kernel(
    blocks, rows_ref, table_ref, base_ref, slope_ref, base_grad_ref, rim_ref, rim_grad_ref, *refs
):
    ins, out_ref, grad_ref, source = refs[:blocks], refs[blocks], refs[blocks + 1], refs[blocks + 2]
    slots, lon_count, chans = base_ref.shape
    me = lax.axis_index("space")
    live = rows_ref[me]
    depth = source.shape[0] // blocks
    for shift in range(blocks):
        block = jnp.bitwise_xor(me, shift)
        rows = pl.ds(pl.multiple_of(block * depth, 8), depth)
        part = ins[shift][...].astype(F32)
        for at in range(2 * slots):
            source[rows, at * chans : (at + 1) * chans] = part[at * depth : (at + 1) * depth, :]
    sums = jnp.dot(table_ref[...], source[...].astype(BF16), preferred_element_type=F32)
    for slot in range(slots):
        at = slot * chans
        out = base_ref[slot] + sums[:, at : at + chans]
        at = (slots + slot) * chans
        back = sums[:, at : at + chans]
        if slot == 0:
            out = out + rim_ref[0]
            back = back + rim_grad_ref[0]
        out = out + jnp.where(slot == live - 1, rim_ref[1], 0.0)
        back = back + jnp.where(slot == live - 1, rim_grad_ref[1], 0.0)
        grad = base_grad_ref[slot] + back * slope_ref[slot]
        alive = slot < live
        out_ref[slot] = jnp.where(alive, out, 0.0).astype(BF16)
        grad_ref[slot] = jnp.where(alive, grad, 0.0).astype(BF16)


def crossed(values, distance, axis="space"):
    count = lax.axis_size(axis)
    return lax.ppermute(values, axis, [(i, i ^ distance) for i in range(count)])


def crossed_all(parts, distances):
    return {s: crossed(parts[s], s) for s in distances}


def body(
    fields, cotangent, band_rows, tap_shift, quad_weight, legendre, spectral_filter, tap_weight
):
    blocks = lax.axis_size("space")
    members = lax.axis_size("ens")
    _, slots, lon_count, chans = fields.shape
    local_modes, lat_count, degrees = legendre.shape
    padded_modes = round_up(local_modes, 16)
    depth = round_up(2 * local_modes, 8)
    pairs = len(lat_pairs(lat_count))
    pair_rows = round_up(pairs * padded_modes, 128)
    share = 2 * degrees // blocks
    big = 32 if pair_rows <= 4096 else 60
    shape = jax.ShapeDtypeStruct
    table = fourier_table(lon_count, blocks, local_modes, depth)
    table_in = jnp.asarray(table)
    table_out = jnp.asarray(np.ascontiguousarray(table.reshape(blocks * depth, lon_count).T))
    x, dy = fields[0], cotangent[0]
    field = shape((slots, lon_count, chans), F32)
    coded = shape((2 * slots * depth, chans), BF16)
    rim = shape((2, lon_count, chans), BF16)

    coded_parts = call(
        functools.partial(forward_kernel, blocks),
        [coded] * blocks,
        [HBM] * 3,
        (x, dy, table_in),
        scratch=[
            pltpu.VMEM(x.shape, BF16),
            pltpu.VMEM(dy.shape, BF16),
            pltpu.VMEM(table.shape, BF16),
            pltpu.VMEM(x.shape, BF16),
            pltpu.SemaphoreType.DMA((3,)),
        ],
        limit=60,
        flops=2 * blocks * depth * lon_count * 2 * slots * chans,
    )
    far = list(range(blocks - 1, 0, -1))
    got = [coded_parts[0], *reversed(crossed_all(coded_parts, far).values())]
    leg_rows = jnp.pad(
        jnp.transpose(legendre, (1, 0, 2)), ((0, 0), (0, padded_modes - local_modes), (0, 0))
    )
    padded = (lon_count + 2 * REACH, chans)
    tap_shape = shape((TAP_ROWS, chans), F32)
    mixer, back, first_rim, second_rim, base, slope, base_grad, tap_part = call(
        functools.partial(prepare_kernel, local_modes, blocks),
        [shape((pair_rows, 2 * chans), F32), shape((degrees, pair_rows), BF16), rim, rim]
        + [field, field, field, tap_shape],
        [SMEM, SMEM] + [VMEM] * 5,
        (band_rows, tap_shift, leg_rows, spectral_filter, x, dy, tap_weight),
        scratch=[pltpu.VMEM((pair_rows, degrees), BF16), pltpu.VMEM(x.shape, BF16)]
        + [pltpu.VMEM((slots + 1, *padded), F32)] * 2,
        limit=big,
        flops=2 * pair_rows * degrees * 2 * chans,
        moved=8 * pair_rows * chans,
    )
    first_rim, second_rim, got[-1] = lax.optimization_barrier((first_rim, second_rim, got[-1]))
    first_rim = crossed(first_rim, 1)
    inner = [(i, i ^ 1) for i in range(blocks)]
    inner = [(i + 1, j + 1) for i, j in inner if max(i, j) + 1 < blocks]
    second_rim = lax.ppermute(second_rim, "space", inner)
    spectral = pltpu.VMEM((lat_count, 2, padded_modes, chans), F32)
    mixed = call(
        functools.partial(mix_kernel, blocks, slots, lat_count, local_modes),
        [coded] * blocks + [shape((degrees, chans), F32), shape((degrees, chans), BF16)],
        [SMEM, SMEM] + [VMEM] * (2 + blocks),
        (band_rows, quad_weight, mixer, back, *got),
        scratch=[spectral] * 4
        + [pltpu.VMEM((pair_rows, 2 * chans), F32), pltpu.VMEM((degrees, 2 * chans), F32)]
        + [pltpu.VMEM((blocks, *coded.shape), F32)],
        limit=big,
        flops=20 * degrees * pair_rows * 2 * chans,
    )
    back_parts, keep, send = mixed[:blocks], mixed[blocks], mixed[blocks + 1]
    got_sum = crossed(send, 1)
    rim_sum, rim_grad, tap_part = call(
        functools.partial(rim_kernel, blocks),
        [shape((2, lon_count, chans), F32)] * 2 + [tap_shape],
        [SMEM, SMEM] + [VMEM] * 5,
        (band_rows, tap_shift, dy, first_rim, second_rim, tap_weight, tap_part),
        scratch=[pltpu.VMEM((2, *padded), F32)] * 2,
    )
    got_sum, tap_part = lax.optimization_barrier((got_sum, tap_part))
    message = shape((degrees + 2 * TAP_ROWS, chans), BF16)
    own = call(half_kernel, message, [VMEM] * 3, (keep, got_sum, tap_part))
    back_parts, own = lax.optimization_barrier((back_parts, own))
    returned = [back_parts[0], *reversed(crossed_all(back_parts, far).values())]
    for bit in range(1, blocks.bit_length() - 1):
        own = call(
            functools.partial(add_kernel, 1, 1), message, [VMEM] * 2, (own, crossed(own, 1 << bit))
        )
    for bit in range(members.bit_length() - 1):
        scales = (members, members * lat_count) if bit == 0 else (1, 1)
        own = call(
            functools.partial(add_kernel, *scales),
            message,
            [VMEM] * 2,
            (own, crossed(own, 1 << bit, "ens")),
            flops=0,
        )
    filter_grad, tap_grad = call(
        spread_kernel,
        [shape((2, degrees, chans), F32), shape((tap_weight.shape[0], chans), F32)],
        [VMEM] * 2,
        (own, crossed(own, 1)),
    )
    output, input_grad = call(
        functools.partial(finish_kernel, blocks),
        [shape(x.shape, BF16)] * 2,
        [SMEM] + [VMEM] * (6 + blocks),
        (band_rows, table_out, base, slope, base_grad, rim_sum, rim_grad, *returned),
        scratch=[pltpu.VMEM((blocks * depth, 2 * slots * chans), F32)],
        flops=2 * blocks * depth * lon_count * 2 * slots * chans,
    )
    return (output[None], input_grad[None], filter_grad, tap_grad)


def solution(mesh):
    in_specs = (
        P(("groups", "ens"), "space", None, "chan"),
        P(("groups", "ens"), "space", None, "chan"),
        P("groups"),
        P(),
        P(),
        P("space", None, None),
        P(None, None, "chan"),
        P(None, "chan"),
    )
    out_specs = (
        P(("groups", "ens"), "space", None, "chan"),
        P(("groups", "ens"), "space", None, "chan"),
        P("groups", None, "chan"),
        P("groups", "chan"),
    )
    return jax.shard_map(body, mesh=mesh, in_specs=in_specs, out_specs=out_specs, check_vma=False)
```

```python
import functools
import math

import jax
import jax.numpy as jnp
import ml_dtypes
import numpy as np
from jax import lax
from jax.experimental import pallas as pl
from jax.experimental.pallas import tpu as pltpu
from jax.sharding import PartitionSpec as P

F32 = jnp.float32
BF16 = jnp.bfloat16
VMEM = pl.BlockSpec(memory_space=pltpu.VMEM)
SMEM = pl.BlockSpec(memory_space=pltpu.SMEM)
HBM = pl.BlockSpec(memory_space=pltpu.HBM)
REACH = 8
TAP_ROWS = 16


def gelu_value(values):
    return 0.5 * values * (1.0 + lax.erf(values * 0.7071067811865476))


def gelu_slope(values):
    return (
        0.5 * (1.0 + lax.erf(values * 0.7071067811865476))
        + values * jnp.exp(-0.5 * values * values) * 0.3989422804014327
    )


def round_up(count, step):
    return -(-count // step) * step


def fourier_table(lon_count, blocks, local_modes, depth):
    lon_ids = np.arange(lon_count)
    mode_ids = np.arange(blocks * local_modes)
    phase = (mode_ids[:, None] * lon_ids[None, :] % lon_count) * (2.0 * math.pi / lon_count)
    factor = 1.0 / math.sqrt(lon_count)
    both = np.stack([np.cos(phase), -np.sin(phase)]) * factor
    both = both.reshape(2, blocks, local_modes, lon_count).transpose(1, 0, 2, 3)
    both = both.reshape(blocks, 2 * local_modes, lon_count)
    both = np.pad(both, ((0, 0), (0, depth - 2 * local_modes), (0, 0)))
    return both.astype(ml_dtypes.bfloat16)


def lat_pairs(lat_count):
    return [(a, b) for a in range(lat_count) for b in range(a, lat_count)]


def first_row_of(rows_ref, block, blocks):
    total = jnp.int32(0)
    for other in range(blocks):
        total = total + jnp.where(other < block, rows_ref[other], 0)
    return total


def call(kernel, out_shape, in_specs, args, scratch=(), limit=32, flops=0, moved=1024, out_specs=None):
    return pl.pallas_call(
        kernel,
        out_shape=out_shape,
        in_specs=in_specs,
        out_specs=out_specs or jax.tree.map(lambda _: VMEM, out_shape),
        scratch_shapes=list(scratch),
        compiler_params=pltpu.CompilerParams(vmem_limit_bytes=limit * 1024 * 1024),
        cost_estimate=pl.CostEstimate(flops=flops, bytes_accessed=moved, transcendentals=0),
    )(*args)


def activate(x_ref, act_ref):
    slots, lon_count, _ = x_ref.shape
    step = 64 if lon_count % 64 == 0 else lon_count

    def run(i, carry):
        part = pl.ds(pl.multiple_of(i * step, step), step)
        for slot in range(slots):
            act_ref[slot, part, :] = gelu_value(x_ref[slot, part, :].astype(F32)).astype(BF16)
        return carry

    lax.fori_loop(0, lon_count // step, run, 0)


def forward_kernel(blocks, x_hbm, dy_hbm, table_hbm, *refs):
    outs, (x_ref, dy_ref, table_ref, act_ref, sems) = refs[:blocks], refs[blocks:]
    slots = x_ref.shape[0]
    me = lax.axis_index("space")
    loads = [
        pltpu.make_async_copy(source, target, sems.at[i])
        for i, (source, target) in enumerate(
            [(x_hbm, x_ref), (dy_hbm, dy_ref), (table_hbm, table_ref)]
        )
    ]
    for load in loads:
        load.start()
    loads[0].wait()
    activate(x_ref, act_ref)
    loads[1].wait()
    source = jnp.concatenate(
        [dy_ref[slot] for slot in range(slots)] + [act_ref[slot] for slot in range(slots)], axis=-1
    )
    loads[2].wait()
    for shift in range(blocks):
        block = jnp.bitwise_xor(me, shift)
        sums = jnp.dot(table_ref[block], source, preferred_element_type=F32)
        outs[shift][...] = sums.astype(BF16)


def wrapped(target, row, value):
    lon_count = value.shape[0]
    target[row, REACH : REACH + lon_count, :] = value
    target[row, :REACH, :] = value[lon_count - REACH :, :]
    target[row, REACH + lon_count :, :] = value[:REACH, :]


def folded(values):
    return jnp.sum(values.reshape(values.shape[0] // 8, 8, values.shape[1]), axis=0)


def prepare_kernel(
    local_modes, blocks, rows_ref, shift_ref, leg_ref, filter_ref, x_ref, dy_ref, taps_ref,
    mixer_ref, back_ref, first_rim, second_rim, base_ref, slope_ref, base_grad_ref, tap_ref,
    pairs_ref, act_ref, acts, grads,
):
    me = lax.axis_index("space")
    activate(x_ref, act_ref)
    last = rows_ref[me] - 1
    odd = jnp.bitwise_and(me, 1)
    for rim_ref, row in ((first_rim, last * (1 - odd)), (second_rim, last * odd)):
        rim_ref[0] = act_ref[row]
        rim_ref[1] = dy_ref[row]
    pair_products(local_modes, leg_ref, filter_ref, mixer_ref, back_ref, pairs_ref)
    disco_inner(
        blocks, rows_ref, shift_ref, x_ref, dy_ref, act_ref, taps_ref,
        base_ref, slope_ref, base_grad_ref, tap_ref, acts, grads,
    )


def pair_products(local_modes, leg_ref, filter_ref, mixer_ref, back_ref, pairs_ref):
    me = lax.axis_index("space")
    lat_count, padded_modes, _ = leg_ref.shape
    pairs = lat_pairs(lat_count)
    used = len(pairs) * padded_modes
    mode = me * local_modes + lax.broadcasted_iota(
        jnp.int32, (padded_modes, 1), 0
    )
    twice = jnp.where(mode == 0, 1.0, 2.0)
    for index, (a, b) in enumerate(pairs):
        at = index * padded_modes
        pairs_ref[at : at + padded_modes, :] = (
            leg_ref[a].astype(F32) * leg_ref[b].astype(F32) * twice
        ).astype(BF16)
    if pairs_ref.shape[0] > used:
        pairs_ref[used:, :] = jnp.zeros((pairs_ref.shape[0] - used, pairs_ref.shape[1]), BF16)
    both = jnp.concatenate([filter_ref[0], filter_ref[1]], axis=-1)
    mixer_ref[...] = jnp.dot(pairs_ref[...], both, preferred_element_type=F32)

    def turn(i, carry):
        part = pl.ds(pl.multiple_of(i * 128, 128), 128)
        back_ref[:, part] = pairs_ref[part, :].astype(F32).T.astype(BF16)
        return carry

    lax.fori_loop(0, pairs_ref.shape[0] // 128, turn, 0)


def mix_kernel(blocks, slots, lat_count, local_modes, rows_ref, quad_ref, mixer_ref, back_ref, *refs):
    ins, outs = refs[:blocks], refs[blocks : 2 * blocks]
    keep_ref, send_ref, coeff, grad, synth, grad_coeff, products, gradient, wide = refs[2 * blocks :]
    padded_modes, chans = coeff.shape[2:]
    me = lax.axis_index("space")
    pairs = lat_pairs(lat_count)
    padding = padded_modes - local_modes
    if padding > 0:
        zeros = jnp.zeros((padding, chans), F32)
        for lat in range(lat_count):
            for part in range(2):
                coeff[lat, part, local_modes:, :] = zeros
                grad[lat, part, local_modes:, :] = zeros

    def place(field, slot, part):
        rows = slice(part * local_modes, (part + 1) * local_modes)
        return rows, slice((field * slots + slot) * chans, (field * slots + slot + 1) * chans)

    for shift in range(blocks):
        block = jnp.bitwise_xor(me, shift)
        start = first_row_of(rows_ref, block, blocks)
        wide[shift] = ins[shift][...].astype(F32)
        for slot in range(slots):
            lat = jnp.minimum(start + slot, lat_count - 1)

            @pl.when(slot < rows_ref[block])
            def _():
                weight = quad_ref[lat]
                for part in range(2):
                    grad[lat, part, :local_modes, :] = wide[(shift, *place(0, slot, part))]
                    coeff[lat, part, :local_modes, :] = (
                        wide[(shift, *place(1, slot, part))] * weight
                    )

    def mix(i, carry):
        rows = pl.ds(pl.multiple_of(i * 8, 8), 8)
        a0 = [coeff[lat, 0, rows, :] for lat in range(lat_count)]
        a1 = [coeff[lat, 1, rows, :] for lat in range(lat_count)]
        b0 = [grad[lat, 0, rows, :] for lat in range(lat_count)]
        b1 = [grad[lat, 1, rows, :] for lat in range(lat_count)]
        zero = jnp.zeros((8, chans), F32)
        y0, y1, z0, z1 = ([zero] * lat_count for _ in range(4))
        for index, (a, b) in enumerate(pairs):
            at = pl.ds(pl.multiple_of(index * padded_modes + i * 8, 8), 8)
            real = mixer_ref[at, :chans]
            imag = mixer_ref[at, chans:]
            h0 = h1 = zero
            for p, q in [(a, b)] if a == b else [(a, b), (b, a)]:
                y0[p] = y0[p] + real * a0[q] - imag * a1[q]
                y1[p] = y1[p] + imag * a0[q] + real * a1[q]
                z0[q] = z0[q] + real * b0[p] + imag * b1[p]
                z1[q] = z1[q] + real * b1[p] - imag * b0[p]
                h0 = h0 + b0[p] * a0[q] + b1[p] * a1[q]
                h1 = h1 + b1[p] * a0[q] - b0[p] * a1[q]
            products[at, :chans] = h0
            products[at, chans:] = h1
        for lat in range(lat_count):
            synth[lat, 0, rows, :] = y0[lat]
            synth[lat, 1, rows, :] = y1[lat]
            grad_coeff[lat, 0, rows, :] = z0[lat] * quad_ref[lat]
            grad_coeff[lat, 1, rows, :] = z1[lat] * quad_ref[lat]
        return carry

    lax.fori_loop(0, padded_modes // 8, mix, 0)
    used = len(pairs) * padded_modes
    if products.shape[0] > used:
        products[used:, :] = jnp.zeros((products.shape[0] - used, products.shape[1]), F32)
    gradient[...] = jnp.dot(
        back_ref[...], products[...].astype(BF16), preferred_element_type=F32
    )
    half = gradient.shape[0] // 2
    upper = jnp.bitwise_and(me, 1)
    for target, which in ((keep_ref, upper), (send_ref, 1 - upper)):
        part = gradient[pl.ds(pl.multiple_of(which * half, half), half), :]
        both = jnp.concatenate([part[:, :chans], part[:, chans:]], axis=0)
        target[...] = both.astype(target.dtype)
    for shift in range(blocks):
        block = jnp.bitwise_xor(me, shift)
        start = first_row_of(rows_ref, block, blocks)
        for slot in range(slots):
            lat = jnp.minimum(start + slot, lat_count - 1)
            for part in range(2):
                wide[(shift, *place(0, slot, part))] = synth[lat, part, :local_modes, :]
                wide[(shift, *place(1, slot, part))] = grad_coeff[lat, part, :local_modes, :]
        outs[shift][...] = wide[shift].astype(BF16)


def disco_inner(
    blocks, rows_ref, shift_ref, x_ref, dy_ref, act_ref, taps_ref,
    base_ref, slope_ref, base_grad_ref, tap_ref, acts, grads,
):
    slots, lon_count, chans = x_ref.shape
    taps = taps_ref.shape[0]
    me = lax.axis_index("space")
    live = rows_ref[me]
    start = first_row_of(rows_ref, me, blocks)
    for slot in range(slots):
        alive = jnp.where(slot < live, 1.0, 0.0)
        wrapped(acts, slot, act_ref[slot].astype(F32))
        wrapped(grads, slot, dy_ref[slot].astype(F32) * alive)
    acts[slots] = jnp.zeros(acts.shape[1:], F32)
    grads[slots] = jnp.zeros(grads.shape[1:], F32)
    weights = taps_ref[...].astype(F32)
    step = 32 if lon_count % 32 == 0 else lon_count
    totals = [jnp.zeros((8, chans), F32)] * taps
    top = shift_ref.shape[0] - 1
    for slot in range(slots):
        below = jnp.where(slot + 1 < live, slot + 1, slots)
        sources = [(1, slot)]
        if slot > 0:
            sources.append((0, slot - 1))
        if slot + 1 < slots:
            sources.append((2, below))
        lat = jnp.clip(start + slot, 0, top)
        ahead, behind = [], []
        for offset, row in sources:
            other = jnp.clip(lat + offset - 1, 0, top)
            for column in range(3):
                t = 3 * offset + column
                ahead.append((t, row, REACH + shift_ref[lat, t]))
                t = 3 * (2 - offset) + column
                behind.append((t, row, REACH - shift_ref[other, t]))

        def inner(i, totals):
            at = pl.multiple_of(i * step, step)
            part = pl.ds(at, step)
            x = x_ref[slot, part, :].astype(F32)
            dy = grads[slot, pl.ds(pl.multiple_of(REACH + at, 8), step), :]
            out = x
            back = jnp.zeros((step, chans), F32)
            fresh = list(totals)
            for t, row, first in ahead:
                moved = acts[row, pl.ds(at + first, step), :]
                out = out + moved * weights[t : t + 1, :]
                fresh[t] = fresh[t] + folded(moved * dy)
            for t, row, first in behind:
                back = back + grads[row, pl.ds(at + first, step), :] * weights[t : t + 1, :]
            slope = gelu_slope(x)
            base_ref[slot, part, :] = out
            slope_ref[slot, part, :] = slope
            base_grad_ref[slot, part, :] = dy + back * slope
            return tuple(fresh)

        totals = list(lax.fori_loop(0, lon_count // step, inner, tuple(totals)))
    lines = [jnp.sum(total, axis=0, keepdims=True) for total in totals]
    lines.append(jnp.zeros((tap_ref.shape[0] - taps, chans), F32))
    tap_ref[...] = jnp.concatenate(lines, axis=0)


def rim_kernel(
    blocks, rows_ref, shift_ref, dy_ref, first_rim, second_rim, taps_ref, inner_ref,
    rim_ref, rim_grad_ref, tap_ref, acts, grads,
):
    _, lon_count, chans = dy_ref.shape
    me = lax.axis_index("space")
    live = rows_ref[me]
    start = first_row_of(rows_ref, me, blocks)
    odd = jnp.bitwise_and(me, 1)
    for source, row in ((first_rim, 1 - odd), (second_rim, odd)):
        wrapped(acts, row, source[0].astype(F32))
        wrapped(grads, row, source[1].astype(F32))
    weights = taps_ref[...].astype(F32)
    step = 128 if lon_count % 128 == 0 else lon_count
    top = shift_ref.shape[0] - 1
    lines = [jnp.zeros((1, chans), F32)] * tap_ref.shape[0]
    for side in range(2):
        slot = 0 if side == 0 else live - 1
        lat = jnp.clip(start + slot, 0, top)
        other = jnp.clip(lat + 2 * side - 1, 0, top)
        ahead = [(t, REACH + shift_ref[lat, t]) for t in range(6 * side, 6 * side + 3)]
        behind = [(t, REACH - shift_ref[other, t]) for t in range(6 - 6 * side, 9 - 6 * side)]

        def rim(i, totals):
            at = pl.multiple_of(i * step, step)
            part = pl.ds(at, step)
            dy = dy_ref[slot, part, :].astype(F32)
            out = back = jnp.zeros((step, chans), F32)
            fresh = []
            for total, (t, first) in zip(totals, ahead):
                moved = acts[side, pl.ds(at + first, step), :]
                out = out + moved * weights[t : t + 1, :]
                fresh.append(total + folded(moved * dy))
            for t, first in behind:
                back = back + grads[side, pl.ds(at + first, step), :] * weights[t : t + 1, :]
            rim_ref[side, part, :] = out
            rim_grad_ref[side, part, :] = back
            return tuple(fresh)

        totals = lax.fori_loop(0, lon_count // step, rim, (jnp.zeros((8, chans), F32),) * 3)
        for (t, _), total in zip(ahead, totals):
            lines[t] = jnp.sum(total, axis=0, keepdims=True)
    tap_ref[...] = inner_ref[...] + jnp.concatenate(lines, axis=0)


def split_taps(taps, out_ref, count):
    high = taps.astype(BF16)
    out_ref[count : count + TAP_ROWS, :] = high
    out_ref[count + TAP_ROWS :, :] = (taps - high.astype(F32)).astype(BF16)


def joined_taps(rows):
    return rows[-2 * TAP_ROWS : -TAP_ROWS, :] + rows[-TAP_ROWS:, :]


def split_taps(taps, out_ref, count):
    high = taps.astype(BF16)
    out_ref[count : count + TAP_ROWS, :] = high
    out_ref[count + TAP_ROWS :, :] = (taps - high.astype(F32)).astype(BF16)


def joined_taps(ref):
    rows = ref[ref.shape[0] - 2 * TAP_ROWS :, :].astype(F32)
    return rows[:TAP_ROWS, :] + rows[TAP_ROWS:, :]


def added(first_ref, second_ref):
    return first_ref[...].astype(F32) + second_ref[...].astype(F32)


def half_kernel(kept_ref, got_ref, tap_ref, out_ref):
    out_ref[: kept_ref.shape[0], :] = added(kept_ref, got_ref).astype(BF16)
    split_taps(tap_ref[...], out_ref, kept_ref.shape[0])


def add_kernel(own_ref, other_ref, out_ref, *cut_refs):
    count = own_ref.shape[0] - 2 * TAP_ROWS
    out_ref[:count, :] = added(own_ref, other_ref)[:count, :].astype(BF16)
    split_taps(joined_taps(own_ref) + joined_taps(other_ref), out_ref, count)
    for at, cut_ref in enumerate(cut_refs):
        rows = cut_ref.shape[0]
        cut_ref[...] = out_ref[at * rows : (at + 1) * rows, :]


def member_kernel(scale, tap_scale, own_ref, head_ref, tail_ref, out_ref, *cut_refs):
    count, head = own_ref.shape[0] - 2 * TAP_ROWS, head_ref.shape[0]
    out_ref[:head, :] = (
        (own_ref[:head, :].astype(F32) + head_ref[...].astype(F32)) / scale
    ).astype(BF16)
    tail = own_ref[head:, :].astype(F32) + tail_ref[...].astype(F32)
    out_ref[head:count, :] = (tail[: count - head, :] / scale).astype(BF16)
    taps = joined_taps(own_ref) + joined_taps(tail_ref)
    split_taps(taps / tap_scale, out_ref, count)
    for at, cut_ref in enumerate(cut_refs):
        rows = cut_ref.shape[0]
        cut_ref[...] = out_ref[at * rows : (at + 1) * rows, :]


def early_kernel(
    rows_ref, table_ref, base_ref, slope_ref, base_grad_ref, rim_ref, rim_grad_ref,
    own_ref, near_ref, sum_ref, grad_ref,
):
    slots, lon_count, chans = base_ref.shape
    me = lax.axis_index("space")
    live = rows_ref[me]
    step = lon_count // 4
    for at in range(0, lon_count, step):
        rows = slice(at, at + step)
        sums = jnp.dot(table_ref[me, rows, :], own_ref[...], preferred_element_type=F32)
        sums = sums + jnp.dot(
            table_ref[jnp.bitwise_xor(me, 1), rows, :], near_ref[...], preferred_element_type=F32
        )
        for slot in range(slots):
            out = base_ref[slot, rows, :] + sums[:, slot * chans : (slot + 1) * chans]
            back = sums[:, (slots + slot) * chans : (slots + slot + 1) * chans]
            if slot == 0:
                out = out + rim_ref[0, rows, :]
                back = back + rim_grad_ref[0, rows, :]
            last = slot == live - 1
            out = out + jnp.where(last, rim_ref[1, rows, :], 0.0)
            back = back + jnp.where(last, rim_grad_ref[1, rows, :], 0.0)
            sum_ref[slot, rows, :] = out
            grad_ref[slot, rows, :] = base_grad_ref[slot, rows, :] + back * slope_ref[slot, rows, :]


def finish_kernel(
    blocks, rows_ref, table_ref, sum_ref, early_ref, slope_ref, own_ref, other_ref, *refs
):
    ins, outs, scratch = refs[: blocks - 2], refs[blocks - 2 : blocks + 2], refs[blocks + 2 :]
    out_hbm, grad_hbm, filter_hbm, tap_ref = outs
    out_ref, grad_ref, filter_ref, sems = scratch
    slots, lon_count, chans = sum_ref.shape
    me = lax.axis_index("space")
    live = rows_ref[me]
    half = filter_ref.shape[1] // 2
    upper = jnp.bitwise_and(me, 1)
    for ref, which in ((own_ref, upper), (other_ref, 1 - upper)):
        at = pl.ds(pl.multiple_of(which * half, half), half)
        rows = ref[: 2 * half, :].astype(F32)
        filter_ref[0, at, :] = rows[:half, :]
        filter_ref[1, at, :] = rows[half:, :]
    tap_ref[...] = (joined_taps(own_ref) + joined_taps(other_ref))[: tap_ref.shape[0], :]
    stores = [pltpu.make_async_copy(filter_ref, filter_hbm, sems.at[0])]
    stores[0].start()
    parts = sems.shape[0] // (2 * slots)
    step = lon_count // parts
    for part in range(parts):
        rows = slice(part * step, (part + 1) * step)
        sums = jnp.zeros((step, 2 * slots * chans), F32)
        for at, ref in enumerate(ins):
            block = jnp.bitwise_xor(me, at + 2)
            sums = sums + jnp.dot(table_ref[block, rows, :], ref[...], preferred_element_type=F32)
        for slot in range(slots):
            out = sum_ref[slot, rows, :] + sums[:, slot * chans : (slot + 1) * chans]
            back = sums[:, (slots + slot) * chans : (slots + slot + 1) * chans]
            grad = early_ref[slot, rows, :] + back * slope_ref[slot, rows, :]
            alive = slot < live
            out_ref[slot, rows, :] = jnp.where(alive, out, 0.0).astype(BF16)
            grad_ref[slot, rows, :] = jnp.where(alive, grad, 0.0).astype(BF16)
            for made, target in ((out_ref, out_hbm), (grad_ref, grad_hbm)):
                place = (slot, pl.ds(part * step, step))
                stores.append(
                    pltpu.make_async_copy(made.at[place], target.at[place], sems.at[len(stores)])
                )
                stores[-1].start()
    for store in stores:
        store.wait()


def crossed(values, distance, axis="space"):
    count = lax.axis_size(axis)
    return lax.ppermute(values, axis, [(i, i ^ distance) for i in range(count)])


def crossed_all(parts, distances):
    return {s: crossed(parts[s], s) for s in distances}


def body(
    fields, cotangent, band_rows, tap_shift, quad_weight, legendre, spectral_filter, tap_weight
):
    blocks = lax.axis_size("space")
    members = lax.axis_size("ens")
    _, slots, lon_count, chans = fields.shape
    local_modes, lat_count, degrees = legendre.shape
    padded_modes = round_up(local_modes, 16)
    depth = round_up(2 * local_modes, 8)
    pairs = len(lat_pairs(lat_count))
    pair_rows = round_up(pairs * padded_modes, 128)
    share = 2 * degrees // blocks
    big = 32 if pair_rows <= 4096 else 60
    shape = jax.ShapeDtypeStruct
    table = fourier_table(lon_count, blocks, local_modes, depth)
    table_in = jnp.asarray(table)
    table_out = jnp.asarray(np.ascontiguousarray(table.transpose(0, 2, 1)))
    x, dy = fields[0], cotangent[0]
    field = shape((slots, lon_count, chans), F32)
    coded = shape((depth, 2 * slots * chans), BF16)
    rim = shape((2, lon_count, chans), BF16)

    coded_parts = call(
        functools.partial(forward_kernel, blocks),
        [coded] * blocks,
        [HBM] * 3,
        (x, dy, table_in),
        scratch=[
            pltpu.VMEM(x.shape, BF16),
            pltpu.VMEM(dy.shape, BF16),
            pltpu.VMEM(table.shape, BF16),
            pltpu.VMEM(x.shape, BF16),
            pltpu.SemaphoreType.DMA((3,)),
        ],
        limit=60,
        flops=2 * blocks * depth * lon_count * 2 * slots * chans,
    )
    far = list(range(blocks - 1, 0, -1))
    got = [coded_parts[0], *reversed(crossed_all(coded_parts, far).values())]
    leg_rows = jnp.pad(
        jnp.transpose(legendre, (1, 0, 2)), ((0, 0), (0, padded_modes - local_modes), (0, 0))
    )
    padded = (lon_count + 2 * REACH, chans)
    tap_shape = shape((TAP_ROWS, chans), F32)
    mixer, back, first_rim, second_rim, base, slope, base_grad, tap_part = call(
        functools.partial(prepare_kernel, local_modes, blocks),
        [shape((pair_rows, 2 * chans), F32), shape((degrees, pair_rows), BF16), rim, rim]
        + [field, field, field, tap_shape],
        [SMEM, SMEM] + [VMEM] * 5,
        (band_rows, tap_shift, leg_rows, spectral_filter, x, dy, tap_weight),
        scratch=[pltpu.VMEM((pair_rows, degrees), BF16), pltpu.VMEM(x.shape, BF16)]
        + [pltpu.VMEM((slots + 1, *padded), F32)] * 2,
        limit=big,
        flops=2 * pair_rows * degrees * 2 * chans,
        moved=8 * pair_rows * chans,
    )
    first_rim, second_rim, got[-1] = lax.optimization_barrier((first_rim, second_rim, got[-1]))
    first_rim = crossed(first_rim, 1)
    inner = [(i, i ^ 1) for i in range(blocks)]
    inner = [(i + 1, j + 1) for i, j in inner if max(i, j) + 1 < blocks]
    second_rim = lax.ppermute(second_rim, "space", inner)
    spectral = pltpu.VMEM((lat_count, 2, padded_modes, chans), F32)
    mixed = call(
        functools.partial(mix_kernel, blocks, slots, lat_count, local_modes),
        [coded] * blocks + [shape((degrees, chans), F32), shape((degrees, chans), BF16)],
        [SMEM, SMEM] + [VMEM] * (2 + blocks),
        (band_rows, quad_weight, mixer, back, *got),
        scratch=[spectral] * 4
        + [pltpu.VMEM((pair_rows, 2 * chans), F32), pltpu.VMEM((degrees, 2 * chans), F32)]
        + [pltpu.VMEM((blocks, *coded.shape), F32)],
        limit=big,
        flops=20 * degrees * pair_rows * 2 * chans,
    )
    back_parts, keep, send = mixed[:blocks], mixed[blocks], mixed[blocks + 1]
    got_sum = crossed(send, 1)
    rim_sum, rim_grad, tap_part = call(
        functools.partial(rim_kernel, blocks),
        [shape((2, lon_count, chans), F32)] * 2 + [tap_shape],
        [SMEM, SMEM] + [VMEM] * 5,
        (band_rows, tap_shift, dy, first_rim, second_rim, tap_weight, tap_part),
        scratch=[pltpu.VMEM((2, *padded), F32)] * 2,
    )
    got_sum, tap_part = lax.optimization_barrier((got_sum, tap_part))
    message = shape((degrees + 2 * TAP_ROWS, chans), BF16)
    own = call(half_kernel, message, [VMEM] * 3, (keep, got_sum, tap_part))
    back_parts, own = lax.optimization_barrier((back_parts, own))
    returned = [back_parts[0], *reversed(crossed_all(back_parts, far).values())]
    cut = shape((message.shape[0] // 2, chans), BF16)
    for bit in range(1, blocks.bit_length() - 1):
        own, *cuts = call(
            add_kernel, [message, cut, cut], [VMEM] * 2, (own, crossed(own, 1 << bit))
        )
    for bit in range(members.bit_length() - 1):
        last = bit == members.bit_length() - 2
        scales = (members, members * lat_count) if last else (1, 1)
        own, *cuts = call(
            functools.partial(member_kernel, *scales),
            [message] if last else [message, cut, cut],
            [VMEM] * 3,
            (own, *[crossed(part, 1 << bit, "ens") for part in cuts]),
            flops=300000000,
        )
    early_sum, early_grad = call(
        early_kernel,
        [field, field],
        [SMEM] + [VMEM] * 8,
        (band_rows, table_out, base, slope, base_grad, rim_sum, rim_grad, *returned[:2]),
    )
    pieces = 4
    output, input_grad, filter_grad, tap_grad = call(
        functools.partial(finish_kernel, blocks),
        [shape(x.shape, BF16)] * 2
        + [shape((2, degrees, chans), F32), shape((tap_weight.shape[0], chans), F32)],
        [SMEM] + [VMEM] * (4 + blocks),
        (
            band_rows, table_out, early_sum, early_grad, slope,
            own, crossed(own, 1), *returned[2:],
        ),
        scratch=[
            pltpu.VMEM(x.shape, BF16),
            pltpu.VMEM(x.shape, BF16),
            pltpu.VMEM((2, degrees, chans), F32),
            pltpu.SemaphoreType.DMA((1 + 2 * slots * pieces,)),
        ],
        flops=2 * blocks * depth * lon_count * 2 * slots * chans,
        out_specs=[HBM, HBM, HBM, VMEM],
    )
    return (output[None], input_grad[None], filter_grad, tap_grad)


def solution(mesh):
    in_specs = (
        P(("groups", "ens"), "space", None, "chan"),
        P(("groups", "ens"), "space", None, "chan"),
        P("groups"),
        P(),
        P(),
        P("space", None, None),
        P(None, None, "chan"),
        P(None, "chan"),
    )
    out_specs = (
        P(("groups", "ens"), "space", None, "chan"),
        P(("groups", "ens"), "space", None, "chan"),
        P("groups", None, "chan"),
        P("groups", "chan"),
    )
    return jax.shard_map(body, mesh=mesh, in_specs=in_specs, out_specs=out_specs, check_vma=False)
```

```python
import functools
import math

import jax
import jax.numpy as jnp
import ml_dtypes
import numpy as np
from jax import lax
from jax.experimental import pallas as pl
from jax.experimental.pallas import tpu as pltpu
from jax.sharding import PartitionSpec as P

F32 = jnp.float32
BF16 = jnp.bfloat16
VMEM = pl.BlockSpec(memory_space=pltpu.VMEM)
SMEM = pl.BlockSpec(memory_space=pltpu.SMEM)
HBM = pl.BlockSpec(memory_space=pltpu.HBM)
REACH = 8
TAP_ROWS = 16


def gelu_value(values):
    return 0.5 * values * (1.0 + lax.erf(values * 0.7071067811865476))


def gelu_slope(values):
    return (
        0.5 * (1.0 + lax.erf(values * 0.7071067811865476))
        + values * jnp.exp(-0.5 * values * values) * 0.3989422804014327
    )


def round_up(count, step):
    return -(-count // step) * step


def fourier_table(lon_count, blocks, local_modes, depth):
    lon_ids = np.arange(lon_count)
    mode_ids = np.arange(blocks * local_modes)
    phase = (mode_ids[:, None] * lon_ids[None, :] % lon_count) * (2.0 * math.pi / lon_count)
    factor = 1.0 / math.sqrt(lon_count)
    both = np.stack([np.cos(phase), -np.sin(phase)]) * factor
    both = both.reshape(2, blocks, local_modes, lon_count).transpose(1, 0, 2, 3)
    both = both.reshape(blocks, 2 * local_modes, lon_count)
    both = np.pad(both, ((0, 0), (0, depth - 2 * local_modes), (0, 0)))
    return both.astype(ml_dtypes.bfloat16)


def lat_pairs(lat_count):
    return [(a, b) for a in range(lat_count) for b in range(a, lat_count)]


def first_row_of(rows_ref, block, blocks):
    total = jnp.int32(0)
    for other in range(blocks):
        total = total + jnp.where(other < block, rows_ref[other], 0)
    return total


def call(kernel, out_shape, in_specs, args, scratch=(), limit=32, flops=0, moved=1024, out_specs=None):
    return pl.pallas_call(
        kernel,
        out_shape=out_shape,
        in_specs=in_specs,
        out_specs=out_specs or jax.tree.map(lambda _: VMEM, out_shape),
        scratch_shapes=list(scratch),
        compiler_params=pltpu.CompilerParams(vmem_limit_bytes=limit * 1024 * 1024),
        cost_estimate=pl.CostEstimate(flops=flops, bytes_accessed=moved, transcendentals=0),
    )(*args)


def activate(x_ref, act_ref):
    slots, lon_count, _ = x_ref.shape
    step = 64 if lon_count % 64 == 0 else lon_count

    def run(i, carry):
        part = pl.ds(pl.multiple_of(i * step, step), step)
        for slot in range(slots):
            act_ref[slot, part, :] = gelu_value(x_ref[slot, part, :].astype(F32)).astype(BF16)
        return carry

    lax.fori_loop(0, lon_count // step, run, 0)


def forward_kernel(blocks, x_hbm, dy_hbm, table_hbm, *refs):
    outs, (x_ref, dy_ref, table_ref, act_ref, sems) = refs[:blocks], refs[blocks:]
    slots = x_ref.shape[0]
    me = lax.axis_index("space")
    loads = [
        pltpu.make_async_copy(source, target, sems.at[i])
        for i, (source, target) in enumerate(
            [(x_hbm, x_ref), (dy_hbm, dy_ref), (table_hbm, table_ref)]
        )
    ]
    for load in loads:
        load.start()
    loads[0].wait()
    activate(x_ref, act_ref)
    loads[1].wait()
    source = jnp.concatenate(
        [dy_ref[slot] for slot in range(slots)] + [act_ref[slot] for slot in range(slots)], axis=-1
    )
    loads[2].wait()
    for shift in range(blocks):
        block = jnp.bitwise_xor(me, shift)
        sums = jnp.dot(table_ref[block], source, preferred_element_type=F32)
        outs[shift][...] = sums.astype(BF16)


def wrapped(target, row, value):
    lon_count = value.shape[0]
    target[row, REACH : REACH + lon_count, :] = value
    target[row, :REACH, :] = value[lon_count - REACH :, :]
    target[row, REACH + lon_count :, :] = value[:REACH, :]


def folded(values):
    return jnp.sum(values.reshape(values.shape[0] // 8, 8, values.shape[1]), axis=0)


def prepare_kernel(
    local_modes, blocks, rows_ref, shift_ref, leg_ref, filter_ref, x_ref, dy_ref, taps_ref,
    mixer_ref, back_ref, first_rim, second_rim, base_ref, slope_ref, base_grad_ref, tap_ref,
    pairs_ref, act_ref, acts, grads,
):
    me = lax.axis_index("space")
    activate(x_ref, act_ref)
    last = rows_ref[me] - 1
    odd = jnp.bitwise_and(me, 1)
    for rim_ref, row in ((first_rim, last * (1 - odd)), (second_rim, last * odd)):
        rim_ref[0] = act_ref[row]
        rim_ref[1] = dy_ref[row]
    pair_products(local_modes, leg_ref, filter_ref, mixer_ref, back_ref, pairs_ref)
    disco_inner(
        blocks, rows_ref, shift_ref, x_ref, dy_ref, act_ref, taps_ref,
        base_ref, slope_ref, base_grad_ref, tap_ref, acts, grads,
    )


def pair_products(local_modes, leg_ref, filter_ref, mixer_ref, back_ref, pairs_ref):
    me = lax.axis_index("space")
    lat_count, padded_modes, _ = leg_ref.shape
    pairs = lat_pairs(lat_count)
    used = len(pairs) * padded_modes
    mode = me * local_modes + lax.broadcasted_iota(
        jnp.int32, (padded_modes, 1), 0
    )
    twice = jnp.where(mode == 0, 1.0, 2.0)
    for index, (a, b) in enumerate(pairs):
        at = index * padded_modes
        pairs_ref[at : at + padded_modes, :] = (
            leg_ref[a].astype(F32) * leg_ref[b].astype(F32) * twice
        ).astype(BF16)
    if pairs_ref.shape[0] > used:
        pairs_ref[used:, :] = jnp.zeros((pairs_ref.shape[0] - used, pairs_ref.shape[1]), BF16)
    both = jnp.concatenate([filter_ref[0], filter_ref[1]], axis=-1)
    mixer_ref[...] = jnp.dot(pairs_ref[...], both, preferred_element_type=F32)

    def turn(i, carry):
        part = pl.ds(pl.multiple_of(i * 128, 128), 128)
        back_ref[:, part] = pairs_ref[part, :].astype(F32).T.astype(BF16)
        return carry

    lax.fori_loop(0, pairs_ref.shape[0] // 128, turn, 0)


def own_quarter():
    space_bit = jnp.bitwise_and(lax.axis_index("space"), 1)
    return 2 * space_bit + jnp.bitwise_and(lax.axis_index("ens"), 1)


def gradient_kernel(blocks, slots, lat_count, local_modes, rows_ref, quad_ref, back_ref, *refs):
    ins, sums, coeff, grad = refs[:blocks], refs[blocks : blocks + 4], *refs[blocks + 4 : blocks + 6]
    products, gradient, wide = refs[blocks + 6 :]
    padded_modes, chans = coeff.shape[2:]
    me = lax.axis_index("space")
    pairs = lat_pairs(lat_count)
    padding = padded_modes - local_modes
    if padding > 0:
        zeros = jnp.zeros((padding, chans), F32)
        for lat in range(lat_count):
            for part in range(2):
                coeff[lat, part, local_modes:, :] = zeros
                grad[lat, part, local_modes:, :] = zeros

    for shift in range(blocks):
        block = jnp.bitwise_xor(me, shift)
        start = first_row_of(rows_ref, block, blocks)
        wide[shift] = ins[shift][...].astype(F32)
        for slot in range(slots):
            lat = jnp.minimum(start + slot, lat_count - 1)

            @pl.when(slot < rows_ref[block])
            def _():
                weight = quad_ref[lat]
                for part in range(2):
                    grad[lat, part, :local_modes, :] = wide[(shift, *place(slots, local_modes, chans, 0, slot, part))]
                    coeff[lat, part, :local_modes, :] = (
                        wide[(shift, *place(slots, local_modes, chans, 1, slot, part))] * weight
                    )

    def multiply(i, carry):
        rows = pl.ds(pl.multiple_of(i * 8, 8), 8)
        a0, a1, b0, b1 = loaded(coeff, grad, rows)
        for index, (a, b) in enumerate(pairs):
            at = pl.ds(pl.multiple_of(index * padded_modes + i * 8, 8), 8)
            h0 = h1 = jnp.zeros((8, chans), F32)
            for p, q in [(a, b)] if a == b else [(a, b), (b, a)]:
                h0 = h0 + b0[p] * a0[q] + b1[p] * a1[q]
                h1 = h1 + b1[p] * a0[q] - b0[p] * a1[q]
            products[at, :chans] = h0
            products[at, chans:] = h1
        return carry

    lax.fori_loop(0, padded_modes // 8, multiply, 0)
    used = len(pairs) * padded_modes
    if products.shape[0] > used:
        products[used:, :] = jnp.zeros((products.shape[0] - used, products.shape[1]), F32)
    gradient[...] = jnp.dot(
        back_ref[...], products[...].astype(BF16), preferred_element_type=F32
    )
    share = gradient.shape[0] // 4
    for shift, target in enumerate(sums):
        at = jnp.bitwise_xor(own_quarter(), shift) * share
        part = gradient[pl.ds(pl.multiple_of(at, share), share), :]
        both = jnp.concatenate([part[:, :chans], part[:, chans:]], axis=0)
        target[...] = both.astype(target.dtype)


def loaded(coeff, grad, rows):
    return [
        [ref[lat, part, rows, :] for lat in range(ref.shape[0])]
        for ref in (coeff, grad)
        for part in range(2)
    ]


def place(slots, local_modes, chans, field, slot, part):
    at = (field * slots + slot) * chans
    return slice(part * local_modes, (part + 1) * local_modes), slice(at, at + chans)


def return_kernel(blocks, local_modes, rows_ref, quad_ref, mixer_ref, coeff, grad, *refs):
    outs, (synth, grad_coeff, wide) = refs[:blocks], refs[blocks:]
    lat_count, _, padded_modes, chans = coeff.shape
    slots = wide.shape[1] // (2 * chans)
    me = lax.axis_index("space")
    pairs = lat_pairs(lat_count)

    def mix(i, carry):
        rows = pl.ds(pl.multiple_of(i * 8, 8), 8)
        a0, a1, b0, b1 = loaded(coeff, grad, rows)
        zero = jnp.zeros((8, chans), F32)
        y0, y1, z0, z1 = ([zero] * lat_count for _ in range(4))
        for index, (a, b) in enumerate(pairs):
            at = pl.ds(pl.multiple_of(index * padded_modes + i * 8, 8), 8)
            real = mixer_ref[at, :chans]
            imag = mixer_ref[at, chans:]
            for p, q in [(a, b)] if a == b else [(a, b), (b, a)]:
                y0[p] = y0[p] + real * a0[q] - imag * a1[q]
                y1[p] = y1[p] + imag * a0[q] + real * a1[q]
                z0[q] = z0[q] + real * b0[p] + imag * b1[p]
                z1[q] = z1[q] + real * b1[p] - imag * b0[p]
        for lat in range(lat_count):
            synth[lat, 0, rows, :] = y0[lat]
            synth[lat, 1, rows, :] = y1[lat]
            grad_coeff[lat, 0, rows, :] = z0[lat] * quad_ref[lat]
            grad_coeff[lat, 1, rows, :] = z1[lat] * quad_ref[lat]
        return carry

    lax.fori_loop(0, padded_modes // 8, mix, 0)
    if wide.shape[0] > 2 * local_modes:
        wide[2 * local_modes :, :] = jnp.zeros(
            (wide.shape[0] - 2 * local_modes, wide.shape[1]), F32
        )
    for shift in range(blocks):
        block = jnp.bitwise_xor(me, shift)
        start = first_row_of(rows_ref, block, blocks)
        for slot in range(slots):
            lat = jnp.minimum(start + slot, lat_count - 1)
            for part in range(2):
                at = place(slots, local_modes, chans, 0, slot, part)
                wide[at] = synth[lat, part, :local_modes, :]
                at = place(slots, local_modes, chans, 1, slot, part)
                wide[at] = grad_coeff[lat, part, :local_modes, :]
        outs[shift][...] = wide[...].astype(BF16)


def disco_inner(
    blocks, rows_ref, shift_ref, x_ref, dy_ref, act_ref, taps_ref,
    base_ref, slope_ref, base_grad_ref, tap_ref, acts, grads,
):
    slots, lon_count, chans = x_ref.shape
    taps = taps_ref.shape[0]
    me = lax.axis_index("space")
    live = rows_ref[me]
    start = first_row_of(rows_ref, me, blocks)
    for slot in range(slots):
        alive = jnp.where(slot < live, 1.0, 0.0)
        wrapped(acts, slot, act_ref[slot].astype(F32))
        wrapped(grads, slot, dy_ref[slot].astype(F32) * alive)
    acts[slots] = jnp.zeros(acts.shape[1:], F32)
    grads[slots] = jnp.zeros(grads.shape[1:], F32)
    weights = taps_ref[...].astype(F32)
    step = 32 if lon_count % 32 == 0 else lon_count
    totals = [jnp.zeros((8, chans), F32)] * taps
    top = shift_ref.shape[0] - 1
    for slot in range(slots):
        below = jnp.where(slot + 1 < live, slot + 1, slots)
        sources = [(1, slot)]
        if slot > 0:
            sources.append((0, slot - 1))
        if slot + 1 < slots:
            sources.append((2, below))
        lat = jnp.clip(start + slot, 0, top)
        ahead, behind = [], []
        for offset, row in sources:
            other = jnp.clip(lat + offset - 1, 0, top)
            for column in range(3):
                t = 3 * offset + column
                ahead.append((t, row, REACH + shift_ref[lat, t]))
                t = 3 * (2 - offset) + column
                behind.append((t, row, REACH - shift_ref[other, t]))

        def inner(i, totals):
            at = pl.multiple_of(i * step, step)
            part = pl.ds(at, step)
            x = x_ref[slot, part, :].astype(F32)
            dy = grads[slot, pl.ds(pl.multiple_of(REACH + at, 8), step), :]
            out = x
            back = jnp.zeros((step, chans), F32)
            fresh = list(totals)
            for t, row, first in ahead:
                moved = acts[row, pl.ds(at + first, step), :]
                out = out + moved * weights[t : t + 1, :]
                fresh[t] = fresh[t] + folded(moved * dy)
            for t, row, first in behind:
                back = back + grads[row, pl.ds(at + first, step), :] * weights[t : t + 1, :]
            slope = gelu_slope(x)
            base_ref[slot, part, :] = out
            slope_ref[slot, part, :] = slope
            base_grad_ref[slot, part, :] = dy + back * slope
            return tuple(fresh)

        totals = list(lax.fori_loop(0, lon_count // step, inner, tuple(totals)))
    lines = [jnp.sum(total, axis=0, keepdims=True) for total in totals]
    lines.append(jnp.zeros((tap_ref.shape[0] - taps, chans), F32))
    tap_ref[...] = jnp.concatenate(lines, axis=0)


def rim_kernel(
    blocks, rows_ref, shift_ref, dy_ref, first_rim, second_rim, taps_ref, inner_ref,
    rim_ref, rim_grad_ref, tap_ref, acts, grads,
):
    _, lon_count, chans = dy_ref.shape
    me = lax.axis_index("space")
    live = rows_ref[me]
    start = first_row_of(rows_ref, me, blocks)
    odd = jnp.bitwise_and(me, 1)
    for source, row in ((first_rim, 1 - odd), (second_rim, odd)):
        wrapped(acts, row, source[0].astype(F32))
        wrapped(grads, row, source[1].astype(F32))
    weights = taps_ref[...].astype(F32)
    step = 128 if lon_count % 128 == 0 else lon_count
    top = shift_ref.shape[0] - 1
    lines = [jnp.zeros((1, chans), F32)] * tap_ref.shape[0]
    for side in range(2):
        slot = 0 if side == 0 else live - 1
        lat = jnp.clip(start + slot, 0, top)
        other = jnp.clip(lat + 2 * side - 1, 0, top)
        ahead = [(t, REACH + shift_ref[lat, t]) for t in range(6 * side, 6 * side + 3)]
        behind = [(t, REACH - shift_ref[other, t]) for t in range(6 - 6 * side, 9 - 6 * side)]

        def rim(i, totals):
            at = pl.multiple_of(i * step, step)
            part = pl.ds(at, step)
            dy = dy_ref[slot, part, :].astype(F32)
            out = back = jnp.zeros((step, chans), F32)
            fresh = []
            for total, (t, first) in zip(totals, ahead):
                moved = acts[side, pl.ds(at + first, step), :]
                out = out + moved * weights[t : t + 1, :]
                fresh.append(total + folded(moved * dy))
            for t, first in behind:
                back = back + grads[side, pl.ds(at + first, step), :] * weights[t : t + 1, :]
            rim_ref[side, part, :] = out
            rim_grad_ref[side, part, :] = back
            return tuple(fresh)

        totals = lax.fori_loop(0, lon_count // step, rim, (jnp.zeros((8, chans), F32),) * 3)
        for (t, _), total in zip(ahead, totals):
            lines[t] = jnp.sum(total, axis=0, keepdims=True)
    tap_ref[...] = inner_ref[...] + jnp.concatenate(lines, axis=0)


def split_taps(taps, out_ref, count):
    high = taps.astype(BF16)
    out_ref[count : count + TAP_ROWS, :] = high
    out_ref[count + TAP_ROWS :, :] = (taps - high.astype(F32)).astype(BF16)


def joined_taps(rows):
    return rows[-2 * TAP_ROWS : -TAP_ROWS, :] + rows[-TAP_ROWS:, :]


def split_taps(taps, out_ref, count):
    high = taps.astype(BF16)
    out_ref[count : count + TAP_ROWS, :] = high
    out_ref[count + TAP_ROWS :, :] = (taps - high.astype(F32)).astype(BF16)


def joined_taps(ref):
    rows = ref[ref.shape[0] - 2 * TAP_ROWS :, :].astype(F32)
    return rows[:TAP_ROWS, :] + rows[TAP_ROWS:, :]


def added(first_ref, second_ref):
    return first_ref[...].astype(F32) + second_ref[...].astype(F32)


def quarter_kernel(kept_ref, first_ref, second_ref, third_ref, tap_ref, out_ref):
    total = kept_ref[...]
    for ref in (first_ref, second_ref, third_ref):
        total = total + ref[...].astype(F32)
    out_ref[: total.shape[0], :] = total.astype(BF16)
    split_taps(tap_ref[...], out_ref, total.shape[0])


def add_kernel(scale, tap_scale, own_ref, other_ref, out_ref):
    count = own_ref.shape[0] - 2 * TAP_ROWS
    out_ref[:count, :] = (added(own_ref, other_ref)[:count, :] / scale).astype(BF16)
    split_taps((joined_taps(own_ref) + joined_taps(other_ref)) / tap_scale, out_ref, count)


def early_kernel(
    rows_ref, table_ref, base_ref, slope_ref, base_grad_ref, rim_ref, rim_grad_ref,
    own_ref, near_ref, sum_ref, grad_ref,
):
    slots, lon_count, chans = base_ref.shape
    me = lax.axis_index("space")
    live = rows_ref[me]
    step = lon_count // 4
    for at in range(0, lon_count, step):
        rows = slice(at, at + step)
        sums = jnp.dot(table_ref[me, rows, :], own_ref[...], preferred_element_type=F32)
        sums = sums + jnp.dot(
            table_ref[jnp.bitwise_xor(me, 1), rows, :], near_ref[...], preferred_element_type=F32
        )
        for slot in range(slots):
            out = base_ref[slot, rows, :] + sums[:, slot * chans : (slot + 1) * chans]
            back = sums[:, (slots + slot) * chans : (slots + slot + 1) * chans]
            if slot == 0:
                out = out + rim_ref[0, rows, :]
                back = back + rim_grad_ref[0, rows, :]
            last = slot == live - 1
            out = out + jnp.where(last, rim_ref[1, rows, :], 0.0)
            back = back + jnp.where(last, rim_grad_ref[1, rows, :], 0.0)
            sum_ref[slot, rows, :] = out
            grad_ref[slot, rows, :] = base_grad_ref[slot, rows, :] + back * slope_ref[slot, rows, :]


def finish_kernel(
    blocks, rows_ref, table_ref, sum_ref, early_ref, slope_ref, *refs
):
    quarters, ins, refs = refs[:4], refs[4 : blocks + 2], refs[blocks + 2 :]
    out_hbm, grad_hbm, filter_hbm, tap_ref, out_ref, grad_ref, filter_ref, held, sems = refs
    slots, lon_count, chans = sum_ref.shape
    me = lax.axis_index("space")
    live = rows_ref[me]
    share = filter_ref.shape[1] // 4
    for shift, ref in enumerate(quarters):
        quarter = jnp.bitwise_xor(own_quarter(), shift)
        at = pl.ds(pl.multiple_of(quarter * share, share), share)
        rows = ref[: 2 * share, :].astype(F32)
        filter_ref[0, at, :] = rows[:share, :]
        filter_ref[1, at, :] = rows[share:, :]
        held[quarter] = joined_taps(ref)
    taps = (held[0] + held[1]) + (held[2] + held[3])
    tap_ref[...] = taps[: tap_ref.shape[0], :]
    stores = [pltpu.make_async_copy(filter_ref, filter_hbm, sems.at[0])]
    stores[0].start()
    parts = sems.shape[0] // (2 * slots)
    step = lon_count // parts
    for part in range(parts):
        rows = slice(part * step, (part + 1) * step)
        sums = jnp.zeros((step, 2 * slots * chans), F32)
        for at, ref in enumerate(ins):
            block = jnp.bitwise_xor(me, at + 2)
            sums = sums + jnp.dot(table_ref[block, rows, :], ref[...], preferred_element_type=F32)
        for slot in range(slots):
            out = sum_ref[slot, rows, :] + sums[:, slot * chans : (slot + 1) * chans]
            back = sums[:, (slots + slot) * chans : (slots + slot + 1) * chans]
            grad = early_ref[slot, rows, :] + back * slope_ref[slot, rows, :]
            alive = slot < live
            out_ref[slot, rows, :] = jnp.where(alive, out, 0.0).astype(BF16)
            grad_ref[slot, rows, :] = jnp.where(alive, grad, 0.0).astype(BF16)
            for made, target in ((out_ref, out_hbm), (grad_ref, grad_hbm)):
                place = (slot, pl.ds(part * step, step))
                stores.append(
                    pltpu.make_async_copy(made.at[place], target.at[place], sems.at[len(stores)])
                )
                stores[-1].start()
    for store in stores:
        store.wait()


def crossed(values, distance, axis="space"):
    count = lax.axis_size(axis)
    return lax.ppermute(values, axis, [(i, i ^ distance) for i in range(count)])


def around(parts):
    count = lax.axis_size("space") * lax.axis_size("ens")
    flip = lax.axis_size("ens") + 1
    return [
        crossed(parts[0], 1, "ens"),
        crossed(parts[1], 1),
        lax.ppermute(parts[2], ("space", "ens"), [(i, i ^ flip) for i in range(count)]),
    ]


def crossed_all(parts, distances):
    return {s: crossed(parts[s], s) for s in distances}


def body(
    fields, cotangent, band_rows, tap_shift, quad_weight, legendre, spectral_filter, tap_weight
):
    blocks = lax.axis_size("space")
    members = lax.axis_size("ens")
    _, slots, lon_count, chans = fields.shape
    local_modes, lat_count, degrees = legendre.shape
    padded_modes = round_up(local_modes, 16)
    depth = round_up(2 * local_modes, 8)
    pairs = len(lat_pairs(lat_count))
    pair_rows = round_up(pairs * padded_modes, 128)
    share = degrees // 2
    big = 32 if pair_rows <= 4096 else 60
    shape = jax.ShapeDtypeStruct
    table = fourier_table(lon_count, blocks, local_modes, depth)
    table_in = jnp.asarray(table)
    table_out = jnp.asarray(np.ascontiguousarray(table.transpose(0, 2, 1)))
    x, dy = fields[0], cotangent[0]
    field = shape((slots, lon_count, chans), F32)
    coded = shape((depth, 2 * slots * chans), BF16)
    rim = shape((2, lon_count, chans), BF16)

    coded_parts = call(
        functools.partial(forward_kernel, blocks),
        [coded] * blocks,
        [HBM] * 3,
        (x, dy, table_in),
        scratch=[
            pltpu.VMEM(x.shape, BF16),
            pltpu.VMEM(dy.shape, BF16),
            pltpu.VMEM(table.shape, BF16),
            pltpu.VMEM(x.shape, BF16),
            pltpu.SemaphoreType.DMA((3,)),
        ],
        limit=60,
        flops=2 * blocks * depth * lon_count * 2 * slots * chans,
    )
    far = list(range(blocks - 1, 0, -1))
    got = [coded_parts[0], *reversed(crossed_all(coded_parts, far).values())]
    leg_rows = jnp.pad(
        jnp.transpose(legendre, (1, 0, 2)), ((0, 0), (0, padded_modes - local_modes), (0, 0))
    )
    padded = (lon_count + 2 * REACH, chans)
    tap_shape = shape((TAP_ROWS, chans), F32)
    mixer, back, first_rim, second_rim, base, slope, base_grad, tap_part = call(
        functools.partial(prepare_kernel, local_modes, blocks),
        [shape((pair_rows, 2 * chans), F32), shape((degrees, pair_rows), BF16), rim, rim]
        + [field, field, field, tap_shape],
        [SMEM, SMEM] + [VMEM] * 5,
        (band_rows, tap_shift, leg_rows, spectral_filter, x, dy, tap_weight),
        scratch=[pltpu.VMEM((pair_rows, degrees), BF16), pltpu.VMEM(x.shape, BF16)]
        + [pltpu.VMEM((slots + 1, *padded), F32)] * 2,
        limit=big,
        flops=2 * pair_rows * degrees * 2 * chans,
        moved=8 * pair_rows * chans,
    )
    first_rim, second_rim, got[-1] = lax.optimization_barrier((first_rim, second_rim, got[-1]))
    first_rim = crossed(first_rim, 1)
    inner = [(i, i ^ 1) for i in range(blocks)]
    inner = [(i + 1, j + 1) for i, j in inner if max(i, j) + 1 < blocks]
    second_rim = lax.ppermute(second_rim, "space", inner)
    spectral = shape((lat_count, 2, padded_modes, chans), F32)
    keep, *sends, coeff, grad = call(
        functools.partial(gradient_kernel, blocks, slots, lat_count, local_modes),
        [shape((share, chans), F32)] + [shape((share, chans), BF16)] * 3 + [spectral] * 2,
        [SMEM, SMEM] + [VMEM] * (1 + blocks),
        (band_rows, quad_weight, back, *got),
        scratch=[
            pltpu.VMEM((pair_rows, 2 * chans), F32),
            pltpu.VMEM((degrees, 2 * chans), F32),
            pltpu.VMEM((blocks, *coded.shape), F32),
        ],
        limit=big,
        flops=20 * degrees * pair_rows * 2 * chans,
    )
    got_sums = around(sends)
    back_parts = call(
        functools.partial(return_kernel, blocks, local_modes),
        [coded] * blocks,
        [SMEM, SMEM] + [VMEM] * 3,
        (band_rows, quad_weight, mixer, coeff, grad),
        scratch=[pltpu.VMEM(spectral.shape, F32)] * 2 + [pltpu.VMEM(coded.shape, F32)],
        limit=big,
    )
    rim_sum, rim_grad, tap_part = call(
        functools.partial(rim_kernel, blocks),
        [shape((2, lon_count, chans), F32)] * 2 + [tap_shape],
        [SMEM, SMEM] + [VMEM] * 5,
        (band_rows, tap_shift, dy, first_rim, second_rim, tap_weight, tap_part),
        scratch=[pltpu.VMEM((2, *padded), F32)] * 2,
    )
    message = shape((share + 2 * TAP_ROWS, chans), BF16)
    back_parts, tap_part = lax.optimization_barrier((back_parts, tap_part))
    own = call(quarter_kernel, message, [VMEM] * 5, (keep, *[got_sums[at] for at in (2, 0, 1)], tap_part))
    back_parts, own = lax.optimization_barrier((back_parts, own))
    returned = [back_parts[0], *reversed(crossed_all(back_parts, far).values())]
    steps = [(1 << bit, "space") for bit in range(1, blocks.bit_length() - 1)]
    steps += [(1 << bit, "ens") for bit in range(1, members.bit_length() - 1)]
    for at, (distance, axis) in enumerate(steps):
        scales = (members, members * lat_count) if at == len(steps) - 1 else (1, 1)
        own = call(
            functools.partial(add_kernel, *scales),
            message,
            [VMEM] * 2,
            (own, crossed(own, distance, axis)),
            flops=3900000000 if at == 0 else 0,
        )
    quarters = [own, *around([own] * 3)]
    early_sum, early_grad = call(
        early_kernel,
        [field, field],
        [SMEM] + [VMEM] * 8,
        (band_rows, table_out, base, slope, base_grad, rim_sum, rim_grad, *returned[:2]),
    )
    pieces = 4
    output, input_grad, filter_grad, tap_grad = call(
        functools.partial(finish_kernel, blocks),
        [shape(x.shape, BF16)] * 2
        + [shape((2, degrees, chans), F32), shape((tap_weight.shape[0], chans), F32)],
        [SMEM] + [VMEM] * (6 + blocks),
        (
            band_rows, table_out, early_sum, early_grad, slope,
            *quarters, *returned[2:],
        ),
        scratch=[
            pltpu.VMEM(x.shape, BF16),
            pltpu.VMEM(x.shape, BF16),
            pltpu.VMEM((2, degrees, chans), F32),
            pltpu.VMEM((4, TAP_ROWS, chans), F32),
            pltpu.SemaphoreType.DMA((1 + 2 * slots * pieces,)),
        ],
        flops=2 * blocks * depth * lon_count * 2 * slots * chans,
        out_specs=[HBM, HBM, HBM, VMEM],
    )
    return (output[None], input_grad[None], filter_grad, tap_grad)


def solution(mesh):
    in_specs = (
        P(("groups", "ens"), "space", None, "chan"),
        P(("groups", "ens"), "space", None, "chan"),
        P("groups"),
        P(),
        P(),
        P("space", None, None),
        P(None, None, "chan"),
        P(None, "chan"),
    )
    out_specs = (
        P(("groups", "ens"), "space", None, "chan"),
        P(("groups", "ens"), "space", None, "chan"),
        P("groups", None, "chan"),
        P("groups", "chan"),
    )
    return jax.shard_map(body, mesh=mesh, in_specs=in_specs, out_specs=out_specs, check_vma=False)
```

```python
import functools
import math

import jax
import jax.numpy as jnp
import ml_dtypes
import numpy as np
from jax import lax
from jax.experimental import pallas as pl
from jax.experimental.pallas import tpu as pltpu
from jax.sharding import PartitionSpec as P

F32 = jnp.float32
BF16 = jnp.bfloat16
VMEM = pl.BlockSpec(memory_space=pltpu.VMEM)
SMEM = pl.BlockSpec(memory_space=pltpu.SMEM)
HBM = pl.BlockSpec(memory_space=pltpu.HBM)
REACH = 8
TAP_ROWS = 16


def gelu_value(values):
    return 0.5 * values * (1.0 + lax.erf(values * 0.7071067811865476))


def gelu_slope(values):
    return (
        0.5 * (1.0 + lax.erf(values * 0.7071067811865476))
        + values * jnp.exp(-0.5 * values * values) * 0.3989422804014327
    )


def round_up(count, step):
    return -(-count // step) * step


def fourier_table(lon_count, blocks, local_modes, depth):
    lon_ids = np.arange(lon_count)
    mode_ids = np.arange(blocks * local_modes)
    phase = (mode_ids[:, None] * lon_ids[None, :] % lon_count) * (2.0 * math.pi / lon_count)
    factor = 1.0 / math.sqrt(lon_count)
    both = np.stack([np.cos(phase), -np.sin(phase)]) * factor
    both = both.reshape(2, blocks, local_modes, lon_count).transpose(1, 0, 2, 3)
    both = both.reshape(blocks, 2 * local_modes, lon_count)
    both = np.pad(both, ((0, 0), (0, depth - 2 * local_modes), (0, 0)))
    return both.astype(ml_dtypes.bfloat16)


def lat_pairs(lat_count):
    return [(a, b) for a in range(lat_count) for b in range(a, lat_count)]


def first_row_of(rows_ref, block, blocks):
    total = jnp.int32(0)
    for other in range(blocks):
        total = total + jnp.where(other < block, rows_ref[other], 0)
    return total


def call(kernel, out_shape, in_specs, args, scratch=(), limit=32, flops=0, moved=1024, out_specs=None):
    return pl.pallas_call(
        kernel,
        out_shape=out_shape,
        in_specs=in_specs,
        out_specs=out_specs or jax.tree.map(lambda _: VMEM, out_shape),
        scratch_shapes=list(scratch),
        compiler_params=pltpu.CompilerParams(vmem_limit_bytes=limit * 1024 * 1024),
        cost_estimate=pl.CostEstimate(flops=flops, bytes_accessed=moved, transcendentals=0),
    )(*args)


def activate(x_ref, act_ref):
    slots, lon_count, _ = x_ref.shape
    step = 64 if lon_count % 64 == 0 else lon_count

    def run(i, carry):
        part = pl.ds(pl.multiple_of(i * step, step), step)
        for slot in range(slots):
            act_ref[slot, part, :] = gelu_value(x_ref[slot, part, :].astype(F32)).astype(BF16)
        return carry

    lax.fori_loop(0, lon_count // step, run, 0)


def forward_kernel(blocks, x_hbm, dy_hbm, table_hbm, *refs):
    outs, (x_ref, dy_ref, table_ref, act_ref, sems) = refs[:blocks], refs[blocks:]
    slots = x_ref.shape[0]
    me = lax.axis_index("space")
    loads = [
        pltpu.make_async_copy(source, target, sems.at[i])
        for i, (source, target) in enumerate(
            [(x_hbm, x_ref), (dy_hbm, dy_ref), (table_hbm, table_ref)]
        )
    ]
    for load in loads:
        load.start()
    loads[0].wait()
    activate(x_ref, act_ref)
    loads[1].wait()
    source = jnp.concatenate(
        [dy_ref[slot] for slot in range(slots)] + [act_ref[slot] for slot in range(slots)], axis=-1
    )
    loads[2].wait()
    for shift in range(blocks):
        block = jnp.bitwise_xor(me, shift)
        sums = jnp.dot(table_ref[block], source, preferred_element_type=F32)
        outs[shift][...] = sums.astype(BF16)


def wrapped(target, row, value):
    lon_count = value.shape[0]
    target[row, REACH : REACH + lon_count, :] = value
    target[row, :REACH, :] = value[lon_count - REACH :, :]
    target[row, REACH + lon_count :, :] = value[:REACH, :]


def folded(values):
    return jnp.sum(values.reshape(values.shape[0] // 8, 8, values.shape[1]), axis=0)


def prepare_kernel(
    local_modes, blocks, rows_ref, shift_ref, leg_ref, filter_ref, x_ref, dy_ref, taps_ref,
    mixer_ref, back_ref, first_rim, second_rim, base_ref, slope_ref, base_grad_ref, tap_ref,
    pairs_ref, act_ref, acts, grads,
):
    me = lax.axis_index("space")
    activate(x_ref, act_ref)
    last = rows_ref[me] - 1
    odd = jnp.bitwise_and(me, 1)
    for rim_ref, row in ((first_rim, last * (1 - odd)), (second_rim, last * odd)):
        rim_ref[0] = act_ref[row]
        rim_ref[1] = dy_ref[row]
    pair_products(local_modes, leg_ref, filter_ref, mixer_ref, back_ref, pairs_ref)
    disco_inner(
        blocks, rows_ref, shift_ref, x_ref, dy_ref, act_ref, taps_ref,
        base_ref, slope_ref, base_grad_ref, tap_ref, acts, grads,
    )


def pair_products(local_modes, leg_ref, filter_ref, mixer_ref, back_ref, pairs_ref):
    me = lax.axis_index("space")
    lat_count, padded_modes, _ = leg_ref.shape
    pairs = lat_pairs(lat_count)
    used = len(pairs) * padded_modes
    mode = me * local_modes + lax.broadcasted_iota(
        jnp.int32, (padded_modes, 1), 0
    )
    twice = jnp.where(mode == 0, 1.0, 2.0)
    for index, (a, b) in enumerate(pairs):
        at = index * padded_modes
        pairs_ref[at : at + padded_modes, :] = (
            leg_ref[a].astype(F32) * leg_ref[b].astype(F32) * twice
        ).astype(BF16)
    if pairs_ref.shape[0] > used:
        pairs_ref[used:, :] = jnp.zeros((pairs_ref.shape[0] - used, pairs_ref.shape[1]), BF16)
    both = jnp.concatenate([filter_ref[0], filter_ref[1]], axis=-1)
    mixer_ref[...] = jnp.dot(pairs_ref[...], both, preferred_element_type=F32)

    def turn(i, carry):
        part = pl.ds(pl.multiple_of(i * 128, 128), 128)
        back_ref[:, part] = pairs_ref[part, :].astype(F32).T.astype(BF16)
        return carry

    lax.fori_loop(0, pairs_ref.shape[0] // 128, turn, 0)


def own_quarter():
    space_bit = jnp.bitwise_and(lax.axis_index("space"), 1)
    return 2 * space_bit + jnp.bitwise_and(lax.axis_index("ens"), 1)


def gradient_kernel(blocks, slots, lat_count, local_modes, rows_ref, quad_ref, back_ref, *refs):
    ins, sums, coeff, grad = refs[:blocks], refs[blocks : blocks + 4], *refs[blocks + 4 : blocks + 6]
    products, gradient, wide = refs[blocks + 6 :]
    padded_modes, chans = coeff.shape[2:]
    me = lax.axis_index("space")
    pairs = lat_pairs(lat_count)
    padding = padded_modes - local_modes
    if padding > 0:
        zeros = jnp.zeros((padding, chans), F32)
        for lat in range(lat_count):
            for part in range(2):
                coeff[lat, part, local_modes:, :] = zeros
                grad[lat, part, local_modes:, :] = zeros

    for shift in range(blocks):
        block = jnp.bitwise_xor(me, shift)
        start = first_row_of(rows_ref, block, blocks)
        wide[shift] = ins[shift][...].astype(F32)
        for slot in range(slots):
            lat = jnp.minimum(start + slot, lat_count - 1)

            @pl.when(slot < rows_ref[block])
            def _():
                weight = quad_ref[lat]
                for part in range(2):
                    grad[lat, part, :local_modes, :] = wide[(shift, *place(slots, local_modes, chans, 0, slot, part))]
                    coeff[lat, part, :local_modes, :] = (
                        wide[(shift, *place(slots, local_modes, chans, 1, slot, part))] * weight
                    )

    def multiply(i, carry):
        rows = pl.ds(pl.multiple_of(i * 8, 8), 8)
        a0, a1, b0, b1 = loaded(coeff, grad, rows)
        for index, (a, b) in enumerate(pairs):
            at = pl.ds(pl.multiple_of(index * padded_modes + i * 8, 8), 8)
            h0 = h1 = jnp.zeros((8, chans), F32)
            for p, q in [(a, b)] if a == b else [(a, b), (b, a)]:
                h0 = h0 + b0[p] * a0[q] + b1[p] * a1[q]
                h1 = h1 + b1[p] * a0[q] - b0[p] * a1[q]
            products[at, :chans] = h0
            products[at, chans:] = h1
        return carry

    lax.fori_loop(0, padded_modes // 8, multiply, 0)
    used = len(pairs) * padded_modes
    if products.shape[0] > used:
        products[used:, :] = jnp.zeros((products.shape[0] - used, products.shape[1]), F32)
    gradient[...] = jnp.dot(
        back_ref[...], products[...].astype(BF16), preferred_element_type=F32
    )
    share = gradient.shape[0] // 4
    for shift, target in enumerate(sums):
        at = jnp.bitwise_xor(own_quarter(), shift) * share
        part = gradient[pl.ds(pl.multiple_of(at, share), share), :]
        both = jnp.concatenate([part[:, :chans], part[:, chans:]], axis=0)
        target[...] = both.astype(target.dtype)


def loaded(coeff, grad, rows):
    return [
        [ref[lat, part, rows, :] for lat in range(ref.shape[0])]
        for ref in (coeff, grad)
        for part in range(2)
    ]


def place(slots, local_modes, chans, field, slot, part):
    at = (field * slots + slot) * chans
    return slice(part * local_modes, (part + 1) * local_modes), slice(at, at + chans)


def return_kernel(blocks, local_modes, rows_ref, quad_ref, mixer_ref, coeff, grad, *refs):
    outs, (synth, grad_coeff, wide) = refs[:blocks], refs[blocks:]
    lat_count, _, padded_modes, chans = coeff.shape
    slots = wide.shape[1] // (2 * chans)
    me = lax.axis_index("space")
    pairs = lat_pairs(lat_count)

    def mix(i, carry):
        rows = pl.ds(pl.multiple_of(i * 8, 8), 8)
        a0, a1, b0, b1 = loaded(coeff, grad, rows)
        zero = jnp.zeros((8, chans), F32)
        y0, y1, z0, z1 = ([zero] * lat_count for _ in range(4))
        for index, (a, b) in enumerate(pairs):
            at = pl.ds(pl.multiple_of(index * padded_modes + i * 8, 8), 8)
            real = mixer_ref[at, :chans]
            imag = mixer_ref[at, chans:]
            for p, q in [(a, b)] if a == b else [(a, b), (b, a)]:
                y0[p] = y0[p] + real * a0[q] - imag * a1[q]
                y1[p] = y1[p] + imag * a0[q] + real * a1[q]
                z0[q] = z0[q] + real * b0[p] + imag * b1[p]
                z1[q] = z1[q] + real * b1[p] - imag * b0[p]
        for lat in range(lat_count):
            synth[lat, 0, rows, :] = y0[lat]
            synth[lat, 1, rows, :] = y1[lat]
            grad_coeff[lat, 0, rows, :] = z0[lat] * quad_ref[lat]
            grad_coeff[lat, 1, rows, :] = z1[lat] * quad_ref[lat]
        return carry

    lax.fori_loop(0, padded_modes // 8, mix, 0)
    if wide.shape[0] > 2 * local_modes:
        wide[2 * local_modes :, :] = jnp.zeros(
            (wide.shape[0] - 2 * local_modes, wide.shape[1]), F32
        )
    for shift in range(blocks):
        block = jnp.bitwise_xor(me, shift)
        start = first_row_of(rows_ref, block, blocks)
        for slot in range(slots):
            lat = jnp.minimum(start + slot, lat_count - 1)
            for part in range(2):
                at = place(slots, local_modes, chans, 0, slot, part)
                wide[at] = synth[lat, part, :local_modes, :]
                at = place(slots, local_modes, chans, 1, slot, part)
                wide[at] = grad_coeff[lat, part, :local_modes, :]
        outs[shift][...] = wide[...].astype(BF16)


def disco_inner(
    blocks, rows_ref, shift_ref, x_ref, dy_ref, act_ref, taps_ref,
    base_ref, slope_ref, base_grad_ref, tap_ref, acts, grads,
):
    slots, lon_count, chans = x_ref.shape
    taps = taps_ref.shape[0]
    me = lax.axis_index("space")
    live = rows_ref[me]
    start = first_row_of(rows_ref, me, blocks)
    for slot in range(slots):
        alive = jnp.where(slot < live, 1.0, 0.0)
        wrapped(acts, slot, act_ref[slot].astype(F32))
        wrapped(grads, slot, dy_ref[slot].astype(F32) * alive)
    acts[slots] = jnp.zeros(acts.shape[1:], F32)
    grads[slots] = jnp.zeros(grads.shape[1:], F32)
    weights = taps_ref[...].astype(F32)
    step = 32 if lon_count % 32 == 0 else lon_count
    totals = [jnp.zeros((8, chans), F32)] * taps
    top = shift_ref.shape[0] - 1
    for slot in range(slots):
        below = jnp.where(slot + 1 < live, slot + 1, slots)
        sources = [(1, slot)]
        if slot > 0:
            sources.append((0, slot - 1))
        if slot + 1 < slots:
            sources.append((2, below))
        lat = jnp.clip(start + slot, 0, top)
        ahead, behind = [], []
        for offset, row in sources:
            other = jnp.clip(lat + offset - 1, 0, top)
            for column in range(3):
                t = 3 * offset + column
                ahead.append((t, row, REACH + shift_ref[lat, t]))
                t = 3 * (2 - offset) + column
                behind.append((t, row, REACH - shift_ref[other, t]))

        def inner(i, totals):
            at = pl.multiple_of(i * step, step)
            part = pl.ds(at, step)
            x = x_ref[slot, part, :].astype(F32)
            dy = grads[slot, pl.ds(pl.multiple_of(REACH + at, 8), step), :]
            out = x
            back = jnp.zeros((step, chans), F32)
            fresh = list(totals)
            for t, row, first in ahead:
                moved = acts[row, pl.ds(at + first, step), :]
                out = out + moved * weights[t : t + 1, :]
                fresh[t] = fresh[t] + folded(moved * dy)
            for t, row, first in behind:
                back = back + grads[row, pl.ds(at + first, step), :] * weights[t : t + 1, :]
            slope = gelu_slope(x)
            base_ref[slot, part, :] = out
            slope_ref[slot, part, :] = slope
            base_grad_ref[slot, part, :] = dy + back * slope
            return tuple(fresh)

        totals = list(lax.fori_loop(0, lon_count // step, inner, tuple(totals)))
    lines = [jnp.sum(total, axis=0, keepdims=True) for total in totals]
    lines.append(jnp.zeros((tap_ref.shape[0] - taps, chans), F32))
    tap_ref[...] = jnp.concatenate(lines, axis=0)


def rim_kernel(
    blocks, rows_ref, shift_ref, dy_ref, first_rim, second_rim, taps_ref, inner_ref,
    rim_ref, rim_grad_ref, tap_ref, acts, grads,
):
    _, lon_count, chans = dy_ref.shape
    me = lax.axis_index("space")
    live = rows_ref[me]
    start = first_row_of(rows_ref, me, blocks)
    odd = jnp.bitwise_and(me, 1)
    for source, row in ((first_rim, 1 - odd), (second_rim, odd)):
        wrapped(acts, row, source[0].astype(F32))
        wrapped(grads, row, source[1].astype(F32))
    weights = taps_ref[...].astype(F32)
    step = 128 if lon_count % 128 == 0 else lon_count
    top = shift_ref.shape[0] - 1
    lines = [jnp.zeros((1, chans), F32)] * tap_ref.shape[0]
    for side in range(2):
        slot = 0 if side == 0 else live - 1
        lat = jnp.clip(start + slot, 0, top)
        other = jnp.clip(lat + 2 * side - 1, 0, top)
        ahead = [(t, REACH + shift_ref[lat, t]) for t in range(6 * side, 6 * side + 3)]
        behind = [(t, REACH - shift_ref[other, t]) for t in range(6 - 6 * side, 9 - 6 * side)]

        def rim(i, totals):
            at = pl.multiple_of(i * step, step)
            part = pl.ds(at, step)
            dy = dy_ref[slot, part, :].astype(F32)
            out = back = jnp.zeros((step, chans), F32)
            fresh = []
            for total, (t, first) in zip(totals, ahead):
                moved = acts[side, pl.ds(at + first, step), :]
                out = out + moved * weights[t : t + 1, :]
                fresh.append(total + folded(moved * dy))
            for t, first in behind:
                back = back + grads[side, pl.ds(at + first, step), :] * weights[t : t + 1, :]
            rim_ref[side, part, :] = out
            rim_grad_ref[side, part, :] = back
            return tuple(fresh)

        totals = lax.fori_loop(0, lon_count // step, rim, (jnp.zeros((8, chans), F32),) * 3)
        for (t, _), total in zip(ahead, totals):
            lines[t] = jnp.sum(total, axis=0, keepdims=True)
    tap_ref[...] = inner_ref[...] + jnp.concatenate(lines, axis=0)


def split_taps(taps, out_ref, count):
    high = taps.astype(BF16)
    out_ref[count : count + TAP_ROWS, :] = high
    out_ref[count + TAP_ROWS :, :] = (taps - high.astype(F32)).astype(BF16)


def joined_taps(rows):
    return rows[-2 * TAP_ROWS : -TAP_ROWS, :] + rows[-TAP_ROWS:, :]


def split_taps(taps, out_ref, count):
    high = taps.astype(BF16)
    out_ref[count : count + TAP_ROWS, :] = high
    out_ref[count + TAP_ROWS :, :] = (taps - high.astype(F32)).astype(BF16)


def joined_taps(ref):
    rows = ref[ref.shape[0] - 2 * TAP_ROWS :, :].astype(F32)
    return rows[:TAP_ROWS, :] + rows[TAP_ROWS:, :]


def added(first_ref, second_ref):
    return first_ref[...].astype(F32) + second_ref[...].astype(F32)


def quarter_kernel(kept_ref, first_ref, second_ref, third_ref, tap_ref, out_ref):
    total = kept_ref[...]
    for ref in (first_ref, second_ref, third_ref):
        total = total + ref[...].astype(F32)
    out_ref[: total.shape[0], :] = total.astype(BF16)
    split_taps(tap_ref[...], out_ref, total.shape[0])


def add_kernel(scale, tap_scale, own_ref, other_ref, out_ref):
    count = own_ref.shape[0] - 2 * TAP_ROWS
    out_ref[:count, :] = (added(own_ref, other_ref)[:count, :] / scale).astype(BF16)
    split_taps((joined_taps(own_ref) + joined_taps(other_ref)) / tap_scale, out_ref, count)


def early_kernel(
    rows_ref, table_ref, base_ref, slope_ref, base_grad_ref, rim_ref, rim_grad_ref,
    own_ref, near_ref, sum_ref, grad_ref,
):
    slots, lon_count, chans = base_ref.shape
    me = lax.axis_index("space")
    live = rows_ref[me]
    step = lon_count // 4
    for at in range(0, lon_count, step):
        rows = slice(at, at + step)
        sums = jnp.dot(table_ref[me, rows, :], own_ref[...], preferred_element_type=F32)
        sums = sums + jnp.dot(
            table_ref[jnp.bitwise_xor(me, 1), rows, :], near_ref[...], preferred_element_type=F32
        )
        for slot in range(slots):
            out = base_ref[slot, rows, :] + sums[:, slot * chans : (slot + 1) * chans]
            back = sums[:, (slots + slot) * chans : (slots + slot + 1) * chans]
            if slot == 0:
                out = out + rim_ref[0, rows, :]
                back = back + rim_grad_ref[0, rows, :]
            last = slot == live - 1
            out = out + jnp.where(last, rim_ref[1, rows, :], 0.0)
            back = back + jnp.where(last, rim_grad_ref[1, rows, :], 0.0)
            sum_ref[slot, rows, :] = out
            grad_ref[slot, rows, :] = base_grad_ref[slot, rows, :] + back * slope_ref[slot, rows, :]


def spread_kernel(*refs):
    quarters, (filter_ref, tap_ref, held) = refs[:4], refs[4:]
    share = filter_ref.shape[1] // 4
    for shift, ref in enumerate(quarters):
        quarter = jnp.bitwise_xor(own_quarter(), shift)
        at = pl.ds(pl.multiple_of(quarter * share, share), share)
        rows = ref[: 2 * share, :].astype(F32)
        filter_ref[0, at, :] = rows[:share, :]
        filter_ref[1, at, :] = rows[share:, :]
        held[quarter] = joined_taps(ref)
    taps = (held[0] + held[1]) + (held[2] + held[3])
    tap_ref[...] = taps[: tap_ref.shape[0], :]


def finish_kernel(
    blocks, rows_ref, table_ref, sum_ref, early_ref, slope_ref, *refs
):
    ins, refs = refs[: blocks - 2], refs[blocks - 2 :]
    out_hbm, grad_hbm, out_ref, grad_ref, sems = refs
    slots, lon_count, chans = sum_ref.shape
    me = lax.axis_index("space")
    live = rows_ref[me]
    stores = []
    parts = sems.shape[0] // (2 * slots)
    step = lon_count // parts
    for part in range(parts):
        rows = slice(part * step, (part + 1) * step)
        sums = jnp.zeros((step, 2 * slots * chans), F32)
        for at, ref in enumerate(ins):
            block = jnp.bitwise_xor(me, at + 2)
            sums = sums + jnp.dot(table_ref[block, rows, :], ref[...], preferred_element_type=F32)
        for slot in range(slots):
            out = sum_ref[slot, rows, :] + sums[:, slot * chans : (slot + 1) * chans]
            back = sums[:, (slots + slot) * chans : (slots + slot + 1) * chans]
            grad = early_ref[slot, rows, :] + back * slope_ref[slot, rows, :]
            alive = slot < live
            out_ref[slot, rows, :] = jnp.where(alive, out, 0.0).astype(BF16)
            grad_ref[slot, rows, :] = jnp.where(alive, grad, 0.0).astype(BF16)
            for made, target in ((out_ref, out_hbm), (grad_ref, grad_hbm)):
                place = (slot, pl.ds(part * step, step))
                stores.append(
                    pltpu.make_async_copy(made.at[place], target.at[place], sems.at[len(stores)])
                )
                stores[-1].start()
    for store in stores:
        store.wait()


def crossed(values, distance, axis="space"):
    count = lax.axis_size(axis)
    return lax.ppermute(values, axis, [(i, i ^ distance) for i in range(count)])


def around(parts):
    count = lax.axis_size("space") * lax.axis_size("ens")
    flip = lax.axis_size("ens") + 1
    return [
        crossed(parts[0], 1, "ens"),
        crossed(parts[1], 1),
        lax.ppermute(parts[2], ("space", "ens"), [(i, i ^ flip) for i in range(count)]),
    ]


def crossed_all(parts, distances):
    return {s: crossed(parts[s], s) for s in distances}


def body(
    fields, cotangent, band_rows, tap_shift, quad_weight, legendre, spectral_filter, tap_weight
):
    blocks = lax.axis_size("space")
    members = lax.axis_size("ens")
    _, slots, lon_count, chans = fields.shape
    local_modes, lat_count, degrees = legendre.shape
    padded_modes = round_up(local_modes, 16)
    depth = round_up(2 * local_modes, 8)
    pairs = len(lat_pairs(lat_count))
    pair_rows = round_up(pairs * padded_modes, 128)
    share = degrees // 2
    big = 32 if pair_rows <= 4096 else 60
    shape = jax.ShapeDtypeStruct
    table = fourier_table(lon_count, blocks, local_modes, depth)
    table_in = jnp.asarray(table)
    table_out = jnp.asarray(np.ascontiguousarray(table.transpose(0, 2, 1)))
    x, dy = fields[0], cotangent[0]
    field = shape((slots, lon_count, chans), F32)
    coded = shape((depth, 2 * slots * chans), BF16)
    rim = shape((2, lon_count, chans), BF16)

    coded_parts = call(
        functools.partial(forward_kernel, blocks),
        [coded] * blocks,
        [HBM] * 3,
        (x, dy, table_in),
        scratch=[
            pltpu.VMEM(x.shape, BF16),
            pltpu.VMEM(dy.shape, BF16),
            pltpu.VMEM(table.shape, BF16),
            pltpu.VMEM(x.shape, BF16),
            pltpu.SemaphoreType.DMA((3,)),
        ],
        limit=60,
        flops=2 * blocks * depth * lon_count * 2 * slots * chans,
    )
    far = list(range(blocks - 1, 0, -1))
    got = [coded_parts[0], *reversed(crossed_all(coded_parts, far).values())]
    leg_rows = jnp.pad(
        jnp.transpose(legendre, (1, 0, 2)), ((0, 0), (0, padded_modes - local_modes), (0, 0))
    )
    padded = (lon_count + 2 * REACH, chans)
    tap_shape = shape((TAP_ROWS, chans), F32)
    mixer, back, first_rim, second_rim, base, slope, base_grad, tap_part = call(
        functools.partial(prepare_kernel, local_modes, blocks),
        [shape((pair_rows, 2 * chans), F32), shape((degrees, pair_rows), BF16), rim, rim]
        + [field, field, field, tap_shape],
        [SMEM, SMEM] + [VMEM] * 5,
        (band_rows, tap_shift, leg_rows, spectral_filter, x, dy, tap_weight),
        scratch=[pltpu.VMEM((pair_rows, degrees), BF16), pltpu.VMEM(x.shape, BF16)]
        + [pltpu.VMEM((slots + 1, *padded), F32)] * 2,
        limit=big,
        flops=2 * pair_rows * degrees * 2 * chans,
        moved=8 * pair_rows * chans,
    )
    first_rim, second_rim, got[-1] = lax.optimization_barrier((first_rim, second_rim, got[-1]))
    first_rim = crossed(first_rim, 1)
    inner = [(i, i ^ 1) for i in range(blocks)]
    inner = [(i + 1, j + 1) for i, j in inner if max(i, j) + 1 < blocks]
    second_rim = lax.ppermute(second_rim, "space", inner)
    spectral = shape((lat_count, 2, padded_modes, chans), F32)
    keep, *sends, coeff, grad = call(
        functools.partial(gradient_kernel, blocks, slots, lat_count, local_modes),
        [shape((share, chans), F32)] + [shape((share, chans), BF16)] * 3 + [spectral] * 2,
        [SMEM, SMEM] + [VMEM] * (1 + blocks),
        (band_rows, quad_weight, back, *got),
        scratch=[
            pltpu.VMEM((pair_rows, 2 * chans), F32),
            pltpu.VMEM((degrees, 2 * chans), F32),
            pltpu.VMEM((blocks, *coded.shape), F32),
        ],
        limit=big,
        flops=20 * degrees * pair_rows * 2 * chans,
    )
    got_sums = around(sends)
    back_parts = call(
        functools.partial(return_kernel, blocks, local_modes),
        [coded] * blocks,
        [SMEM, SMEM] + [VMEM] * 3,
        (band_rows, quad_weight, mixer, coeff, grad),
        scratch=[pltpu.VMEM(spectral.shape, F32)] * 2 + [pltpu.VMEM(coded.shape, F32)],
        limit=big,
    )
    rim_sum, rim_grad, tap_part = call(
        functools.partial(rim_kernel, blocks),
        [shape((2, lon_count, chans), F32)] * 2 + [tap_shape],
        [SMEM, SMEM] + [VMEM] * 5,
        (band_rows, tap_shift, dy, first_rim, second_rim, tap_weight, tap_part),
        scratch=[pltpu.VMEM((2, *padded), F32)] * 2,
    )
    message = shape((share + 2 * TAP_ROWS, chans), BF16)
    back_parts, tap_part = lax.optimization_barrier((back_parts, tap_part))
    own = call(quarter_kernel, message, [VMEM] * 5, (keep, *[got_sums[at] for at in (2, 0, 1)], tap_part))
    back_parts, own = lax.optimization_barrier((back_parts, own))
    returned = [back_parts[0], *reversed(crossed_all(back_parts, far).values())]
    steps = [(1 << bit, "space") for bit in range(1, blocks.bit_length() - 1)]
    steps += [(1 << bit, "ens") for bit in range(1, members.bit_length() - 1)]
    for at, (distance, axis) in enumerate(steps):
        scales = (members, members * lat_count) if at == len(steps) - 1 else (1, 1)
        own = call(
            functools.partial(add_kernel, *scales),
            message,
            [VMEM] * 2,
            (own, crossed(own, distance, axis)),
            flops=3900000000 if at == 0 else 0,
        )
    quarters = [own, *around([own] * 3)]
    early_sum, early_grad = call(
        early_kernel,
        [field, field],
        [SMEM] + [VMEM] * 8,
        (band_rows, table_out, base, slope, base_grad, rim_sum, rim_grad, *returned[:2]),
    )
    quarters, early_sum = lax.optimization_barrier((quarters, early_sum))
    filter_grad, tap_grad = call(
        spread_kernel,
        [shape((2, degrees, chans), F32), shape((tap_weight.shape[0], chans), F32)],
        [VMEM] * 4,
        quarters,
        scratch=[pltpu.VMEM((4, TAP_ROWS, chans), F32)],
    )
    far_parts, filter_grad = lax.optimization_barrier((returned[2:], filter_grad))
    pieces = 4
    output, input_grad = call(
        functools.partial(finish_kernel, blocks),
        [shape(x.shape, BF16)] * 2,
        [SMEM] + [VMEM] * (2 + blocks),
        (band_rows, table_out, early_sum, early_grad, slope, *far_parts),
        scratch=[
            pltpu.VMEM(x.shape, BF16),
            pltpu.VMEM(x.shape, BF16),
            pltpu.SemaphoreType.DMA((2 * slots * pieces,)),
        ],
        flops=2 * blocks * depth * lon_count * 2 * slots * chans,
        out_specs=[HBM, HBM],
    )
    return (output[None], input_grad[None], filter_grad, tap_grad)


def solution(mesh):
    in_specs = (
        P(("groups", "ens"), "space", None, "chan"),
        P(("groups", "ens"), "space", None, "chan"),
        P("groups"),
        P(),
        P(),
        P("space", None, None),
        P(None, None, "chan"),
        P(None, "chan"),
    )
    out_specs = (
        P(("groups", "ens"), "space", None, "chan"),
        P(("groups", "ens"), "space", None, "chan"),
        P("groups", None, "chan"),
        P("groups", "chan"),
    )
    return jax.shard_map(body, mesh=mesh, in_specs=in_specs, out_specs=out_specs, check_vma=False)
```

```python
import functools
import math

import jax
import jax.numpy as jnp
import ml_dtypes
import numpy as np
from jax import lax
from jax.experimental import pallas as pl
from jax.experimental.pallas import tpu as pltpu
from jax.sharding import PartitionSpec as P

F32 = jnp.float32
BF16 = jnp.bfloat16
VMEM = pl.BlockSpec(memory_space=pltpu.VMEM)
SMEM = pl.BlockSpec(memory_space=pltpu.SMEM)
HBM = pl.BlockSpec(memory_space=pltpu.HBM)
REACH = 8
TAP_ROWS = 16


def gelu_value(values):
    return 0.5 * values * (1.0 + lax.erf(values * 0.7071067811865476))


def gelu_slope(values):
    return (
        0.5 * (1.0 + lax.erf(values * 0.7071067811865476))
        + values * jnp.exp(-0.5 * values * values) * 0.3989422804014327
    )


def round_up(count, step):
    return -(-count // step) * step


def fourier_table(lon_count, blocks, local_modes, depth):
    lon_ids = np.arange(lon_count)
    mode_ids = np.arange(blocks * local_modes)
    phase = (mode_ids[:, None] * lon_ids[None, :] % lon_count) * (2.0 * math.pi / lon_count)
    factor = 1.0 / math.sqrt(lon_count)
    both = np.stack([np.cos(phase), -np.sin(phase)]) * factor
    both = both.reshape(2, blocks, local_modes, lon_count).transpose(1, 0, 2, 3)
    both = both.reshape(blocks, 2 * local_modes, lon_count)
    both = np.pad(both, ((0, 0), (0, depth - 2 * local_modes), (0, 0)))
    return both.astype(ml_dtypes.bfloat16)


def lat_pairs(lat_count):
    return [(a, b) for a in range(lat_count) for b in range(a, lat_count)]


def first_row_of(rows_ref, block, blocks):
    total = jnp.int32(0)
    for other in range(blocks):
        total = total + jnp.where(other < block, rows_ref[other], 0)
    return total


def call(kernel, out_shape, in_specs, args, scratch=(), limit=32, flops=0, moved=1024, out_specs=None):
    return pl.pallas_call(
        kernel,
        out_shape=out_shape,
        in_specs=in_specs,
        out_specs=out_specs or jax.tree.map(lambda _: VMEM, out_shape),
        scratch_shapes=list(scratch),
        compiler_params=pltpu.CompilerParams(vmem_limit_bytes=limit * 1024 * 1024),
        cost_estimate=pl.CostEstimate(flops=flops, bytes_accessed=moved, transcendentals=0),
    )(*args)


def activate(x_ref, act_ref):
    slots, lon_count, _ = x_ref.shape
    step = 64 if lon_count % 64 == 0 else lon_count

    def run(i, carry):
        part = pl.ds(pl.multiple_of(i * step, step), step)
        for slot in range(slots):
            act_ref[slot, part, :] = gelu_value(x_ref[slot, part, :].astype(F32)).astype(BF16)
        return carry

    lax.fori_loop(0, lon_count // step, run, 0)


def forward_kernel(blocks, x_hbm, dy_hbm, table_hbm, *refs):
    outs, (x_ref, dy_ref, table_ref, act_ref, sems) = refs[:blocks], refs[blocks:]
    slots = x_ref.shape[0]
    me = lax.axis_index("space")
    loads = [
        pltpu.make_async_copy(source, target, sems.at[i])
        for i, (source, target) in enumerate(
            [(x_hbm, x_ref), (dy_hbm, dy_ref), (table_hbm, table_ref)]
        )
    ]
    for load in loads:
        load.start()
    loads[0].wait()
    activate(x_ref, act_ref)
    loads[1].wait()
    source = jnp.concatenate(
        [dy_ref[slot] for slot in range(slots)] + [act_ref[slot] for slot in range(slots)], axis=-1
    )
    loads[2].wait()
    for shift in range(blocks):
        block = jnp.bitwise_xor(me, shift)
        sums = jnp.dot(table_ref[block], source, preferred_element_type=F32)
        outs[shift][...] = sums.astype(BF16)


def wrapped(target, row, value):
    lon_count = value.shape[0]
    target[row, REACH : REACH + lon_count, :] = value
    target[row, :REACH, :] = value[lon_count - REACH :, :]
    target[row, REACH + lon_count :, :] = value[:REACH, :]


def folded(values):
    return jnp.sum(values.reshape(values.shape[0] // 8, 8, values.shape[1]), axis=0)


def prepare_kernel(
    local_modes, blocks, rows_ref, shift_ref, leg_ref, filter_ref, x_ref, dy_ref, taps_ref,
    mixer_ref, back_ref, first_rim, second_rim, base_ref, slope_ref, base_grad_ref, tap_ref,
    pairs_ref, act_ref, acts, grads,
):
    me = lax.axis_index("space")
    activate(x_ref, act_ref)
    last = rows_ref[me] - 1
    odd = jnp.bitwise_and(me, 1)
    for rim_ref, row in ((first_rim, last * (1 - odd)), (second_rim, last * odd)):
        rim_ref[0] = act_ref[row]
        rim_ref[1] = dy_ref[row]
    pair_products(local_modes, leg_ref, filter_ref, mixer_ref, back_ref, pairs_ref)
    disco_inner(
        blocks, rows_ref, shift_ref, x_ref, dy_ref, act_ref, taps_ref,
        base_ref, slope_ref, base_grad_ref, tap_ref, acts, grads,
    )


def pair_products(local_modes, leg_ref, filter_ref, mixer_ref, back_ref, pairs_ref):
    me = lax.axis_index("space")
    lat_count, padded_modes, _ = leg_ref.shape
    pairs = lat_pairs(lat_count)
    used = len(pairs) * padded_modes
    mode = me * local_modes + lax.broadcasted_iota(
        jnp.int32, (padded_modes, 1), 0
    )
    twice = jnp.where(mode == 0, 1.0, 2.0)
    for index, (a, b) in enumerate(pairs):
        at = index * padded_modes
        pairs_ref[at : at + padded_modes, :] = (
            leg_ref[a].astype(F32) * leg_ref[b].astype(F32) * twice
        ).astype(BF16)
    if pairs_ref.shape[0] > used:
        pairs_ref[used:, :] = jnp.zeros((pairs_ref.shape[0] - used, pairs_ref.shape[1]), BF16)
    both = jnp.concatenate([filter_ref[0], filter_ref[1]], axis=-1)
    mixer_ref[...] = jnp.dot(pairs_ref[...], both, preferred_element_type=F32)

    def turn(i, carry):
        part = pl.ds(pl.multiple_of(i * 128, 128), 128)
        back_ref[:, part] = pairs_ref[part, :].astype(F32).T.astype(BF16)
        return carry

    lax.fori_loop(0, pairs_ref.shape[0] // 128, turn, 0)


def own_quarter():
    space_bit = jnp.bitwise_and(lax.axis_index("space"), 1)
    return 2 * space_bit + jnp.bitwise_and(lax.axis_index("ens"), 1)


def gradient_kernel(blocks, slots, lat_count, local_modes, rows_ref, quad_ref, back_ref, *refs):
    ins, sums, coeff, grad = refs[:blocks], refs[blocks : blocks + 4], *refs[blocks + 4 : blocks + 6]
    products, gradient, wide = refs[blocks + 6 :]
    padded_modes, chans = coeff.shape[2:]
    me = lax.axis_index("space")
    pairs = lat_pairs(lat_count)
    whole = local_modes // 8 * 8
    if padded_modes > whole:
        zeros = jnp.zeros((padded_modes - whole, chans), F32)
        for lat in range(lat_count):
            for part in range(2):
                coeff[lat, part, whole:, :] = zeros
                grad[lat, part, whole:, :] = zeros

    for shift in range(blocks):
        block = jnp.bitwise_xor(me, shift)
        start = first_row_of(rows_ref, block, blocks)
        wide[shift, : ins[shift].shape[0], :] = ins[shift][...].astype(F32)
        for slot in range(slots):
            lat = jnp.minimum(start + slot, lat_count - 1)

            @pl.when(slot < rows_ref[block])
            def _():
                weight = quad_ref[lat]
                for part in range(2):
                    at = place(slots, local_modes, chans, 0, slot, part)
                    grad[lat, part, :local_modes, :] = wide[(shift, *at)]
                    at = place(slots, local_modes, chans, 1, slot, part)
                    coeff[lat, part, :local_modes, :] = wide[(shift, *at)] * weight

    def multiply(i, carry):
        rows = pl.ds(pl.multiple_of(i * 8, 8), 8)
        a0, a1, b0, b1 = loaded(coeff, grad, rows)
        for index, (a, b) in enumerate(pairs):
            at = pl.ds(pl.multiple_of(index * padded_modes + i * 8, 8), 8)
            h0 = h1 = jnp.zeros((8, chans), F32)
            for p, q in [(a, b)] if a == b else [(a, b), (b, a)]:
                h0 = h0 + b0[p] * a0[q] + b1[p] * a1[q]
                h1 = h1 + b1[p] * a0[q] - b0[p] * a1[q]
            products[at, :chans] = h0
            products[at, chans:] = h1
        return carry

    lax.fori_loop(0, padded_modes // 8, multiply, 0)
    used = len(pairs) * padded_modes
    if products.shape[0] > used:
        products[used:, :] = jnp.zeros((products.shape[0] - used, products.shape[1]), F32)
    gradient[...] = jnp.dot(
        back_ref[...], products[...].astype(BF16), preferred_element_type=F32
    )
    share = gradient.shape[0] // 4
    for shift, target in enumerate(sums):
        at = jnp.bitwise_xor(own_quarter(), shift) * share
        part = gradient[pl.ds(pl.multiple_of(at, share), share), :]
        both = jnp.concatenate([part[:, :chans], part[:, chans:]], axis=0)
        target[...] = both.astype(target.dtype)


def loaded(coeff, grad, rows):
    return [
        [ref[lat, part, rows, :] for lat in range(ref.shape[0])]
        for ref in (coeff, grad)
        for part in range(2)
    ]


def place(slots, local_modes, chans, field, slot, part):
    at = (field * slots + slot) * chans
    return slice(part * local_modes, (part + 1) * local_modes), slice(at, at + chans)


def return_kernel(blocks, local_modes, rows_ref, quad_ref, mixer_ref, coeff, grad, *refs):
    outs, (synth, grad_coeff, wide) = refs[:blocks], refs[blocks:]
    lat_count, _, padded_modes, chans = coeff.shape
    slots = wide.shape[1] // (2 * chans)
    me = lax.axis_index("space")
    pairs = lat_pairs(lat_count)

    def mix(i, carry):
        rows = pl.ds(pl.multiple_of(i * 8, 8), 8)
        a0, a1, b0, b1 = loaded(coeff, grad, rows)
        zero = jnp.zeros((8, chans), F32)
        y0, y1, z0, z1 = ([zero] * lat_count for _ in range(4))
        for index, (a, b) in enumerate(pairs):
            at = pl.ds(pl.multiple_of(index * padded_modes + i * 8, 8), 8)
            real = mixer_ref[at, :chans]
            imag = mixer_ref[at, chans:]
            for p, q in [(a, b)] if a == b else [(a, b), (b, a)]:
                y0[p] = y0[p] + real * a0[q] - imag * a1[q]
                y1[p] = y1[p] + imag * a0[q] + real * a1[q]
                z0[q] = z0[q] + real * b0[p] + imag * b1[p]
                z1[q] = z1[q] + real * b1[p] - imag * b0[p]
        for lat in range(lat_count):
            synth[lat, 0, rows, :] = y0[lat]
            synth[lat, 1, rows, :] = y1[lat]
            grad_coeff[lat, 0, rows, :] = z0[lat] * quad_ref[lat]
            grad_coeff[lat, 1, rows, :] = z1[lat] * quad_ref[lat]
        return carry

    lax.fori_loop(0, padded_modes // 8, mix, 0)
    whole = 2 * local_modes // 8 * 8
    wide[whole:, :] = jnp.zeros((wide.shape[0] - whole, wide.shape[1]), F32)
    for shift in range(blocks):
        block = jnp.bitwise_xor(me, shift)
        start = first_row_of(rows_ref, block, blocks)
        for slot in range(slots):
            lat = jnp.minimum(start + slot, lat_count - 1)
            for part in range(2):
                at = place(slots, local_modes, chans, 0, slot, part)
                wide[at] = synth[lat, part, :local_modes, :]
                at = place(slots, local_modes, chans, 1, slot, part)
                wide[at] = grad_coeff[lat, part, :local_modes, :]
        outs[shift][...] = wide[: outs[shift].shape[0], :].astype(BF16)


def disco_inner(
    blocks, rows_ref, shift_ref, x_ref, dy_ref, act_ref, taps_ref,
    base_ref, slope_ref, base_grad_ref, tap_ref, acts, grads,
):
    slots, lon_count, chans = x_ref.shape
    taps = taps_ref.shape[0]
    me = lax.axis_index("space")
    live = rows_ref[me]
    start = first_row_of(rows_ref, me, blocks)
    for slot in range(slots):
        alive = jnp.where(slot < live, 1.0, 0.0)
        wrapped(acts, slot, act_ref[slot].astype(F32))
        wrapped(grads, slot, dy_ref[slot].astype(F32) * alive)
    acts[slots] = jnp.zeros(acts.shape[1:], F32)
    grads[slots] = jnp.zeros(grads.shape[1:], F32)
    weights = taps_ref[...].astype(F32)
    step = 32 if lon_count % 32 == 0 else lon_count
    totals = [jnp.zeros((8, chans), F32)] * taps
    top = shift_ref.shape[0] - 1
    for slot in range(slots):
        below = jnp.where(slot + 1 < live, slot + 1, slots)
        sources = [(1, slot)]
        if slot > 0:
            sources.append((0, slot - 1))
        if slot + 1 < slots:
            sources.append((2, below))
        lat = jnp.clip(start + slot, 0, top)
        ahead, behind = [], []
        for offset, row in sources:
            other = jnp.clip(lat + offset - 1, 0, top)
            for column in range(3):
                t = 3 * offset + column
                ahead.append((t, row, REACH + shift_ref[lat, t]))
                t = 3 * (2 - offset) + column
                behind.append((t, row, REACH - shift_ref[other, t]))

        def inner(i, totals):
            at = pl.multiple_of(i * step, step)
            part = pl.ds(at, step)
            x = x_ref[slot, part, :].astype(F32)
            dy = grads[slot, pl.ds(pl.multiple_of(REACH + at, 8), step), :]
            out = x
            back = jnp.zeros((step, chans), F32)
            fresh = list(totals)
            for t, row, first in ahead:
                moved = acts[row, pl.ds(at + first, step), :]
                out = out + moved * weights[t : t + 1, :]
                fresh[t] = fresh[t] + folded(moved * dy)
            for t, row, first in behind:
                back = back + grads[row, pl.ds(at + first, step), :] * weights[t : t + 1, :]
            slope = gelu_slope(x)
            base_ref[slot, part, :] = out
            slope_ref[slot, part, :] = slope
            base_grad_ref[slot, part, :] = dy + back * slope
            return tuple(fresh)

        totals = list(lax.fori_loop(0, lon_count // step, inner, tuple(totals)))
    lines = [jnp.sum(total, axis=0, keepdims=True) for total in totals]
    lines.append(jnp.zeros((tap_ref.shape[0] - taps, chans), F32))
    tap_ref[...] = jnp.concatenate(lines, axis=0)


def rim_kernel(
    blocks, rows_ref, shift_ref, dy_ref, first_rim, second_rim, taps_ref, inner_ref,
    rim_ref, rim_grad_ref, tap_ref, acts, grads,
):
    _, lon_count, chans = dy_ref.shape
    me = lax.axis_index("space")
    live = rows_ref[me]
    start = first_row_of(rows_ref, me, blocks)
    odd = jnp.bitwise_and(me, 1)
    for source, row in ((first_rim, 1 - odd), (second_rim, odd)):
        wrapped(acts, row, source[0].astype(F32))
        wrapped(grads, row, source[1].astype(F32))
    weights = taps_ref[...].astype(F32)
    step = 128 if lon_count % 128 == 0 else lon_count
    top = shift_ref.shape[0] - 1
    lines = [jnp.zeros((1, chans), F32)] * tap_ref.shape[0]
    for side in range(2):
        slot = 0 if side == 0 else live - 1
        lat = jnp.clip(start + slot, 0, top)
        other = jnp.clip(lat + 2 * side - 1, 0, top)
        ahead = [(t, REACH + shift_ref[lat, t]) for t in range(6 * side, 6 * side + 3)]
        behind = [(t, REACH - shift_ref[other, t]) for t in range(6 - 6 * side, 9 - 6 * side)]

        def rim(i, totals):
            at = pl.multiple_of(i * step, step)
            part = pl.ds(at, step)
            dy = dy_ref[slot, part, :].astype(F32)
            out = back = jnp.zeros((step, chans), F32)
            fresh = []
            for total, (t, first) in zip(totals, ahead):
                moved = acts[side, pl.ds(at + first, step), :]
                out = out + moved * weights[t : t + 1, :]
                fresh.append(total + folded(moved * dy))
            for t, first in behind:
                back = back + grads[side, pl.ds(at + first, step), :] * weights[t : t + 1, :]
            rim_ref[side, part, :] = out
            rim_grad_ref[side, part, :] = back
            return tuple(fresh)

        totals = lax.fori_loop(0, lon_count // step, rim, (jnp.zeros((8, chans), F32),) * 3)
        for (t, _), total in zip(ahead, totals):
            lines[t] = jnp.sum(total, axis=0, keepdims=True)
    tap_ref[...] = inner_ref[...] + jnp.concatenate(lines, axis=0)


def split_taps(taps, out_ref, count):
    high = taps.astype(BF16)
    out_ref[count : count + TAP_ROWS, :] = high
    out_ref[count + TAP_ROWS :, :] = (taps - high.astype(F32)).astype(BF16)


def joined_taps(rows):
    return rows[-2 * TAP_ROWS : -TAP_ROWS, :] + rows[-TAP_ROWS:, :]


def split_taps(taps, out_ref, count):
    high = taps.astype(BF16)
    out_ref[count : count + TAP_ROWS, :] = high
    out_ref[count + TAP_ROWS :, :] = (taps - high.astype(F32)).astype(BF16)


def joined_taps(ref):
    rows = ref[ref.shape[0] - 2 * TAP_ROWS :, :].astype(F32)
    return rows[:TAP_ROWS, :] + rows[TAP_ROWS:, :]


def added(first_ref, second_ref):
    return first_ref[...].astype(F32) + second_ref[...].astype(F32)


def quarter_kernel(kept_ref, first_ref, second_ref, third_ref, tap_ref, out_ref):
    total = kept_ref[...]
    for ref in (first_ref, second_ref, third_ref):
        total = total + ref[...].astype(F32)
    out_ref[: total.shape[0], :] = total.astype(BF16)
    split_taps(tap_ref[...], out_ref, total.shape[0])


def add_kernel(scale, tap_scale, own_ref, other_ref, out_ref):
    count = own_ref.shape[0] - 2 * TAP_ROWS
    out_ref[:count, :] = (added(own_ref, other_ref)[:count, :] / scale).astype(BF16)
    split_taps((joined_taps(own_ref) + joined_taps(other_ref)) / tap_scale, out_ref, count)


def early_kernel(
    rows_ref, table_ref, base_ref, slope_ref, base_grad_ref, rim_ref, rim_grad_ref,
    own_ref, near_ref, sum_ref, grad_ref,
):
    slots, lon_count, chans = base_ref.shape
    me = lax.axis_index("space")
    live = rows_ref[me]
    step = lon_count // 4
    for at in range(0, lon_count, step):
        rows = slice(at, at + step)
        sums = jnp.dot(table_ref[me, rows, :], own_ref[...], preferred_element_type=F32)
        sums = sums + jnp.dot(
            table_ref[jnp.bitwise_xor(me, 1), rows, :], near_ref[...], preferred_element_type=F32
        )
        for slot in range(slots):
            out = base_ref[slot, rows, :] + sums[:, slot * chans : (slot + 1) * chans]
            back = sums[:, (slots + slot) * chans : (slots + slot + 1) * chans]
            if slot == 0:
                out = out + rim_ref[0, rows, :]
                back = back + rim_grad_ref[0, rows, :]
            last = slot == live - 1
            out = out + jnp.where(last, rim_ref[1, rows, :], 0.0)
            back = back + jnp.where(last, rim_grad_ref[1, rows, :], 0.0)
            sum_ref[slot, rows, :] = out
            grad_ref[slot, rows, :] = base_grad_ref[slot, rows, :] + back * slope_ref[slot, rows, :]


def spread_kernel(*refs):
    quarters, (filter_ref, tap_ref, held) = refs[:4], refs[4:]
    share = filter_ref.shape[1] // 4
    for shift, ref in enumerate(quarters):
        quarter = jnp.bitwise_xor(own_quarter(), shift)
        at = pl.ds(pl.multiple_of(quarter * share, share), share)
        rows = ref[: 2 * share, :].astype(F32)
        filter_ref[0, at, :] = rows[:share, :]
        filter_ref[1, at, :] = rows[share:, :]
        held[quarter] = joined_taps(ref)
    taps = (held[0] + held[1]) + (held[2] + held[3])
    tap_ref[...] = taps[: tap_ref.shape[0], :]


def finish_kernel(
    blocks, rows_ref, table_ref, sum_ref, early_ref, slope_ref, *refs
):
    ins, refs = refs[: blocks - 2], refs[blocks - 2 :]
    out_hbm, grad_hbm, out_ref, grad_ref, sems = refs
    slots, lon_count, chans = sum_ref.shape
    me = lax.axis_index("space")
    live = rows_ref[me]
    stores = []
    parts = sems.shape[0] // (2 * slots)
    step = lon_count // parts
    for part in range(parts):
        rows = slice(part * step, (part + 1) * step)
        sums = jnp.zeros((step, 2 * slots * chans), F32)
        for at, ref in enumerate(ins):
            block = jnp.bitwise_xor(me, at + 2)
            sums = sums + jnp.dot(table_ref[block, rows, :], ref[...], preferred_element_type=F32)
        for slot in range(slots):
            out = sum_ref[slot, rows, :] + sums[:, slot * chans : (slot + 1) * chans]
            back = sums[:, (slots + slot) * chans : (slots + slot + 1) * chans]
            grad = early_ref[slot, rows, :] + back * slope_ref[slot, rows, :]
            alive = slot < live
            out_ref[slot, rows, :] = jnp.where(alive, out, 0.0).astype(BF16)
            grad_ref[slot, rows, :] = jnp.where(alive, grad, 0.0).astype(BF16)
            for made, target in ((out_ref, out_hbm), (grad_ref, grad_hbm)):
                place = (slot, pl.ds(part * step, step))
                stores.append(
                    pltpu.make_async_copy(made.at[place], target.at[place], sems.at[len(stores)])
                )
                stores[-1].start()
    for store in stores:
        store.wait()


def crossed(values, distance, axis="space"):
    count = lax.axis_size(axis)
    return lax.ppermute(values, axis, [(i, i ^ distance) for i in range(count)])


def around(parts):
    count = lax.axis_size("space") * lax.axis_size("ens")
    flip = lax.axis_size("ens") + 1
    return [
        crossed(parts[0], 1, "ens"),
        crossed(parts[1], 1),
        lax.ppermute(parts[2], ("space", "ens"), [(i, i ^ flip) for i in range(count)]),
    ]


def crossed_all(parts, distances):
    return {s: crossed(parts[s], s) for s in distances}


def body(
    fields, cotangent, band_rows, tap_shift, quad_weight, legendre, spectral_filter, tap_weight
):
    blocks = lax.axis_size("space")
    members = lax.axis_size("ens")
    _, slots, lon_count, chans = fields.shape
    local_modes, lat_count, degrees = legendre.shape
    padded_modes = round_up(local_modes, 16)
    depth = round_up(2 * local_modes, 8)
    pairs = len(lat_pairs(lat_count))
    pair_rows = round_up(pairs * padded_modes, 128)
    share = degrees // 2
    big = 32 if pair_rows <= 4096 else 60
    shape = jax.ShapeDtypeStruct
    table = fourier_table(lon_count, blocks, local_modes, depth)
    table_in = jnp.asarray(table)
    table_out = jnp.asarray(np.ascontiguousarray(table.transpose(0, 2, 1)))
    x, dy = fields[0], cotangent[0]
    field = shape((slots, lon_count, chans), F32)
    coded = shape((depth, 2 * slots * chans), BF16)
    rim = shape((2, lon_count, chans), BF16)

    coded_parts = call(
        functools.partial(forward_kernel, blocks),
        [coded] * blocks,
        [HBM] * 3,
        (x, dy, table_in),
        scratch=[
            pltpu.VMEM(x.shape, BF16),
            pltpu.VMEM(dy.shape, BF16),
            pltpu.VMEM(table.shape, BF16),
            pltpu.VMEM(x.shape, BF16),
            pltpu.SemaphoreType.DMA((3,)),
        ],
        limit=60,
        flops=2 * blocks * depth * lon_count * 2 * slots * chans,
    )
    far = list(range(blocks - 1, 0, -1))
    got = [coded_parts[0], *reversed(crossed_all(coded_parts, far).values())]
    leg_rows = jnp.pad(
        jnp.transpose(legendre, (1, 0, 2)), ((0, 0), (0, padded_modes - local_modes), (0, 0))
    )
    padded = (lon_count + 2 * REACH, chans)
    tap_shape = shape((TAP_ROWS, chans), F32)
    mixer, back, first_rim, second_rim, base, slope, base_grad, tap_part = call(
        functools.partial(prepare_kernel, local_modes, blocks),
        [shape((pair_rows, 2 * chans), F32), shape((degrees, pair_rows), BF16), rim, rim]
        + [field, field, field, tap_shape],
        [SMEM, SMEM] + [VMEM] * 5,
        (band_rows, tap_shift, leg_rows, spectral_filter, x, dy, tap_weight),
        scratch=[pltpu.VMEM((pair_rows, degrees), BF16), pltpu.VMEM(x.shape, BF16)]
        + [pltpu.VMEM((slots + 1, *padded), F32)] * 2,
        limit=big,
        flops=2 * pair_rows * degrees * 2 * chans,
        moved=8 * pair_rows * chans,
    )
    first_rim, second_rim, got[-1] = lax.optimization_barrier((first_rim, second_rim, got[-1]))
    first_rim = crossed(first_rim, 1)
    inner = [(i, i ^ 1) for i in range(blocks)]
    inner = [(i + 1, j + 1) for i, j in inner if max(i, j) + 1 < blocks]
    second_rim = lax.ppermute(second_rim, "space", inner)
    spectral = shape((lat_count, 2, padded_modes, chans), F32)
    keep, *sends, coeff, grad = call(
        functools.partial(gradient_kernel, blocks, slots, lat_count, local_modes),
        [shape((share, chans), F32)] + [shape((share, chans), BF16)] * 3 + [spectral] * 2,
        [SMEM, SMEM] + [VMEM] * (1 + blocks),
        (band_rows, quad_weight, back, *got),
        scratch=[
            pltpu.VMEM((pair_rows, 2 * chans), F32),
            pltpu.VMEM((degrees, 2 * chans), F32),
            pltpu.VMEM((blocks, depth + 8, 2 * slots * chans), F32),
        ],
        limit=big,
        flops=20 * degrees * pair_rows * 2 * chans,
    )
    got_sums = around(sends)
    back_parts = call(
        functools.partial(return_kernel, blocks, local_modes),
        [coded] * blocks,
        [SMEM, SMEM] + [VMEM] * 3,
        (band_rows, quad_weight, mixer, coeff, grad),
        scratch=[pltpu.VMEM(spectral.shape, F32)] * 2 + [pltpu.VMEM((depth + 8, 2 * slots * chans), F32)],
        limit=big,
    )
    rim_sum, rim_grad, tap_part = call(
        functools.partial(rim_kernel, blocks),
        [shape((2, lon_count, chans), F32)] * 2 + [tap_shape],
        [SMEM, SMEM] + [VMEM] * 5,
        (band_rows, tap_shift, dy, first_rim, second_rim, tap_weight, tap_part),
        scratch=[pltpu.VMEM((2, *padded), F32)] * 2,
    )
    message = shape((share + 2 * TAP_ROWS, chans), BF16)
    back_parts, tap_part = lax.optimization_barrier((back_parts, tap_part))
    own = call(quarter_kernel, message, [VMEM] * 5, (keep, *[got_sums[at] for at in (2, 0, 1)], tap_part))
    back_parts, own = lax.optimization_barrier((back_parts, own))
    returned = [back_parts[0], *reversed(crossed_all(back_parts, far).values())]
    steps = [(1 << bit, "space") for bit in range(1, blocks.bit_length() - 1)]
    steps += [(1 << bit, "ens") for bit in range(1, members.bit_length() - 1)]
    for at, (distance, axis) in enumerate(steps):
        scales = (members, members * lat_count) if at == len(steps) - 1 else (1, 1)
        own = call(
            functools.partial(add_kernel, *scales),
            message,
            [VMEM] * 2,
            (own, crossed(own, distance, axis)),
            flops=3900000000 if at == 0 else 0,
        )
    quarters = [own, *around([own] * 3)]
    early_sum, early_grad = call(
        early_kernel,
        [field, field],
        [SMEM] + [VMEM] * 8,
        (band_rows, table_out, base, slope, base_grad, rim_sum, rim_grad, *returned[:2]),
    )
    quarters, early_sum = lax.optimization_barrier((quarters, early_sum))
    filter_grad, tap_grad = call(
        spread_kernel,
        [shape((2, degrees, chans), F32), shape((tap_weight.shape[0], chans), F32)],
        [VMEM] * 4,
        quarters,
        scratch=[pltpu.VMEM((4, TAP_ROWS, chans), F32)],
    )
    far_parts, filter_grad = lax.optimization_barrier((returned[2:], filter_grad))
    pieces = 4
    output, input_grad = call(
        functools.partial(finish_kernel, blocks),
        [shape(x.shape, BF16)] * 2,
        [SMEM] + [VMEM] * (2 + blocks),
        (band_rows, table_out, early_sum, early_grad, slope, *far_parts),
        scratch=[
            pltpu.VMEM(x.shape, BF16),
            pltpu.VMEM(x.shape, BF16),
            pltpu.SemaphoreType.DMA((2 * slots * pieces,)),
        ],
        flops=2 * blocks * depth * lon_count * 2 * slots * chans,
        out_specs=[HBM, HBM],
    )
    return (output[None], input_grad[None], filter_grad, tap_grad)


def solution(mesh):
    in_specs = (
        P(("groups", "ens"), "space", None, "chan"),
        P(("groups", "ens"), "space", None, "chan"),
        P("groups"),
        P(),
        P(),
        P("space", None, None),
        P(None, None, "chan"),
        P(None, "chan"),
    )
    out_specs = (
        P(("groups", "ens"), "space", None, "chan"),
        P(("groups", "ens"), "space", None, "chan"),
        P("groups", None, "chan"),
        P("groups", "chan"),
    )
    return jax.shard_map(body, mesh=mesh, in_specs=in_specs, out_specs=out_specs, check_vma=False)
```

```python
import functools
import math

import jax
import jax.numpy as jnp
import ml_dtypes
import numpy as np
from jax import lax
from jax.experimental import pallas as pl
from jax.experimental.pallas import tpu as pltpu
from jax.sharding import PartitionSpec as P

F32 = jnp.float32
BF16 = jnp.bfloat16
VMEM = pl.BlockSpec(memory_space=pltpu.VMEM)
SMEM = pl.BlockSpec(memory_space=pltpu.SMEM)
HBM = pl.BlockSpec(memory_space=pltpu.HBM)
REACH = 8
TAP_ROWS = 16


def gelu_value(values):
    return 0.5 * values * (1.0 + lax.erf(values * 0.7071067811865476))


def gelu_slope(values):
    return (
        0.5 * (1.0 + lax.erf(values * 0.7071067811865476))
        + values * jnp.exp(-0.5 * values * values) * 0.3989422804014327
    )


def round_up(count, step):
    return -(-count // step) * step


def fourier_table(lon_count, blocks, local_modes, depth):
    lon_ids = np.arange(lon_count)
    mode_ids = np.arange(blocks * local_modes)
    phase = (mode_ids[:, None] * lon_ids[None, :] % lon_count) * (2.0 * math.pi / lon_count)
    factor = 1.0 / math.sqrt(lon_count)
    both = np.stack([np.cos(phase), -np.sin(phase)]) * factor
    both = both.reshape(2, blocks, local_modes, lon_count).transpose(1, 0, 2, 3)
    both = both.reshape(blocks, 2 * local_modes, lon_count)
    both = np.pad(both, ((0, 0), (0, depth - 2 * local_modes), (0, 0)))
    return both.astype(ml_dtypes.bfloat16)


def lat_pairs(lat_count):
    return [(a, b) for a in range(lat_count) for b in range(a, lat_count)]


def first_row_of(rows_ref, block, blocks):
    total = jnp.int32(0)
    for other in range(blocks):
        total = total + jnp.where(other < block, rows_ref[other], 0)
    return total


def call(kernel, out_shape, in_specs, args, scratch=(), limit=32, flops=0, moved=1024, out_specs=None):
    return pl.pallas_call(
        kernel,
        out_shape=out_shape,
        in_specs=in_specs,
        out_specs=out_specs or jax.tree.map(lambda _: VMEM, out_shape),
        scratch_shapes=list(scratch),
        compiler_params=pltpu.CompilerParams(vmem_limit_bytes=limit * 1024 * 1024),
        cost_estimate=pl.CostEstimate(flops=flops, bytes_accessed=moved, transcendentals=0),
    )(*args)


def activate(x_ref, act_ref):
    slots, lon_count, _ = x_ref.shape
    step = 64 if lon_count % 64 == 0 else lon_count

    def run(i, carry):
        part = pl.ds(pl.multiple_of(i * step, step), step)
        for slot in range(slots):
            act_ref[slot, part, :] = gelu_value(x_ref[slot, part, :].astype(F32)).astype(BF16)
        return carry

    lax.fori_loop(0, lon_count // step, run, 0)


def forward_kernel(blocks, x_hbm, dy_hbm, table_hbm, *refs):
    outs, (x_ref, dy_ref, table_ref, act_ref, sems) = refs[:blocks], refs[blocks:]
    slots = x_ref.shape[0]
    me = lax.axis_index("space")
    loads = [
        pltpu.make_async_copy(source, target, sems.at[i])
        for i, (source, target) in enumerate(
            [(x_hbm, x_ref), (dy_hbm, dy_ref), (table_hbm, table_ref)]
        )
    ]
    for load in loads:
        load.start()
    loads[0].wait()
    activate(x_ref, act_ref)
    loads[1].wait()
    source = jnp.concatenate(
        [dy_ref[slot] for slot in range(slots)] + [act_ref[slot] for slot in range(slots)], axis=-1
    )
    loads[2].wait()
    for shift in range(blocks):
        block = jnp.bitwise_xor(me, shift)
        sums = jnp.dot(table_ref[block], source, preferred_element_type=F32)
        outs[shift][...] = sums.astype(BF16)


def wrapped(target, row, value):
    lon_count = value.shape[0]
    target[row, REACH : REACH + lon_count, :] = value
    target[row, :REACH, :] = value[lon_count - REACH :, :]
    target[row, REACH + lon_count :, :] = value[:REACH, :]


def folded(values):
    return jnp.sum(values.reshape(values.shape[0] // 8, 8, values.shape[1]), axis=0)


def prepare_kernel(
    local_modes, blocks, rows_ref, shift_ref, leg_ref, filter_ref, x_ref, dy_ref, taps_ref,
    mixer_ref, back_ref, first_rim, second_rim, base_ref, slope_ref, base_grad_ref, tap_ref,
    pairs_ref, act_ref, acts, grads,
):
    me = lax.axis_index("space")
    activate(x_ref, act_ref)
    last = rows_ref[me] - 1
    odd = jnp.bitwise_and(me, 1)
    for rim_ref, row in ((first_rim, last * (1 - odd)), (second_rim, last * odd)):
        rim_ref[0] = act_ref[row]
        rim_ref[1] = dy_ref[row]
    pair_products(local_modes, leg_ref, filter_ref, mixer_ref, back_ref, pairs_ref)
    disco_inner(
        blocks, rows_ref, shift_ref, x_ref, dy_ref, act_ref, taps_ref,
        base_ref, slope_ref, base_grad_ref, tap_ref, acts, grads,
    )


def pair_products(local_modes, leg_ref, filter_ref, mixer_ref, back_ref, pairs_ref):
    me = lax.axis_index("space")
    lat_count, padded_modes, _ = leg_ref.shape
    pairs = lat_pairs(lat_count)
    used = len(pairs) * padded_modes
    mode = me * local_modes + lax.broadcasted_iota(
        jnp.int32, (padded_modes, 1), 0
    )
    twice = jnp.where(mode == 0, 1.0, 2.0)
    for index, (a, b) in enumerate(pairs):
        at = index * padded_modes
        pairs_ref[at : at + padded_modes, :] = (
            leg_ref[a].astype(F32) * leg_ref[b].astype(F32) * twice
        ).astype(BF16)
    if pairs_ref.shape[0] > used:
        pairs_ref[used:, :] = jnp.zeros((pairs_ref.shape[0] - used, pairs_ref.shape[1]), BF16)
    both = jnp.concatenate([filter_ref[0], filter_ref[1]], axis=-1)
    mixer_ref[...] = jnp.dot(pairs_ref[...], both, preferred_element_type=F32)

    def turn(i, carry):
        part = pl.ds(pl.multiple_of(i * 128, 128), 128)
        back_ref[:, part] = pairs_ref[part, :].astype(F32).T.astype(BF16)
        return carry

    lax.fori_loop(0, pairs_ref.shape[0] // 128, turn, 0)


def own_quarter():
    space_bit = jnp.bitwise_and(lax.axis_index("space"), 1)
    return 2 * space_bit + jnp.bitwise_and(lax.axis_index("ens"), 1)


def gradient_kernel(blocks, slots, lat_count, local_modes, rows_ref, quad_ref, back_ref, *refs):
    ins, sums, coeff, grad = refs[:blocks], refs[blocks : blocks + 4], *refs[blocks + 4 : blocks + 6]
    products, gradient, wide = refs[blocks + 6 :]
    padded_modes, chans = coeff.shape[2:]
    me = lax.axis_index("space")
    pairs = lat_pairs(lat_count)
    whole = local_modes // 8 * 8
    if padded_modes > whole:
        zeros = jnp.zeros((padded_modes - whole, chans), F32)
        for lat in range(lat_count):
            for part in range(2):
                coeff[lat, part, whole:, :] = zeros
                grad[lat, part, whole:, :] = zeros

    for shift in range(blocks):
        block = jnp.bitwise_xor(me, shift)
        start = first_row_of(rows_ref, block, blocks)
        wide[shift, : ins[shift].shape[0], :] = ins[shift][...].astype(F32)
        for slot in range(slots):
            lat = jnp.minimum(start + slot, lat_count - 1)

            @pl.when(slot < rows_ref[block])
            def _():
                weight = quad_ref[lat]
                for part in range(2):
                    at = place(slots, local_modes, chans, 0, slot, part)
                    grad[lat, part, :local_modes, :] = wide[(shift, *at)]
                    at = place(slots, local_modes, chans, 1, slot, part)
                    coeff[lat, part, :local_modes, :] = wide[(shift, *at)] * weight

    def multiply(i, carry):
        rows = pl.ds(pl.multiple_of(i * 8, 8), 8)
        a0, a1, b0, b1 = loaded(coeff, grad, rows)
        for index, (a, b) in enumerate(pairs):
            at = pl.ds(pl.multiple_of(index * padded_modes + i * 8, 8), 8)
            h0 = h1 = jnp.zeros((8, chans), F32)
            for p, q in [(a, b)] if a == b else [(a, b), (b, a)]:
                h0 = h0 + b0[p] * a0[q] + b1[p] * a1[q]
                h1 = h1 + b1[p] * a0[q] - b0[p] * a1[q]
            products[at, :chans] = h0
            products[at, chans:] = h1
        return carry

    lax.fori_loop(0, padded_modes // 8, multiply, 0)
    used = len(pairs) * padded_modes
    if products.shape[0] > used:
        products[used:, :] = jnp.zeros((products.shape[0] - used, products.shape[1]), F32)
    gradient[...] = jnp.dot(
        back_ref[...], products[...].astype(BF16), preferred_element_type=F32
    )
    share = gradient.shape[0] // 4
    for shift, target in enumerate(sums):
        at = jnp.bitwise_xor(own_quarter(), shift) * share
        part = gradient[pl.ds(pl.multiple_of(at, share), share), :]
        both = jnp.concatenate([part[:, :chans], part[:, chans:]], axis=0)
        target[...] = both.astype(target.dtype)


def loaded(coeff, grad, rows):
    return [
        [ref[lat, part, rows, :] for lat in range(ref.shape[0])]
        for ref in (coeff, grad)
        for part in range(2)
    ]


def place(slots, local_modes, chans, field, slot, part):
    at = (field * slots + slot) * chans
    return slice(part * local_modes, (part + 1) * local_modes), slice(at, at + chans)


def return_kernel(blocks, local_modes, rows_ref, quad_ref, mixer_ref, coeff, grad, *refs):
    outs, (synth, grad_coeff, wide) = refs[:blocks], refs[blocks:]
    lat_count, _, padded_modes, chans = coeff.shape
    slots = wide.shape[1] // (2 * chans)
    me = lax.axis_index("space")
    pairs = lat_pairs(lat_count)

    def mix(i, carry):
        rows = pl.ds(pl.multiple_of(i * 8, 8), 8)
        a0, a1, b0, b1 = loaded(coeff, grad, rows)
        zero = jnp.zeros((8, chans), F32)
        y0, y1, z0, z1 = ([zero] * lat_count for _ in range(4))
        for index, (a, b) in enumerate(pairs):
            at = pl.ds(pl.multiple_of(index * padded_modes + i * 8, 8), 8)
            real = mixer_ref[at, :chans]
            imag = mixer_ref[at, chans:]
            for p, q in [(a, b)] if a == b else [(a, b), (b, a)]:
                y0[p] = y0[p] + real * a0[q] - imag * a1[q]
                y1[p] = y1[p] + imag * a0[q] + real * a1[q]
                z0[q] = z0[q] + real * b0[p] + imag * b1[p]
                z1[q] = z1[q] + real * b1[p] - imag * b0[p]
        for lat in range(lat_count):
            synth[lat, 0, rows, :] = y0[lat]
            synth[lat, 1, rows, :] = y1[lat]
            grad_coeff[lat, 0, rows, :] = z0[lat] * quad_ref[lat]
            grad_coeff[lat, 1, rows, :] = z1[lat] * quad_ref[lat]
        return carry

    lax.fori_loop(0, padded_modes // 8, mix, 0)
    whole = 2 * local_modes // 8 * 8
    wide[whole:, :] = jnp.zeros((wide.shape[0] - whole, wide.shape[1]), F32)
    for shift in range(blocks):
        block = jnp.bitwise_xor(me, shift)
        start = first_row_of(rows_ref, block, blocks)
        for slot in range(slots):
            lat = jnp.minimum(start + slot, lat_count - 1)
            for part in range(2):
                at = place(slots, local_modes, chans, 0, slot, part)
                wide[at] = synth[lat, part, :local_modes, :]
                at = place(slots, local_modes, chans, 1, slot, part)
                wide[at] = grad_coeff[lat, part, :local_modes, :]
        outs[shift][...] = wide[: outs[shift].shape[0], :].astype(BF16)


def disco_inner(
    blocks, rows_ref, shift_ref, x_ref, dy_ref, act_ref, taps_ref,
    base_ref, slope_ref, base_grad_ref, tap_ref, acts, grads,
):
    slots, lon_count, chans = x_ref.shape
    taps = taps_ref.shape[0]
    me = lax.axis_index("space")
    live = rows_ref[me]
    start = first_row_of(rows_ref, me, blocks)
    for slot in range(slots):
        alive = jnp.where(slot < live, 1.0, 0.0)
        wrapped(acts, slot, act_ref[slot].astype(F32))
        wrapped(grads, slot, dy_ref[slot].astype(F32) * alive)
    acts[slots] = jnp.zeros(acts.shape[1:], F32)
    grads[slots] = jnp.zeros(grads.shape[1:], F32)
    weights = taps_ref[...].astype(F32)
    step = 32 if lon_count % 32 == 0 else lon_count
    totals = [jnp.zeros((8, chans), F32)] * taps
    top = shift_ref.shape[0] - 1
    for slot in range(slots):
        below = jnp.where(slot + 1 < live, slot + 1, slots)
        sources = [(1, slot)]
        if slot > 0:
            sources.append((0, slot - 1))
        if slot + 1 < slots:
            sources.append((2, below))
        lat = jnp.clip(start + slot, 0, top)
        ahead, behind = [], []
        for offset, row in sources:
            other = jnp.clip(lat + offset - 1, 0, top)
            for column in range(3):
                t = 3 * offset + column
                ahead.append((t, row, REACH + shift_ref[lat, t]))
                t = 3 * (2 - offset) + column
                behind.append((t, row, REACH - shift_ref[other, t]))

        def inner(i, totals):
            at = pl.multiple_of(i * step, step)
            part = pl.ds(at, step)
            x = x_ref[slot, part, :].astype(F32)
            dy = grads[slot, pl.ds(pl.multiple_of(REACH + at, 8), step), :]
            out = x
            back = jnp.zeros((step, chans), F32)
            fresh = list(totals)
            for t, row, first in ahead:
                moved = acts[row, pl.ds(at + first, step), :]
                out = out + moved * weights[t : t + 1, :]
                fresh[t] = fresh[t] + folded(moved * dy)
            for t, row, first in behind:
                back = back + grads[row, pl.ds(at + first, step), :] * weights[t : t + 1, :]
            slope = gelu_slope(x)
            base_ref[slot, part, :] = out
            slope_ref[slot, part, :] = slope
            base_grad_ref[slot, part, :] = dy + back * slope
            return tuple(fresh)

        totals = list(lax.fori_loop(0, lon_count // step, inner, tuple(totals)))
    lines = [jnp.sum(total, axis=0, keepdims=True) for total in totals]
    lines.append(jnp.zeros((tap_ref.shape[0] - taps, chans), F32))
    tap_ref[...] = jnp.concatenate(lines, axis=0)


def rim_tap_kernel(
    blocks, rows_ref, shift_ref, dy_ref, first_rim, second_rim, inner_ref, tap_ref, acts,
):
    _, lon_count, chans = dy_ref.shape
    me = lax.axis_index("space")
    live = rows_ref[me]
    start = first_row_of(rows_ref, me, blocks)
    odd = jnp.bitwise_and(me, 1)
    for source, row in ((first_rim, 1 - odd), (second_rim, odd)):
        wrapped(acts, row, source[0].astype(F32))
    step = 256 if lon_count % 256 == 0 else lon_count
    top = shift_ref.shape[0] - 1
    lines = [jnp.zeros((1, chans), F32)] * tap_ref.shape[0]
    for side in range(2):
        slot = 0 if side == 0 else live - 1
        lat = jnp.clip(start + slot, 0, top)
        ahead = [(t, REACH + shift_ref[lat, t]) for t in range(6 * side, 6 * side + 3)]

        def rim(i, totals):
            at = pl.multiple_of(i * step, step)
            part = pl.ds(at, step)
            dy = dy_ref[slot, part, :].astype(F32)
            fresh = []
            for total, (t, first) in zip(totals, ahead):
                moved = acts[side, pl.ds(at + first, step), :]
                fresh.append(total + folded(moved * dy))
            return tuple(fresh)

        totals = lax.fori_loop(0, lon_count // step, rim, (jnp.zeros((8, chans), F32),) * 3)
        for (t, _), total in zip(ahead, totals):
            lines[t] = jnp.sum(total, axis=0, keepdims=True)
    tap_ref[...] = inner_ref[...] + jnp.concatenate(lines, axis=0)


def rim_kernel(
    blocks, rows_ref, shift_ref, first_rim, second_rim, taps_ref, rim_ref, rim_grad_ref, acts, grads,
):
    _, lon_count, chans = first_rim.shape
    me = lax.axis_index("space")
    live = rows_ref[me]
    start = first_row_of(rows_ref, me, blocks)
    odd = jnp.bitwise_and(me, 1)
    for source, row in ((first_rim, 1 - odd), (second_rim, odd)):
        wrapped(acts, row, source[0].astype(F32))
        wrapped(grads, row, source[1].astype(F32))
    weights = taps_ref[...].astype(F32)
    step = 128 if lon_count % 128 == 0 else lon_count
    top = shift_ref.shape[0] - 1
    for side in range(2):
        slot = 0 if side == 0 else live - 1
        lat = jnp.clip(start + slot, 0, top)
        other = jnp.clip(lat + 2 * side - 1, 0, top)
        ahead = [(t, REACH + shift_ref[lat, t]) for t in range(6 * side, 6 * side + 3)]
        behind = [(t, REACH - shift_ref[other, t]) for t in range(6 - 6 * side, 9 - 6 * side)]

        def rim(i, carry):
            at = pl.multiple_of(i * step, step)
            part = pl.ds(at, step)
            out = back = jnp.zeros((step, chans), F32)
            for t, first in ahead:
                moved = acts[side, pl.ds(at + first, step), :]
                out = out + moved * weights[t : t + 1, :]
            for t, first in behind:
                back = back + grads[side, pl.ds(at + first, step), :] * weights[t : t + 1, :]
            rim_ref[side, part, :] = out
            rim_grad_ref[side, part, :] = back
            return carry

        lax.fori_loop(0, lon_count // step, rim, 0)


def split_taps(taps, out_ref, count):
    high = taps.astype(BF16)
    out_ref[count : count + TAP_ROWS, :] = high
    out_ref[count + TAP_ROWS :, :] = (taps - high.astype(F32)).astype(BF16)


def joined_taps(rows):
    return rows[-2 * TAP_ROWS : -TAP_ROWS, :] + rows[-TAP_ROWS:, :]


def split_taps(taps, out_ref, count):
    high = taps.astype(BF16)
    out_ref[count : count + TAP_ROWS, :] = high
    out_ref[count + TAP_ROWS :, :] = (taps - high.astype(F32)).astype(BF16)


def joined_taps(ref):
    rows = ref[ref.shape[0] - 2 * TAP_ROWS :, :].astype(F32)
    return rows[:TAP_ROWS, :] + rows[TAP_ROWS:, :]


def added(first_ref, second_ref):
    return first_ref[...].astype(F32) + second_ref[...].astype(F32)


def quarter_kernel(kept_ref, first_ref, second_ref, third_ref, tap_ref, out_ref):
    total = kept_ref[...]
    for ref in (first_ref, second_ref, third_ref):
        total = total + ref[...].astype(F32)
    out_ref[: total.shape[0], :] = total.astype(BF16)
    split_taps(tap_ref[...], out_ref, total.shape[0])


def add_kernel(scale, tap_scale, own_ref, other_ref, out_ref):
    count = own_ref.shape[0] - 2 * TAP_ROWS
    out_ref[:count, :] = (added(own_ref, other_ref)[:count, :] / scale).astype(BF16)
    split_taps((joined_taps(own_ref) + joined_taps(other_ref)) / tap_scale, out_ref, count)


def early_kernel(
    rows_ref, table_ref, base_ref, slope_ref, base_grad_ref, rim_ref, rim_grad_ref,
    own_ref, near_ref, sum_ref, grad_ref,
):
    slots, lon_count, chans = base_ref.shape
    me = lax.axis_index("space")
    live = rows_ref[me]
    step = lon_count // 4
    for at in range(0, lon_count, step):
        rows = slice(at, at + step)
        sums = jnp.dot(table_ref[me, rows, :], own_ref[...], preferred_element_type=F32)
        sums = sums + jnp.dot(
            table_ref[jnp.bitwise_xor(me, 1), rows, :], near_ref[...], preferred_element_type=F32
        )
        for slot in range(slots):
            out = base_ref[slot, rows, :] + sums[:, slot * chans : (slot + 1) * chans]
            back = sums[:, (slots + slot) * chans : (slots + slot + 1) * chans]
            if slot == 0:
                out = out + rim_ref[0, rows, :]
                back = back + rim_grad_ref[0, rows, :]
            last = slot == live - 1
            out = out + jnp.where(last, rim_ref[1, rows, :], 0.0)
            back = back + jnp.where(last, rim_grad_ref[1, rows, :], 0.0)
            sum_ref[slot, rows, :] = out
            grad_ref[slot, rows, :] = base_grad_ref[slot, rows, :] + back * slope_ref[slot, rows, :]


def spread_kernel(*refs):
    quarters, (filter_ref, tap_ref, held) = refs[:4], refs[4:]
    share = filter_ref.shape[1] // 4
    for shift, ref in enumerate(quarters):
        quarter = jnp.bitwise_xor(own_quarter(), shift)
        at = pl.ds(pl.multiple_of(quarter * share, share), share)
        rows = ref[: 2 * share, :].astype(F32)
        filter_ref[0, at, :] = rows[:share, :]
        filter_ref[1, at, :] = rows[share:, :]
        held[quarter] = joined_taps(ref)
    taps = (held[0] + held[1]) + (held[2] + held[3])
    tap_ref[...] = taps[: tap_ref.shape[0], :]


def finish_kernel(
    blocks, rows_ref, table_ref, sum_ref, early_ref, slope_ref, *refs
):
    ins, refs = refs[: blocks - 2], refs[blocks - 2 :]
    out_hbm, grad_hbm, out_ref, grad_ref, sems = refs
    slots, lon_count, chans = sum_ref.shape
    me = lax.axis_index("space")
    live = rows_ref[me]
    stores = []
    parts = sems.shape[0] // (2 * slots)
    step = lon_count // parts
    for part in range(parts):
        rows = slice(part * step, (part + 1) * step)
        sums = jnp.zeros((step, 2 * slots * chans), F32)
        for at, ref in enumerate(ins):
            block = jnp.bitwise_xor(me, at + 2)
            sums = sums + jnp.dot(table_ref[block, rows, :], ref[...], preferred_element_type=F32)
        for slot in range(slots):
            out = sum_ref[slot, rows, :] + sums[:, slot * chans : (slot + 1) * chans]
            back = sums[:, (slots + slot) * chans : (slots + slot + 1) * chans]
            grad = early_ref[slot, rows, :] + back * slope_ref[slot, rows, :]
            alive = slot < live
            out_ref[slot, rows, :] = jnp.where(alive, out, 0.0).astype(BF16)
            grad_ref[slot, rows, :] = jnp.where(alive, grad, 0.0).astype(BF16)
            for made, target in ((out_ref, out_hbm), (grad_ref, grad_hbm)):
                place = (slot, pl.ds(part * step, step))
                stores.append(
                    pltpu.make_async_copy(made.at[place], target.at[place], sems.at[len(stores)])
                )
                stores[-1].start()
    for store in stores:
        store.wait()


def crossed(values, distance, axis="space"):
    count = lax.axis_size(axis)
    return lax.ppermute(values, axis, [(i, i ^ distance) for i in range(count)])


def around(parts):
    count = lax.axis_size("space") * lax.axis_size("ens")
    flip = lax.axis_size("ens") + 1
    return [
        crossed(parts[0], 1, "ens"),
        crossed(parts[1], 1),
        lax.ppermute(parts[2], ("space", "ens"), [(i, i ^ flip) for i in range(count)]),
    ]


def crossed_all(parts, distances):
    return {s: crossed(parts[s], s) for s in distances}


def body(
    fields, cotangent, band_rows, tap_shift, quad_weight, legendre, spectral_filter, tap_weight
):
    blocks = lax.axis_size("space")
    members = lax.axis_size("ens")
    _, slots, lon_count, chans = fields.shape
    local_modes, lat_count, degrees = legendre.shape
    padded_modes = round_up(local_modes, 16)
    depth = round_up(2 * local_modes, 8)
    pairs = len(lat_pairs(lat_count))
    pair_rows = round_up(pairs * padded_modes, 128)
    share = degrees // 2
    big = 32 if pair_rows <= 4096 else 60
    shape = jax.ShapeDtypeStruct
    table = fourier_table(lon_count, blocks, local_modes, depth)
    table_in = jnp.asarray(table)
    table_out = jnp.asarray(np.ascontiguousarray(table.transpose(0, 2, 1)))
    x, dy = fields[0], cotangent[0]
    field = shape((slots, lon_count, chans), F32)
    coded = shape((depth, 2 * slots * chans), BF16)
    rim = shape((2, lon_count, chans), BF16)

    coded_parts = call(
        functools.partial(forward_kernel, blocks),
        [coded] * blocks,
        [HBM] * 3,
        (x, dy, table_in),
        scratch=[
            pltpu.VMEM(x.shape, BF16),
            pltpu.VMEM(dy.shape, BF16),
            pltpu.VMEM(table.shape, BF16),
            pltpu.VMEM(x.shape, BF16),
            pltpu.SemaphoreType.DMA((3,)),
        ],
        limit=60,
        flops=2 * blocks * depth * lon_count * 2 * slots * chans,
    )
    far = list(range(blocks - 1, 0, -1))
    got = [coded_parts[0], *reversed(crossed_all(coded_parts, far).values())]
    leg_rows = jnp.pad(
        jnp.transpose(legendre, (1, 0, 2)), ((0, 0), (0, padded_modes - local_modes), (0, 0))
    )
    padded = (lon_count + 2 * REACH, chans)
    tap_shape = shape((TAP_ROWS, chans), F32)
    mixer, back, first_rim, second_rim, base, slope, base_grad, tap_part = call(
        functools.partial(prepare_kernel, local_modes, blocks),
        [shape((pair_rows, 2 * chans), F32), shape((degrees, pair_rows), BF16), rim, rim]
        + [field, field, field, tap_shape],
        [SMEM, SMEM] + [VMEM] * 5,
        (band_rows, tap_shift, leg_rows, spectral_filter, x, dy, tap_weight),
        scratch=[pltpu.VMEM((pair_rows, degrees), BF16), pltpu.VMEM(x.shape, BF16)]
        + [pltpu.VMEM((slots + 1, *padded), F32)] * 2,
        limit=big,
        flops=2 * pair_rows * degrees * 2 * chans,
        moved=8 * pair_rows * chans,
    )
    first_rim, second_rim, got[-1] = lax.optimization_barrier((first_rim, second_rim, got[-1]))
    first_rim = crossed(first_rim, 1)
    inner = [(i, i ^ 1) for i in range(blocks)]
    inner = [(i + 1, j + 1) for i, j in inner if max(i, j) + 1 < blocks]
    second_rim = lax.ppermute(second_rim, "space", inner)
    spectral = shape((lat_count, 2, padded_modes, chans), F32)
    keep, *sends, coeff, grad = call(
        functools.partial(gradient_kernel, blocks, slots, lat_count, local_modes),
        [shape((share, chans), F32)] + [shape((share, chans), BF16)] * 3 + [spectral] * 2,
        [SMEM, SMEM] + [VMEM] * (1 + blocks),
        (band_rows, quad_weight, back, *got),
        scratch=[
            pltpu.VMEM((pair_rows, 2 * chans), F32),
            pltpu.VMEM((degrees, 2 * chans), F32),
            pltpu.VMEM((blocks, depth + 8, 2 * slots * chans), F32),
        ],
        limit=big,
        flops=20 * degrees * pair_rows * 2 * chans,
    )
    got_sums = around(sends)
    back_parts = call(
        functools.partial(return_kernel, blocks, local_modes),
        [coded] * blocks,
        [SMEM, SMEM] + [VMEM] * 3,
        (band_rows, quad_weight, mixer, coeff, grad),
        scratch=[pltpu.VMEM(spectral.shape, F32)] * 2 + [pltpu.VMEM((depth + 8, 2 * slots * chans), F32)],
        limit=big,
    )
    tap_part = call(
        functools.partial(rim_tap_kernel, blocks),
        tap_shape,
        [SMEM, SMEM] + [VMEM] * 4,
        (band_rows, tap_shift, dy, first_rim, second_rim, tap_part),
        scratch=[pltpu.VMEM((2, *padded), F32)],
    )
    back_parts, tap_part = lax.optimization_barrier((back_parts, tap_part))
    message = shape((share + 2 * TAP_ROWS, chans), BF16)
    back_parts, tap_part = lax.optimization_barrier((back_parts, tap_part))
    own = call(quarter_kernel, message, [VMEM] * 5, (keep, *[got_sums[at] for at in (2, 0, 1)], tap_part))
    back_parts, own = lax.optimization_barrier((back_parts, own))
    returned = [back_parts[0], *reversed(crossed_all(back_parts, far).values())]
    steps = [(1 << bit, "space") for bit in range(1, blocks.bit_length() - 1)]
    steps += [(1 << bit, "ens") for bit in range(1, members.bit_length() - 1)]
    for at, (distance, axis) in enumerate(steps):
        scales = (members, members * lat_count) if at == len(steps) - 1 else (1, 1)
        own = call(
            functools.partial(add_kernel, *scales),
            message,
            [VMEM] * 2,
            (own, crossed(own, distance, axis)),
            flops=3900000000 if at == 0 else 0,
        )
    quarters = [own, *around([own] * 3)]
    rim_sum, rim_grad = call(
        functools.partial(rim_kernel, blocks),
        [shape((2, lon_count, chans), F32)] * 2,
        [SMEM, SMEM] + [VMEM] * 3,
        (band_rows, tap_shift, first_rim, second_rim, tap_weight),
        scratch=[pltpu.VMEM((2, *padded), F32)] * 2,
    )
    early_sum, early_grad = call(
        early_kernel,
        [field, field],
        [SMEM] + [VMEM] * 8,
        (band_rows, table_out, base, slope, base_grad, rim_sum, rim_grad, *returned[:2]),
    )
    quarters, early_sum = lax.optimization_barrier((quarters, early_sum))
    filter_grad, tap_grad = call(
        spread_kernel,
        [shape((2, degrees, chans), F32), shape((tap_weight.shape[0], chans), F32)],
        [VMEM] * 4,
        quarters,
        scratch=[pltpu.VMEM((4, TAP_ROWS, chans), F32)],
    )
    far_parts, filter_grad = lax.optimization_barrier((returned[2:], filter_grad))
    pieces = 4
    output, input_grad = call(
        functools.partial(finish_kernel, blocks),
        [shape(x.shape, BF16)] * 2,
        [SMEM] + [VMEM] * (2 + blocks),
        (band_rows, table_out, early_sum, early_grad, slope, *far_parts),
        scratch=[
            pltpu.VMEM(x.shape, BF16),
            pltpu.VMEM(x.shape, BF16),
            pltpu.SemaphoreType.DMA((2 * slots * pieces,)),
        ],
        flops=2 * blocks * depth * lon_count * 2 * slots * chans,
        out_specs=[HBM, HBM],
    )
    return (output[None], input_grad[None], filter_grad, tap_grad)


def solution(mesh):
    in_specs = (
        P(("groups", "ens"), "space", None, "chan"),
        P(("groups", "ens"), "space", None, "chan"),
        P("groups"),
        P(),
        P(),
        P("space", None, None),
        P(None, None, "chan"),
        P(None, "chan"),
    )
    out_specs = (
        P(("groups", "ens"), "space", None, "chan"),
        P(("groups", "ens"), "space", None, "chan"),
        P("groups", None, "chan"),
        P("groups", "chan"),
    )
    return jax.shard_map(body, mesh=mesh, in_specs=in_specs, out_specs=out_specs, check_vma=False)
```

```python
import functools
import math

import jax
import jax.numpy as jnp
import ml_dtypes
import numpy as np
from jax import lax
from jax.experimental import pallas as pl
from jax.experimental.pallas import tpu as pltpu
from jax.sharding import PartitionSpec as P

F32 = jnp.float32
BF16 = jnp.bfloat16
VMEM = pl.BlockSpec(memory_space=pltpu.VMEM)
SMEM = pl.BlockSpec(memory_space=pltpu.SMEM)
HBM = pl.BlockSpec(memory_space=pltpu.HBM)
REACH = 8
TAP_ROWS = 16


def gelu_value(values):
    return 0.5 * values * (1.0 + lax.erf(values * 0.7071067811865476))


def gelu_slope(values):
    return (
        0.5 * (1.0 + lax.erf(values * 0.7071067811865476))
        + values * jnp.exp(-0.5 * values * values) * 0.3989422804014327
    )


def round_up(count, step):
    return -(-count // step) * step


def fourier_table(lon_count, blocks, local_modes, depth):
    lon_ids = np.arange(lon_count)
    mode_ids = np.arange(blocks * local_modes)
    phase = (mode_ids[:, None] * lon_ids[None, :] % lon_count) * (2.0 * math.pi / lon_count)
    factor = 1.0 / math.sqrt(lon_count)
    both = np.stack([np.cos(phase), -np.sin(phase)]) * factor
    both = both.reshape(2, blocks, local_modes, lon_count).transpose(1, 0, 2, 3)
    both = both.reshape(blocks, 2 * local_modes, lon_count)
    both = np.pad(both, ((0, 0), (0, depth - 2 * local_modes), (0, 0)))
    return both.astype(ml_dtypes.bfloat16)


def lat_pairs(lat_count):
    return [(a, b) for a in range(lat_count) for b in range(a, lat_count)]


def first_row_of(rows_ref, block, blocks):
    total = jnp.int32(0)
    for other in range(blocks):
        total = total + jnp.where(other < block, rows_ref[other], 0)
    return total


def call(kernel, out_shape, in_specs, args, scratch=(), limit=32, flops=0, moved=1024, out_specs=None):
    return pl.pallas_call(
        kernel,
        out_shape=out_shape,
        in_specs=in_specs,
        out_specs=out_specs or jax.tree.map(lambda _: VMEM, out_shape),
        scratch_shapes=list(scratch),
        compiler_params=pltpu.CompilerParams(vmem_limit_bytes=limit * 1024 * 1024),
        cost_estimate=pl.CostEstimate(flops=flops, bytes_accessed=moved, transcendentals=0),
    )(*args)


def activate(x_ref, act_ref):
    slots, lon_count, _ = x_ref.shape
    step = 64 if lon_count % 64 == 0 else lon_count

    def run(i, carry):
        part = pl.ds(pl.multiple_of(i * step, step), step)
        for slot in range(slots):
            act_ref[slot, part, :] = gelu_value(x_ref[slot, part, :].astype(F32)).astype(BF16)
        return carry

    lax.fori_loop(0, lon_count // step, run, 0)


def forward_kernel(blocks, x_hbm, dy_hbm, table_hbm, *refs):
    outs, (x_ref, dy_ref, table_ref, act_ref, sems) = refs[:blocks], refs[blocks:]
    slots = x_ref.shape[0]
    me = lax.axis_index("space")
    loads = [
        pltpu.make_async_copy(source, target, sems.at[i])
        for i, (source, target) in enumerate(
            [(x_hbm, x_ref), (dy_hbm, dy_ref), (table_hbm, table_ref)]
        )
    ]
    for load in (loads[0], loads[2], loads[1]):
        load.start()
    loads[0].wait()
    activate(x_ref, act_ref)
    loads[1].wait()
    source = jnp.concatenate(
        [dy_ref[slot] for slot in range(slots)] + [act_ref[slot] for slot in range(slots)], axis=-1
    )
    loads[2].wait()
    for shift in range(blocks):
        block = jnp.bitwise_xor(me, shift)
        sums = jnp.dot(table_ref[block], source, preferred_element_type=F32)
        outs[shift][...] = sums.astype(BF16)


def wrapped(target, row, value):
    lon_count = value.shape[0]
    target[row, REACH : REACH + lon_count, :] = value
    target[row, :REACH, :] = value[lon_count - REACH :, :]
    target[row, REACH + lon_count :, :] = value[:REACH, :]


def folded(values):
    return jnp.sum(values.reshape(values.shape[0] // 8, 8, values.shape[1]), axis=0)


def prepare_kernel(
    local_modes, blocks, rows_ref, shift_ref, leg_ref, filter_ref, x_ref, dy_ref, taps_ref,
    mixer_ref, back_ref, first_rim, second_rim, base_ref, slope_ref, base_grad_ref, tap_ref,
    pairs_ref, act_ref, acts, grads,
):
    me = lax.axis_index("space")
    activate(x_ref, act_ref)
    last = rows_ref[me] - 1
    odd = jnp.bitwise_and(me, 1)
    for rim_ref, row in ((first_rim, last * (1 - odd)), (second_rim, last * odd)):
        rim_ref[0] = act_ref[row]
        rim_ref[1] = dy_ref[row]
    pair_products(local_modes, leg_ref, filter_ref, mixer_ref, back_ref, pairs_ref)
    disco_inner(
        blocks, rows_ref, shift_ref, x_ref, dy_ref, act_ref, taps_ref,
        base_ref, slope_ref, base_grad_ref, tap_ref, acts, grads,
    )


def pair_products(local_modes, leg_ref, filter_ref, mixer_ref, back_ref, pairs_ref):
    me = lax.axis_index("space")
    lat_count, padded_modes, _ = leg_ref.shape
    pairs = lat_pairs(lat_count)
    used = len(pairs) * padded_modes
    mode = me * local_modes + lax.broadcasted_iota(
        jnp.int32, (padded_modes, 1), 0
    )
    twice = jnp.where(mode == 0, 1.0, 2.0)
    for index, (a, b) in enumerate(pairs):
        at = index * padded_modes
        pairs_ref[at : at + padded_modes, :] = (
            leg_ref[a].astype(F32) * leg_ref[b].astype(F32) * twice
        ).astype(BF16)
    if pairs_ref.shape[0] > used:
        pairs_ref[used:, :] = jnp.zeros((pairs_ref.shape[0] - used, pairs_ref.shape[1]), BF16)
    both = jnp.concatenate([filter_ref[0], filter_ref[1]], axis=-1)
    mixer_ref[...] = jnp.dot(pairs_ref[...], both, preferred_element_type=F32)

    def turn(i, carry):
        part = pl.ds(pl.multiple_of(i * 128, 128), 128)
        back_ref[:, part] = pairs_ref[part, :].astype(F32).T.astype(BF16)
        return carry

    lax.fori_loop(0, pairs_ref.shape[0] // 128, turn, 0)


def own_quarter():
    space_bit = jnp.bitwise_and(lax.axis_index("space"), 1)
    return 2 * space_bit + jnp.bitwise_and(lax.axis_index("ens"), 1)


def gradient_kernel(blocks, slots, lat_count, local_modes, rows_ref, quad_ref, back_ref, *refs):
    ins, sums, coeff, grad = refs[:blocks], refs[blocks : blocks + 4], *refs[blocks + 4 : blocks + 6]
    products, gradient, wide = refs[blocks + 6 :]
    padded_modes, chans = coeff.shape[2:]
    me = lax.axis_index("space")
    pairs = lat_pairs(lat_count)
    whole = local_modes // 8 * 8
    if padded_modes > whole:
        zeros = jnp.zeros((padded_modes - whole, chans), F32)
        for lat in range(lat_count):
            for part in range(2):
                coeff[lat, part, whole:, :] = zeros
                grad[lat, part, whole:, :] = zeros

    for shift in range(blocks):
        block = jnp.bitwise_xor(me, shift)
        start = first_row_of(rows_ref, block, blocks)
        wide[shift, : ins[shift].shape[0], :] = ins[shift][...].astype(F32)
        for slot in range(slots):
            lat = jnp.minimum(start + slot, lat_count - 1)

            @pl.when(slot < rows_ref[block])
            def _():
                weight = quad_ref[lat]
                for part in range(2):
                    at = place(slots, local_modes, chans, 0, slot, part)
                    grad[lat, part, :local_modes, :] = wide[(shift, *at)]
                    at = place(slots, local_modes, chans, 1, slot, part)
                    coeff[lat, part, :local_modes, :] = wide[(shift, *at)] * weight

    def multiply(i, carry):
        rows = pl.ds(pl.multiple_of(i * 8, 8), 8)
        a0, a1, b0, b1 = loaded(coeff, grad, rows)
        for index, (a, b) in enumerate(pairs):
            at = pl.ds(pl.multiple_of(index * padded_modes + i * 8, 8), 8)
            h0 = h1 = jnp.zeros((8, chans), F32)
            for p, q in [(a, b)] if a == b else [(a, b), (b, a)]:
                h0 = h0 + b0[p] * a0[q] + b1[p] * a1[q]
                h1 = h1 + b1[p] * a0[q] - b0[p] * a1[q]
            products[at, :chans] = h0
            products[at, chans:] = h1
        return carry

    lax.fori_loop(0, padded_modes // 8, multiply, 0)
    used = len(pairs) * padded_modes
    if products.shape[0] > used:
        products[used:, :] = jnp.zeros((products.shape[0] - used, products.shape[1]), F32)
    gradient[...] = jnp.dot(
        back_ref[...], products[...].astype(BF16), preferred_element_type=F32
    )
    share = gradient.shape[0] // 4
    for shift, target in enumerate(sums):
        at = jnp.bitwise_xor(own_quarter(), shift) * share
        part = gradient[pl.ds(pl.multiple_of(at, share), share), :]
        both = jnp.concatenate([part[:, :chans], part[:, chans:]], axis=0)
        target[...] = both.astype(target.dtype)


def loaded(coeff, grad, rows):
    return [
        [ref[lat, part, rows, :] for lat in range(ref.shape[0])]
        for ref in (coeff, grad)
        for part in range(2)
    ]


def place(slots, local_modes, chans, field, slot, part):
    at = (field * slots + slot) * chans
    return slice(part * local_modes, (part + 1) * local_modes), slice(at, at + chans)


def return_kernel(blocks, local_modes, rows_ref, quad_ref, mixer_ref, coeff, grad, *refs):
    outs, (synth, grad_coeff, wide) = refs[:blocks], refs[blocks:]
    lat_count, _, padded_modes, chans = coeff.shape
    slots = wide.shape[1] // (2 * chans)
    me = lax.axis_index("space")
    pairs = lat_pairs(lat_count)

    def mix(i, carry):
        rows = pl.ds(pl.multiple_of(i * 8, 8), 8)
        a0, a1, b0, b1 = loaded(coeff, grad, rows)
        zero = jnp.zeros((8, chans), F32)
        y0, y1, z0, z1 = ([zero] * lat_count for _ in range(4))
        for index, (a, b) in enumerate(pairs):
            at = pl.ds(pl.multiple_of(index * padded_modes + i * 8, 8), 8)
            real = mixer_ref[at, :chans]
            imag = mixer_ref[at, chans:]
            for p, q in [(a, b)] if a == b else [(a, b), (b, a)]:
                y0[p] = y0[p] + real * a0[q] - imag * a1[q]
                y1[p] = y1[p] + imag * a0[q] + real * a1[q]
                z0[q] = z0[q] + real * b0[p] + imag * b1[p]
                z1[q] = z1[q] + real * b1[p] - imag * b0[p]
        for lat in range(lat_count):
            synth[lat, 0, rows, :] = y0[lat]
            synth[lat, 1, rows, :] = y1[lat]
            grad_coeff[lat, 0, rows, :] = z0[lat] * quad_ref[lat]
            grad_coeff[lat, 1, rows, :] = z1[lat] * quad_ref[lat]
        return carry

    lax.fori_loop(0, padded_modes // 8, mix, 0)
    whole = 2 * local_modes // 8 * 8
    wide[whole:, :] = jnp.zeros((wide.shape[0] - whole, wide.shape[1]), F32)
    for shift in range(blocks):
        block = jnp.bitwise_xor(me, shift)
        start = first_row_of(rows_ref, block, blocks)
        for slot in range(slots):
            lat = jnp.minimum(start + slot, lat_count - 1)
            for part in range(2):
                at = place(slots, local_modes, chans, 0, slot, part)
                wide[at] = synth[lat, part, :local_modes, :]
                at = place(slots, local_modes, chans, 1, slot, part)
                wide[at] = grad_coeff[lat, part, :local_modes, :]
        outs[shift][...] = wide[: outs[shift].shape[0], :].astype(BF16)


def disco_inner(
    blocks, rows_ref, shift_ref, x_ref, dy_ref, act_ref, taps_ref,
    base_ref, slope_ref, base_grad_ref, tap_ref, acts, grads,
):
    slots, lon_count, chans = x_ref.shape
    taps = taps_ref.shape[0]
    me = lax.axis_index("space")
    live = rows_ref[me]
    start = first_row_of(rows_ref, me, blocks)
    for slot in range(slots):
        alive = jnp.where(slot < live, 1.0, 0.0)
        wrapped(acts, slot, act_ref[slot].astype(F32))
        wrapped(grads, slot, dy_ref[slot].astype(F32) * alive)
    acts[slots] = jnp.zeros(acts.shape[1:], F32)
    grads[slots] = jnp.zeros(grads.shape[1:], F32)
    weights = taps_ref[...].astype(F32)
    step = 64 if lon_count % 64 == 0 else lon_count
    totals = [jnp.zeros((8, chans), F32)] * taps
    top = shift_ref.shape[0] - 1
    for slot in range(slots):
        below = jnp.where(slot + 1 < live, slot + 1, slots)
        sources = [(1, slot)]
        if slot > 0:
            sources.append((0, slot - 1))
        if slot + 1 < slots:
            sources.append((2, below))
        lat = jnp.clip(start + slot, 0, top)
        ahead, behind = [], []
        for offset, row in sources:
            other = jnp.clip(lat + offset - 1, 0, top)
            for column in range(3):
                t = 3 * offset + column
                ahead.append((t, row, REACH + shift_ref[lat, t]))
                t = 3 * (2 - offset) + column
                behind.append((t, row, REACH - shift_ref[other, t]))

        def inner(i, totals):
            at = pl.multiple_of(i * step, step)
            part = pl.ds(at, step)
            x = x_ref[slot, part, :].astype(F32)
            dy = grads[slot, pl.ds(pl.multiple_of(REACH + at, 8), step), :]
            out = x
            back = jnp.zeros((step, chans), F32)
            fresh = list(totals)
            for t, row, first in ahead:
                moved = acts[row, pl.ds(at + first, step), :]
                out = out + moved * weights[t : t + 1, :]
                fresh[t] = fresh[t] + folded(moved * dy)
            for t, row, first in behind:
                back = back + grads[row, pl.ds(at + first, step), :] * weights[t : t + 1, :]
            slope = gelu_slope(x)
            base_ref[slot, part, :] = out
            slope_ref[slot, part, :] = slope
            base_grad_ref[slot, part, :] = dy + back * slope
            return tuple(fresh)

        totals = list(lax.fori_loop(0, lon_count // step, inner, tuple(totals)))
    lines = [jnp.sum(total, axis=0, keepdims=True) for total in totals]
    lines.append(jnp.zeros((tap_ref.shape[0] - taps, chans), F32))
    tap_ref[...] = jnp.concatenate(lines, axis=0)


def rim_tap_kernel(
    blocks, rows_ref, shift_ref, dy_ref, first_rim, second_rim, inner_ref, tap_ref, acts,
):
    _, lon_count, chans = dy_ref.shape
    me = lax.axis_index("space")
    live = rows_ref[me]
    start = first_row_of(rows_ref, me, blocks)
    odd = jnp.bitwise_and(me, 1)
    for source, row in ((first_rim, 1 - odd), (second_rim, odd)):
        wrapped(acts, row, source[0].astype(F32))
    step = 256 if lon_count % 256 == 0 else lon_count
    top = shift_ref.shape[0] - 1
    lines = [jnp.zeros((1, chans), F32)] * tap_ref.shape[0]
    for side in range(2):
        slot = 0 if side == 0 else live - 1
        lat = jnp.clip(start + slot, 0, top)
        ahead = [(t, REACH + shift_ref[lat, t]) for t in range(6 * side, 6 * side + 3)]

        def rim(i, totals):
            at = pl.multiple_of(i * step, step)
            part = pl.ds(at, step)
            dy = dy_ref[slot, part, :].astype(F32)
            fresh = []
            for total, (t, first) in zip(totals, ahead):
                moved = acts[side, pl.ds(at + first, step), :]
                fresh.append(total + folded(moved * dy))
            return tuple(fresh)

        totals = lax.fori_loop(0, lon_count // step, rim, (jnp.zeros((8, chans), F32),) * 3)
        for (t, _), total in zip(ahead, totals):
            lines[t] = jnp.sum(total, axis=0, keepdims=True)
    tap_ref[...] = inner_ref[...] + jnp.concatenate(lines, axis=0)


def rim_kernel(
    blocks, rows_ref, shift_ref, first_rim, second_rim, taps_ref, rim_ref, rim_grad_ref, acts, grads,
):
    _, lon_count, chans = first_rim.shape
    me = lax.axis_index("space")
    live = rows_ref[me]
    start = first_row_of(rows_ref, me, blocks)
    odd = jnp.bitwise_and(me, 1)
    for source, row in ((first_rim, 1 - odd), (second_rim, odd)):
        wrapped(acts, row, source[0].astype(F32))
        wrapped(grads, row, source[1].astype(F32))
    weights = taps_ref[...].astype(F32)
    step = 128 if lon_count % 128 == 0 else lon_count
    top = shift_ref.shape[0] - 1
    for side in range(2):
        slot = 0 if side == 0 else live - 1
        lat = jnp.clip(start + slot, 0, top)
        other = jnp.clip(lat + 2 * side - 1, 0, top)
        ahead = [(t, REACH + shift_ref[lat, t]) for t in range(6 * side, 6 * side + 3)]
        behind = [(t, REACH - shift_ref[other, t]) for t in range(6 - 6 * side, 9 - 6 * side)]

        def rim(i, carry):
            at = pl.multiple_of(i * step, step)
            part = pl.ds(at, step)
            out = back = jnp.zeros((step, chans), F32)
            for t, first in ahead:
                moved = acts[side, pl.ds(at + first, step), :]
                out = out + moved * weights[t : t + 1, :]
            for t, first in behind:
                back = back + grads[side, pl.ds(at + first, step), :] * weights[t : t + 1, :]
            rim_ref[side, part, :] = out
            rim_grad_ref[side, part, :] = back
            return carry

        lax.fori_loop(0, lon_count // step, rim, 0)


def split_taps(taps, out_ref, count):
    high = taps.astype(BF16)
    out_ref[count : count + TAP_ROWS, :] = high
    out_ref[count + TAP_ROWS :, :] = (taps - high.astype(F32)).astype(BF16)


def joined_taps(rows):
    return rows[-2 * TAP_ROWS : -TAP_ROWS, :] + rows[-TAP_ROWS:, :]


def split_taps(taps, out_ref, count):
    high = taps.astype(BF16)
    out_ref[count : count + TAP_ROWS, :] = high
    out_ref[count + TAP_ROWS :, :] = (taps - high.astype(F32)).astype(BF16)


def joined_taps(ref):
    rows = ref[ref.shape[0] - 2 * TAP_ROWS :, :].astype(F32)
    return rows[:TAP_ROWS, :] + rows[TAP_ROWS:, :]


def added(first_ref, second_ref):
    return first_ref[...].astype(F32) + second_ref[...].astype(F32)


def quarter_kernel(kept_ref, first_ref, second_ref, third_ref, tap_ref, out_ref):
    total = kept_ref[...]
    for ref in (first_ref, second_ref, third_ref):
        total = total + ref[...].astype(F32)
    out_ref[: total.shape[0], :] = total.astype(BF16)
    split_taps(tap_ref[...], out_ref, total.shape[0])


def add_kernel(scale, tap_scale, own_ref, other_ref, out_ref):
    count = own_ref.shape[0] - 2 * TAP_ROWS
    out_ref[:count, :] = (added(own_ref, other_ref)[:count, :] / scale).astype(BF16)
    split_taps((joined_taps(own_ref) + joined_taps(other_ref)) / tap_scale, out_ref, count)


def early_kernel(
    rows_ref, table_ref, base_ref, slope_ref, base_grad_ref, rim_ref, rim_grad_ref,
    own_ref, near_ref, sum_ref, grad_ref,
):
    slots, lon_count, chans = base_ref.shape
    me = lax.axis_index("space")
    live = rows_ref[me]
    step = lon_count // 4
    for at in range(0, lon_count, step):
        rows = slice(at, at + step)
        sums = jnp.dot(table_ref[me, rows, :], own_ref[...], preferred_element_type=F32)
        sums = sums + jnp.dot(
            table_ref[jnp.bitwise_xor(me, 1), rows, :], near_ref[...], preferred_element_type=F32
        )
        for slot in range(slots):
            out = base_ref[slot, rows, :] + sums[:, slot * chans : (slot + 1) * chans]
            back = sums[:, (slots + slot) * chans : (slots + slot + 1) * chans]
            if slot == 0:
                out = out + rim_ref[0, rows, :]
                back = back + rim_grad_ref[0, rows, :]
            last = slot == live - 1
            out = out + jnp.where(last, rim_ref[1, rows, :], 0.0)
            back = back + jnp.where(last, rim_grad_ref[1, rows, :], 0.0)
            sum_ref[slot, rows, :] = out
            grad_ref[slot, rows, :] = base_grad_ref[slot, rows, :] + back * slope_ref[slot, rows, :]


def spread_kernel(*refs):
    quarters, (filter_ref, tap_ref, held) = refs[:4], refs[4:]
    share = filter_ref.shape[1] // 4
    for shift, ref in enumerate(quarters):
        quarter = jnp.bitwise_xor(own_quarter(), shift)
        at = pl.ds(pl.multiple_of(quarter * share, share), share)
        rows = ref[: 2 * share, :].astype(F32)
        filter_ref[0, at, :] = rows[:share, :]
        filter_ref[1, at, :] = rows[share:, :]
        held[quarter] = joined_taps(ref)
    taps = (held[0] + held[1]) + (held[2] + held[3])
    tap_ref[...] = taps[: tap_ref.shape[0], :]


def finish_kernel(
    blocks, rows_ref, table_ref, sum_ref, early_ref, slope_ref, *refs
):
    ins, refs = refs[: blocks - 2], refs[blocks - 2 :]
    out_hbm, grad_hbm, out_ref, grad_ref, sems = refs
    slots, lon_count, chans = sum_ref.shape
    me = lax.axis_index("space")
    live = rows_ref[me]
    stores = []
    parts = sems.shape[0] // (2 * slots)
    step = lon_count // parts
    for part in range(parts):
        rows = slice(part * step, (part + 1) * step)
        sums = jnp.zeros((step, 2 * slots * chans), F32)
        for at, ref in enumerate(ins):
            block = jnp.bitwise_xor(me, at + 2)
            sums = sums + jnp.dot(table_ref[block, rows, :], ref[...], preferred_element_type=F32)
        for slot in range(slots):
            out = sum_ref[slot, rows, :] + sums[:, slot * chans : (slot + 1) * chans]
            back = sums[:, (slots + slot) * chans : (slots + slot + 1) * chans]
            grad = early_ref[slot, rows, :] + back * slope_ref[slot, rows, :]
            alive = slot < live
            out_ref[slot, rows, :] = jnp.where(alive, out, 0.0).astype(BF16)
            grad_ref[slot, rows, :] = jnp.where(alive, grad, 0.0).astype(BF16)
            for made, target in ((out_ref, out_hbm), (grad_ref, grad_hbm)):
                place = (slot, pl.ds(part * step, step))
                stores.append(
                    pltpu.make_async_copy(made.at[place], target.at[place], sems.at[len(stores)])
                )
                stores[-1].start()
    for store in stores:
        store.wait()


def crossed(values, distance, axis="space"):
    count = lax.axis_size(axis)
    return lax.ppermute(values, axis, [(i, i ^ distance) for i in range(count)])


def around(parts):
    count = lax.axis_size("space") * lax.axis_size("ens")
    flip = lax.axis_size("ens") + 1
    return [
        crossed(parts[0], 1, "ens"),
        crossed(parts[1], 1),
        lax.ppermute(parts[2], ("space", "ens"), [(i, i ^ flip) for i in range(count)]),
    ]


def crossed_all(parts, distances):
    return {s: crossed(parts[s], s) for s in distances}


def body(
    fields, cotangent, band_rows, tap_shift, quad_weight, legendre, spectral_filter, tap_weight
):
    blocks = lax.axis_size("space")
    members = lax.axis_size("ens")
    _, slots, lon_count, chans = fields.shape
    local_modes, lat_count, degrees = legendre.shape
    padded_modes = round_up(local_modes, 16)
    depth = round_up(2 * local_modes, 8)
    pairs = len(lat_pairs(lat_count))
    pair_rows = round_up(pairs * padded_modes, 128)
    share = degrees // 2
    big = 32 if pair_rows <= 4096 else 60
    shape = jax.ShapeDtypeStruct
    table = fourier_table(lon_count, blocks, local_modes, depth)
    table_in = jnp.asarray(table)
    table_out = jnp.asarray(np.ascontiguousarray(table.transpose(0, 2, 1)))
    x, dy = fields[0], cotangent[0]
    field = shape((slots, lon_count, chans), F32)
    coded = shape((depth, 2 * slots * chans), BF16)
    rim = shape((2, lon_count, chans), BF16)

    coded_parts = call(
        functools.partial(forward_kernel, blocks),
        [coded] * blocks,
        [HBM] * 3,
        (x, dy, table_in),
        scratch=[
            pltpu.VMEM(x.shape, BF16),
            pltpu.VMEM(dy.shape, BF16),
            pltpu.VMEM(table.shape, BF16),
            pltpu.VMEM(x.shape, BF16),
            pltpu.SemaphoreType.DMA((3,)),
        ],
        limit=60,
        flops=2 * blocks * depth * lon_count * 2 * slots * chans,
    )
    far = list(range(blocks - 1, 0, -1))
    got = [coded_parts[0], *reversed(crossed_all(coded_parts, far).values())]
    leg_rows = jnp.pad(
        jnp.transpose(legendre, (1, 0, 2)), ((0, 0), (0, padded_modes - local_modes), (0, 0))
    )
    padded = (lon_count + 2 * REACH, chans)
    tap_shape = shape((TAP_ROWS, chans), F32)
    mixer, back, first_rim, second_rim, base, slope, base_grad, tap_part = call(
        functools.partial(prepare_kernel, local_modes, blocks),
        [shape((pair_rows, 2 * chans), F32), shape((degrees, pair_rows), BF16), rim, rim]
        + [field, field, field, tap_shape],
        [SMEM, SMEM] + [VMEM] * 5,
        (band_rows, tap_shift, leg_rows, spectral_filter, x, dy, tap_weight),
        scratch=[pltpu.VMEM((pair_rows, degrees), BF16), pltpu.VMEM(x.shape, BF16)]
        + [pltpu.VMEM((slots + 1, *padded), F32)] * 2,
        limit=big,
        flops=2 * pair_rows * degrees * 2 * chans,
        moved=8 * pair_rows * chans,
    )
    first_rim, second_rim, got[-1] = lax.optimization_barrier((first_rim, second_rim, got[-1]))
    first_rim = crossed(first_rim, 1)
    inner = [(i, i ^ 1) for i in range(blocks)]
    inner = [(i + 1, j + 1) for i, j in inner if max(i, j) + 1 < blocks]
    second_rim = lax.ppermute(second_rim, "space", inner)
    spectral = shape((lat_count, 2, padded_modes, chans), F32)
    keep, *sends, coeff, grad = call(
        functools.partial(gradient_kernel, blocks, slots, lat_count, local_modes),
        [shape((share, chans), F32)] + [shape((share, chans), BF16)] * 3 + [spectral] * 2,
        [SMEM, SMEM] + [VMEM] * (1 + blocks),
        (band_rows, quad_weight, back, *got),
        scratch=[
            pltpu.VMEM((pair_rows, 2 * chans), F32),
            pltpu.VMEM((degrees, 2 * chans), F32),
            pltpu.VMEM((blocks, depth + 8, 2 * slots * chans), F32),
        ],
        limit=big,
        flops=20 * degrees * pair_rows * 2 * chans,
    )
    got_sums = around(sends)
    back_parts = call(
        functools.partial(return_kernel, blocks, local_modes),
        [coded] * blocks,
        [SMEM, SMEM] + [VMEM] * 3,
        (band_rows, quad_weight, mixer, coeff, grad),
        scratch=[pltpu.VMEM(spectral.shape, F32)] * 2 + [pltpu.VMEM((depth + 8, 2 * slots * chans), F32)],
        limit=big,
    )
    tap_part = call(
        functools.partial(rim_tap_kernel, blocks),
        tap_shape,
        [SMEM, SMEM] + [VMEM] * 4,
        (band_rows, tap_shift, dy, first_rim, second_rim, tap_part),
        scratch=[pltpu.VMEM((2, *padded), F32)],
    )
    back_parts, tap_part = lax.optimization_barrier((back_parts, tap_part))
    message = shape((share + 2 * TAP_ROWS, chans), BF16)
    back_parts, tap_part = lax.optimization_barrier((back_parts, tap_part))
    own = call(quarter_kernel, message, [VMEM] * 5, (keep, *[got_sums[at] for at in (2, 0, 1)], tap_part))
    back_parts, own = lax.optimization_barrier((back_parts, own))
    returned = [back_parts[0], *reversed(crossed_all(back_parts, far).values())]
    steps = [(1 << bit, "space") for bit in range(1, blocks.bit_length() - 1)]
    steps += [(1 << bit, "ens") for bit in range(1, members.bit_length() - 1)]
    for at, (distance, axis) in enumerate(steps):
        scales = (members, members * lat_count) if at == len(steps) - 1 else (1, 1)
        own = call(
            functools.partial(add_kernel, *scales),
            message,
            [VMEM] * 2,
            (own, crossed(own, distance, axis)),
            flops=3900000000 if at == 0 else 0,
        )
    quarters = [own, *around([own] * 3)]
    rim_sum, rim_grad = call(
        functools.partial(rim_kernel, blocks),
        [shape((2, lon_count, chans), F32)] * 2,
        [SMEM, SMEM] + [VMEM] * 3,
        (band_rows, tap_shift, first_rim, second_rim, tap_weight),
        scratch=[pltpu.VMEM((2, *padded), F32)] * 2,
    )
    early_sum, early_grad = call(
        early_kernel,
        [field, field],
        [SMEM] + [VMEM] * 8,
        (band_rows, table_out, base, slope, base_grad, rim_sum, rim_grad, *returned[:2]),
    )
    quarters, early_sum = lax.optimization_barrier((quarters, early_sum))
    filter_grad, tap_grad = call(
        spread_kernel,
        [shape((2, degrees, chans), F32), shape((tap_weight.shape[0], chans), F32)],
        [VMEM] * 4,
        quarters,
        scratch=[pltpu.VMEM((4, TAP_ROWS, chans), F32)],
    )
    far_parts, filter_grad = lax.optimization_barrier((returned[2:], filter_grad))
    pieces = 4
    output, input_grad = call(
        functools.partial(finish_kernel, blocks),
        [shape(x.shape, BF16)] * 2,
        [SMEM] + [VMEM] * (2 + blocks),
        (band_rows, table_out, early_sum, early_grad, slope, *far_parts),
        scratch=[
            pltpu.VMEM(x.shape, BF16),
            pltpu.VMEM(x.shape, BF16),
            pltpu.SemaphoreType.DMA((2 * slots * pieces,)),
        ],
        flops=2 * blocks * depth * lon_count * 2 * slots * chans,
        out_specs=[HBM, HBM],
    )
    return (output[None], input_grad[None], filter_grad, tap_grad)


def solution(mesh):
    in_specs = (
        P(("groups", "ens"), "space", None, "chan"),
        P(("groups", "ens"), "space", None, "chan"),
        P("groups"),
        P(),
        P(),
        P("space", None, None),
        P(None, None, "chan"),
        P(None, "chan"),
    )
    out_specs = (
        P(("groups", "ens"), "space", None, "chan"),
        P(("groups", "ens"), "space", None, "chan"),
        P("groups", None, "chan"),
        P("groups", "chan"),
    )
    return jax.shard_map(body, mesh=mesh, in_specs=in_specs, out_specs=out_specs, check_vma=False)
```

```python
import functools
import math

import jax
import jax.numpy as jnp
import ml_dtypes
import numpy as np
from jax import lax
from jax.experimental import pallas as pl
from jax.experimental.pallas import tpu as pltpu
from jax.sharding import PartitionSpec as P

F32 = jnp.float32
BF16 = jnp.bfloat16
VMEM = pl.BlockSpec(memory_space=pltpu.VMEM)
SMEM = pl.BlockSpec(memory_space=pltpu.SMEM)
HBM = pl.BlockSpec(memory_space=pltpu.HBM)
REACH = 8
TAP_ROWS = 16


def gelu_value(values):
    return 0.5 * values * (1.0 + lax.erf(values * 0.7071067811865476))


def gelu_slope(values):
    return (
        0.5 * (1.0 + lax.erf(values * 0.7071067811865476))
        + values * jnp.exp(-0.5 * values * values) * 0.3989422804014327
    )


def round_up(count, step):
    return -(-count // step) * step


def fourier_table(lon_count, blocks, local_modes, depth):
    lon_ids = np.arange(lon_count)
    mode_ids = np.arange(blocks * local_modes)
    phase = (mode_ids[:, None] * lon_ids[None, :] % lon_count) * (2.0 * math.pi / lon_count)
    factor = 1.0 / math.sqrt(lon_count)
    both = np.stack([np.cos(phase), -np.sin(phase)]) * factor
    both = both.reshape(2, blocks, local_modes, lon_count).transpose(1, 0, 2, 3)
    both = both.reshape(blocks, 2 * local_modes, lon_count)
    both = np.pad(both, ((0, 0), (0, depth - 2 * local_modes), (0, 0)))
    return both.astype(ml_dtypes.bfloat16)


def lat_pairs(lat_count):
    return [(a, b) for a in range(lat_count) for b in range(a, lat_count)]


def first_row_of(rows_ref, block, blocks):
    total = jnp.int32(0)
    for other in range(blocks):
        total = total + jnp.where(other < block, rows_ref[other], 0)
    return total


def call(kernel, out_shape, in_specs, args, scratch=(), limit=32, flops=0, moved=1024, out_specs=None):
    return pl.pallas_call(
        kernel,
        out_shape=out_shape,
        in_specs=in_specs,
        out_specs=out_specs or jax.tree.map(lambda _: VMEM, out_shape),
        scratch_shapes=list(scratch),
        compiler_params=pltpu.CompilerParams(vmem_limit_bytes=limit * 1024 * 1024),
        cost_estimate=pl.CostEstimate(flops=flops, bytes_accessed=moved, transcendentals=0),
    )(*args)


def activate(x_ref, act_ref):
    slots, lon_count, _ = x_ref.shape
    step = 64 if lon_count % 64 == 0 else lon_count

    def run(i, carry):
        part = pl.ds(pl.multiple_of(i * step, step), step)
        for slot in range(slots):
            act_ref[slot, part, :] = gelu_value(x_ref[slot, part, :].astype(F32)).astype(BF16)
        return carry

    lax.fori_loop(0, lon_count // step, run, 0)


def forward_kernel(blocks, x_hbm, dy_hbm, table_hbm, *refs):
    outs, (x_ref, dy_ref, table_ref, act_ref, sems) = refs[:blocks], refs[blocks:]
    slots = x_ref.shape[0]
    me = lax.axis_index("space")
    loads = [
        pltpu.make_async_copy(source, target, sems.at[i])
        for i, (source, target) in enumerate(
            [(x_hbm, x_ref), (dy_hbm, dy_ref), (table_hbm, table_ref)]
        )
    ]
    for load in (loads[0], loads[2], loads[1]):
        load.start()
    loads[0].wait()
    activate(x_ref, act_ref)
    loads[1].wait()
    source = jnp.concatenate(
        [dy_ref[slot] for slot in range(slots)] + [act_ref[slot] for slot in range(slots)], axis=-1
    )
    loads[2].wait()
    for shift in range(blocks):
        block = jnp.bitwise_xor(me, shift)
        sums = jnp.dot(table_ref[block], source, preferred_element_type=F32)
        outs[shift][...] = sums.astype(BF16)


def wrapped(target, row, value):
    lon_count = value.shape[0]
    target[row, REACH : REACH + lon_count, :] = value
    target[row, :REACH, :] = value[lon_count - REACH :, :]
    target[row, REACH + lon_count :, :] = value[:REACH, :]


def folded(values):
    return jnp.sum(values.reshape(values.shape[0] // 8, 8, values.shape[1]), axis=0)


def prepare_kernel(
    local_modes, blocks, rows_ref, shift_ref, leg_ref, filter_ref, x_ref, dy_ref, taps_ref,
    mixer_ref, back_ref, first_rim, second_rim, base_ref, slope_ref, base_grad_ref, tap_ref,
    pairs_ref, act_ref, acts, grads,
):
    me = lax.axis_index("space")
    activate(x_ref, act_ref)
    last = rows_ref[me] - 1
    odd = jnp.bitwise_and(me, 1)
    for rim_ref, row in ((first_rim, last * (1 - odd)), (second_rim, last * odd)):
        rim_ref[0] = act_ref[row]
        rim_ref[1] = dy_ref[row]
    pair_products(local_modes, leg_ref, filter_ref, mixer_ref, back_ref, pairs_ref)
    disco_inner(
        blocks, rows_ref, shift_ref, x_ref, dy_ref, act_ref, taps_ref,
        base_ref, slope_ref, base_grad_ref, tap_ref, acts, grads,
    )


def pair_products(local_modes, leg_ref, filter_ref, mixer_ref, back_ref, pairs_ref):
    me = lax.axis_index("space")
    lat_count, padded_modes, _ = leg_ref.shape
    pairs = lat_pairs(lat_count)
    used = len(pairs) * padded_modes
    mode = me * local_modes + lax.broadcasted_iota(
        jnp.int32, (padded_modes, 1), 0
    )
    twice = jnp.where(mode == 0, 1.0, 2.0)
    for index, (a, b) in enumerate(pairs):
        at = index * padded_modes
        pairs_ref[at : at + padded_modes, :] = (
            leg_ref[a].astype(F32) * leg_ref[b].astype(F32) * twice
        ).astype(BF16)
    if pairs_ref.shape[0] > used:
        pairs_ref[used:, :] = jnp.zeros((pairs_ref.shape[0] - used, pairs_ref.shape[1]), BF16)
    both = jnp.concatenate([filter_ref[0], filter_ref[1]], axis=-1)
    mixer_ref[...] = jnp.dot(pairs_ref[...], both, preferred_element_type=F32)

    def turn(i, carry):
        part = pl.ds(pl.multiple_of(i * 128, 128), 128)
        back_ref[:, part] = pairs_ref[part, :].astype(F32).T.astype(BF16)
        return carry

    lax.fori_loop(0, pairs_ref.shape[0] // 128, turn, 0)


def own_quarter():
    space_bit = jnp.bitwise_and(lax.axis_index("space"), 1)
    return 2 * space_bit + jnp.bitwise_and(lax.axis_index("ens"), 1)


def gradient_kernel(blocks, slots, lat_count, local_modes, rows_ref, quad_ref, back_ref, *refs):
    ins, sums, coeff, grad = refs[:blocks], refs[blocks : blocks + 4], *refs[blocks + 4 : blocks + 6]
    products, gradient, wide = refs[blocks + 6 :]
    padded_modes, chans = coeff.shape[2:]
    me = lax.axis_index("space")
    pairs = lat_pairs(lat_count)
    whole = local_modes // 8 * 8
    if padded_modes > whole:
        zeros = jnp.zeros((padded_modes - whole, chans), F32)
        for lat in range(lat_count):
            for part in range(2):
                coeff[lat, part, whole:, :] = zeros
                grad[lat, part, whole:, :] = zeros

    for shift in range(blocks):
        block = jnp.bitwise_xor(me, shift)
        start = first_row_of(rows_ref, block, blocks)
        wide[shift, : ins[shift].shape[0], :] = ins[shift][...].astype(F32)
        for slot in range(slots):
            lat = jnp.minimum(start + slot, lat_count - 1)

            @pl.when(slot < rows_ref[block])
            def _():
                weight = quad_ref[lat]
                for part in range(2):
                    at = place(slots, local_modes, chans, 0, slot, part)
                    grad[lat, part, :local_modes, :] = wide[(shift, *at)]
                    at = place(slots, local_modes, chans, 1, slot, part)
                    coeff[lat, part, :local_modes, :] = wide[(shift, *at)] * weight

    def multiply(i, carry):
        rows = pl.ds(pl.multiple_of(i * 8, 8), 8)
        a0, a1, b0, b1 = loaded(coeff, grad, rows)
        for index, (a, b) in enumerate(pairs):
            at = pl.ds(pl.multiple_of(index * padded_modes + i * 8, 8), 8)
            h0 = h1 = jnp.zeros((8, chans), F32)
            for p, q in [(a, b)] if a == b else [(a, b), (b, a)]:
                h0 = h0 + b0[p] * a0[q] + b1[p] * a1[q]
                h1 = h1 + b1[p] * a0[q] - b0[p] * a1[q]
            products[at, :chans] = h0
            products[at, chans:] = h1
        return carry

    lax.fori_loop(0, padded_modes // 8, multiply, 0)
    used = len(pairs) * padded_modes
    if products.shape[0] > used:
        products[used:, :] = jnp.zeros((products.shape[0] - used, products.shape[1]), F32)
    gradient[...] = jnp.dot(
        back_ref[...], products[...].astype(BF16), preferred_element_type=F32
    )
    share = gradient.shape[0] // 4
    for shift, target in enumerate(sums):
        at = jnp.bitwise_xor(own_quarter(), shift) * share
        part = gradient[pl.ds(pl.multiple_of(at, share), share), :]
        both = jnp.concatenate([part[:, :chans], part[:, chans:]], axis=0)
        target[...] = both.astype(target.dtype)


def loaded(coeff, grad, rows):
    return [
        [ref[lat, part, rows, :] for lat in range(ref.shape[0])]
        for ref in (coeff, grad)
        for part in range(2)
    ]


def place(slots, local_modes, chans, field, slot, part):
    at = (field * slots + slot) * chans
    return slice(part * local_modes, (part + 1) * local_modes), slice(at, at + chans)


def return_kernel(blocks, local_modes, rows_ref, quad_ref, mixer_ref, coeff, grad, *refs):
    outs, (synth, grad_coeff, wide) = refs[:blocks], refs[blocks:]
    lat_count, _, padded_modes, chans = coeff.shape
    slots = wide.shape[1] // (2 * chans)
    me = lax.axis_index("space")
    pairs = lat_pairs(lat_count)

    def mix(i, carry):
        rows = pl.ds(pl.multiple_of(i * 8, 8), 8)
        a0, a1, b0, b1 = loaded(coeff, grad, rows)
        zero = jnp.zeros((8, chans), F32)
        y0, y1, z0, z1 = ([zero] * lat_count for _ in range(4))
        for index, (a, b) in enumerate(pairs):
            at = pl.ds(pl.multiple_of(index * padded_modes + i * 8, 8), 8)
            real = mixer_ref[at, :chans]
            imag = mixer_ref[at, chans:]
            for p, q in [(a, b)] if a == b else [(a, b), (b, a)]:
                y0[p] = y0[p] + real * a0[q] - imag * a1[q]
                y1[p] = y1[p] + imag * a0[q] + real * a1[q]
                z0[q] = z0[q] + real * b0[p] + imag * b1[p]
                z1[q] = z1[q] + real * b1[p] - imag * b0[p]
        for lat in range(lat_count):
            synth[lat, 0, rows, :] = y0[lat]
            synth[lat, 1, rows, :] = y1[lat]
            grad_coeff[lat, 0, rows, :] = z0[lat] * quad_ref[lat]
            grad_coeff[lat, 1, rows, :] = z1[lat] * quad_ref[lat]
        return carry

    lax.fori_loop(0, padded_modes // 8, mix, 0)
    whole = 2 * local_modes // 8 * 8
    wide[whole:, :] = jnp.zeros((wide.shape[0] - whole, wide.shape[1]), F32)
    for shift in range(blocks):
        block = jnp.bitwise_xor(me, shift)
        start = first_row_of(rows_ref, block, blocks)
        for slot in range(slots):
            lat = jnp.minimum(start + slot, lat_count - 1)
            for part in range(2):
                at = place(slots, local_modes, chans, 0, slot, part)
                wide[at] = synth[lat, part, :local_modes, :]
                at = place(slots, local_modes, chans, 1, slot, part)
                wide[at] = grad_coeff[lat, part, :local_modes, :]
        outs[shift][...] = wide[: outs[shift].shape[0], :].astype(BF16)


def disco_inner(
    blocks, rows_ref, shift_ref, x_ref, dy_ref, act_ref, taps_ref,
    base_ref, slope_ref, base_grad_ref, tap_ref, acts, grads,
):
    slots, lon_count, chans = x_ref.shape
    taps = taps_ref.shape[0]
    me = lax.axis_index("space")
    live = rows_ref[me]
    start = first_row_of(rows_ref, me, blocks)
    for slot in range(slots):
        alive = jnp.where(slot < live, 1.0, 0.0)
        wrapped(acts, slot, act_ref[slot].astype(F32))
        wrapped(grads, slot, dy_ref[slot].astype(F32) * alive)
    acts[slots] = jnp.zeros(acts.shape[1:], F32)
    grads[slots] = jnp.zeros(grads.shape[1:], F32)
    weights = taps_ref[...].astype(F32)
    step = 64 if lon_count % 64 == 0 else lon_count
    totals = [jnp.zeros((8, chans), F32)] * taps
    top = shift_ref.shape[0] - 1
    for slot in range(slots):
        below = jnp.where(slot + 1 < live, slot + 1, slots)
        sources = [(1, slot)]
        if slot > 0:
            sources.append((0, slot - 1))
        if slot + 1 < slots:
            sources.append((2, below))
        lat = jnp.clip(start + slot, 0, top)
        ahead, behind = [], []
        for offset, row in sources:
            other = jnp.clip(lat + offset - 1, 0, top)
            for column in range(3):
                t = 3 * offset + column
                ahead.append((t, row, REACH + shift_ref[lat, t]))
                t = 3 * (2 - offset) + column
                behind.append((t, row, REACH - shift_ref[other, t]))

        def inner(i, totals):
            at = pl.multiple_of(i * step, step)
            part = pl.ds(at, step)
            x = x_ref[slot, part, :].astype(F32)
            dy = grads[slot, pl.ds(pl.multiple_of(REACH + at, 8), step), :]
            out = x
            back = jnp.zeros((step, chans), F32)
            fresh = list(totals)
            for t, row, first in ahead:
                moved = acts[row, pl.ds(at + first, step), :]
                out = out + moved * weights[t : t + 1, :]
                fresh[t] = fresh[t] + folded(moved * dy)
            for t, row, first in behind:
                back = back + grads[row, pl.ds(at + first, step), :] * weights[t : t + 1, :]
            slope = gelu_slope(x)
            base_ref[slot, part, :] = out
            slope_ref[slot, part, :] = slope
            base_grad_ref[slot, part, :] = dy + back * slope
            return tuple(fresh)

        totals = list(lax.fori_loop(0, lon_count // step, inner, tuple(totals)))
    lines = [jnp.sum(total, axis=0, keepdims=True) for total in totals]
    lines.append(jnp.zeros((tap_ref.shape[0] - taps, chans), F32))
    tap_ref[...] = jnp.concatenate(lines, axis=0)


def rim_tap_kernel(
    blocks, rows_ref, shift_ref, dy_ref, first_rim, second_rim, inner_ref, tap_ref, acts,
):
    _, lon_count, chans = dy_ref.shape
    me = lax.axis_index("space")
    live = rows_ref[me]
    start = first_row_of(rows_ref, me, blocks)
    odd = jnp.bitwise_and(me, 1)
    for source, row in ((first_rim, 1 - odd), (second_rim, odd)):
        wrapped(acts, row, source[0].astype(F32))
    step = 256 if lon_count % 256 == 0 else lon_count
    top = shift_ref.shape[0] - 1
    lines = [jnp.zeros((1, chans), F32)] * tap_ref.shape[0]
    for side in range(2):
        slot = 0 if side == 0 else live - 1
        lat = jnp.clip(start + slot, 0, top)
        ahead = [(t, REACH + shift_ref[lat, t]) for t in range(6 * side, 6 * side + 3)]

        def rim(i, totals):
            at = pl.multiple_of(i * step, step)
            part = pl.ds(at, step)
            dy = dy_ref[slot, part, :].astype(F32)
            fresh = []
            for total, (t, first) in zip(totals, ahead):
                moved = acts[side, pl.ds(at + first, step), :]
                fresh.append(total + folded(moved * dy))
            return tuple(fresh)

        totals = lax.fori_loop(0, lon_count // step, rim, (jnp.zeros((8, chans), F32),) * 3)
        for (t, _), total in zip(ahead, totals):
            lines[t] = jnp.sum(total, axis=0, keepdims=True)
    tap_ref[...] = inner_ref[...] + jnp.concatenate(lines, axis=0)


def rim_kernel(
    blocks, rows_ref, shift_ref, first_rim, second_rim, taps_ref, rim_ref, rim_grad_ref, acts, grads,
):
    _, lon_count, chans = first_rim.shape
    me = lax.axis_index("space")
    live = rows_ref[me]
    start = first_row_of(rows_ref, me, blocks)
    odd = jnp.bitwise_and(me, 1)
    for source, row in ((first_rim, 1 - odd), (second_rim, odd)):
        wrapped(acts, row, source[0].astype(F32))
        wrapped(grads, row, source[1].astype(F32))
    weights = taps_ref[...].astype(F32)
    step = 128 if lon_count % 128 == 0 else lon_count
    top = shift_ref.shape[0] - 1
    for side in range(2):
        slot = 0 if side == 0 else live - 1
        lat = jnp.clip(start + slot, 0, top)
        other = jnp.clip(lat + 2 * side - 1, 0, top)
        ahead = [(t, REACH + shift_ref[lat, t]) for t in range(6 * side, 6 * side + 3)]
        behind = [(t, REACH - shift_ref[other, t]) for t in range(6 - 6 * side, 9 - 6 * side)]

        def rim(i, carry):
            at = pl.multiple_of(i * step, step)
            part = pl.ds(at, step)
            out = back = jnp.zeros((step, chans), F32)
            for t, first in ahead:
                moved = acts[side, pl.ds(at + first, step), :]
                out = out + moved * weights[t : t + 1, :]
            for t, first in behind:
                back = back + grads[side, pl.ds(at + first, step), :] * weights[t : t + 1, :]
            rim_ref[side, part, :] = out
            rim_grad_ref[side, part, :] = back
            return carry

        lax.fori_loop(0, lon_count // step, rim, 0)


def split_taps(taps, out_ref, count):
    high = taps.astype(BF16)
    out_ref[count : count + TAP_ROWS, :] = high
    out_ref[count + TAP_ROWS :, :] = (taps - high.astype(F32)).astype(BF16)


def joined_taps(rows):
    return rows[-2 * TAP_ROWS : -TAP_ROWS, :] + rows[-TAP_ROWS:, :]


def split_taps(taps, out_ref, count):
    high = taps.astype(BF16)
    out_ref[count : count + TAP_ROWS, :] = high
    out_ref[count + TAP_ROWS :, :] = (taps - high.astype(F32)).astype(BF16)


def joined_taps(ref):
    rows = ref[ref.shape[0] - 2 * TAP_ROWS :, :].astype(F32)
    return rows[:TAP_ROWS, :] + rows[TAP_ROWS:, :]


def added(first_ref, second_ref):
    return first_ref[...].astype(F32) + second_ref[...].astype(F32)


def quarter_kernel(kept_ref, first_ref, second_ref, third_ref, tap_ref, out_ref):
    total = kept_ref[...]
    for ref in (first_ref, second_ref, third_ref):
        total = total + ref[...].astype(F32)
    out_ref[: total.shape[0], :] = total.astype(BF16)
    split_taps(tap_ref[...], out_ref, total.shape[0])


def add_kernel(scale, tap_scale, own_ref, other_ref, out_ref):
    count = own_ref.shape[0] - 2 * TAP_ROWS
    out_ref[:count, :] = (added(own_ref, other_ref)[:count, :] / scale).astype(BF16)
    split_taps((joined_taps(own_ref) + joined_taps(other_ref)) / tap_scale, out_ref, count)


def early_kernel(
    rows_ref, table_ref, base_ref, slope_ref, base_grad_ref, rim_ref, rim_grad_ref,
    own_ref, near_ref, sum_ref, grad_ref,
):
    slots, lon_count, chans = base_ref.shape
    me = lax.axis_index("space")
    live = rows_ref[me]
    step = lon_count // 4
    for at in range(0, lon_count, step):
        rows = slice(at, at + step)
        sums = jnp.dot(table_ref[me, rows, :], own_ref[...], preferred_element_type=F32)
        sums = sums + jnp.dot(
            table_ref[jnp.bitwise_xor(me, 1), rows, :], near_ref[...], preferred_element_type=F32
        )
        for slot in range(slots):
            out = base_ref[slot, rows, :] + sums[:, slot * chans : (slot + 1) * chans]
            back = sums[:, (slots + slot) * chans : (slots + slot + 1) * chans]
            if slot == 0:
                out = out + rim_ref[0, rows, :]
                back = back + rim_grad_ref[0, rows, :]
            last = slot == live - 1
            out = out + jnp.where(last, rim_ref[1, rows, :], 0.0)
            back = back + jnp.where(last, rim_grad_ref[1, rows, :], 0.0)
            sum_ref[slot, rows, :] = out
            grad_ref[slot, rows, :] = base_grad_ref[slot, rows, :] + back * slope_ref[slot, rows, :]


def spread_kernel(*refs):
    quarters, (filter_ref, tap_ref, held) = refs[:4], refs[4:]
    share = filter_ref.shape[1] // 4
    for shift, ref in enumerate(quarters):
        quarter = jnp.bitwise_xor(own_quarter(), shift)
        at = pl.ds(pl.multiple_of(quarter * share, share), share)
        rows = ref[: 2 * share, :].astype(F32)
        filter_ref[0, at, :] = rows[:share, :]
        filter_ref[1, at, :] = rows[share:, :]
        held[quarter] = joined_taps(ref)
    taps = (held[0] + held[1]) + (held[2] + held[3])
    tap_ref[...] = taps[: tap_ref.shape[0], :]


def finish_kernel(
    blocks, rows_ref, table_ref, sum_ref, early_ref, slope_ref, *refs
):
    ins, refs = refs[: blocks - 2], refs[blocks - 2 :]
    out_hbm, grad_hbm, out_ref, grad_ref, sems = refs
    slots, lon_count, chans = sum_ref.shape
    me = lax.axis_index("space")
    live = rows_ref[me]
    stores = []
    parts = sems.shape[0] // (2 * slots)
    step = lon_count // parts
    for part in range(parts):
        rows = slice(part * step, (part + 1) * step)
        sums = jnp.zeros((step, 2 * slots * chans), F32)
        for at, ref in enumerate(ins):
            block = jnp.bitwise_xor(me, at + 2)
            sums = sums + jnp.dot(table_ref[block, rows, :], ref[...], preferred_element_type=F32)
        for slot in range(slots):
            out = sum_ref[slot, rows, :] + sums[:, slot * chans : (slot + 1) * chans]
            back = sums[:, (slots + slot) * chans : (slots + slot + 1) * chans]
            grad = early_ref[slot, rows, :] + back * slope_ref[slot, rows, :]
            alive = slot < live
            out_ref[slot, rows, :] = jnp.where(alive, out, 0.0).astype(BF16)
            grad_ref[slot, rows, :] = jnp.where(alive, grad, 0.0).astype(BF16)
            for made, target in ((out_ref, out_hbm), (grad_ref, grad_hbm)):
                place = (slot, pl.ds(part * step, step))
                stores.append(
                    pltpu.make_async_copy(made.at[place], target.at[place], sems.at[len(stores)])
                )
                stores[-1].start()
    for store in stores:
        store.wait()


def crossed(values, distance, axis="space"):
    count = lax.axis_size(axis)
    return lax.ppermute(values, axis, [(i, i ^ distance) for i in range(count)])


def around(parts):
    count = lax.axis_size("space") * lax.axis_size("ens")
    flip = lax.axis_size("ens") + 1
    return [
        crossed(parts[0], 1, "ens"),
        crossed(parts[1], 1),
        lax.ppermute(parts[2], ("space", "ens"), [(i, i ^ flip) for i in range(count)]),
    ]


def crossed_all(parts, distances):
    return {s: crossed(parts[s], s) for s in distances}


def body(
    fields, cotangent, band_rows, tap_shift, quad_weight, legendre, spectral_filter, tap_weight
):
    blocks = lax.axis_size("space")
    members = lax.axis_size("ens")
    _, slots, lon_count, chans = fields.shape
    local_modes, lat_count, degrees = legendre.shape
    padded_modes = round_up(local_modes, 16)
    depth = round_up(2 * local_modes, 8)
    pairs = len(lat_pairs(lat_count))
    pair_rows = round_up(pairs * padded_modes, 128)
    share = degrees // 2
    big = 32 if pair_rows <= 4096 else 60
    shape = jax.ShapeDtypeStruct
    table = fourier_table(lon_count, blocks, local_modes, depth)
    table_in = jnp.asarray(table)
    table_out = jnp.asarray(np.ascontiguousarray(table.transpose(0, 2, 1)))
    x, dy = fields[0], cotangent[0]
    field = shape((slots, lon_count, chans), F32)
    coded = shape((depth, 2 * slots * chans), BF16)
    rim = shape((2, lon_count, chans), BF16)

    coded_parts = call(
        functools.partial(forward_kernel, blocks),
        [coded] * blocks,
        [HBM] * 3,
        (x, dy, table_in),
        scratch=[
            pltpu.VMEM(x.shape, BF16),
            pltpu.VMEM(dy.shape, BF16),
            pltpu.VMEM(table.shape, BF16),
            pltpu.VMEM(x.shape, BF16),
            pltpu.SemaphoreType.DMA((3,)),
        ],
        limit=60,
        flops=2 * blocks * depth * lon_count * 2 * slots * chans,
    )
    far = list(range(blocks - 1, 0, -1))
    got = [coded_parts[0], *reversed(crossed_all(coded_parts, far).values())]
    leg_rows = jnp.pad(
        jnp.transpose(legendre, (1, 0, 2)), ((0, 0), (0, padded_modes - local_modes), (0, 0))
    )
    padded = (lon_count + 2 * REACH, chans)
    tap_shape = shape((TAP_ROWS, chans), F32)
    mixer, back, first_rim, second_rim, base, slope, base_grad, tap_part = call(
        functools.partial(prepare_kernel, local_modes, blocks),
        [shape((pair_rows, 2 * chans), F32), shape((degrees, pair_rows), BF16), rim, rim]
        + [field, field, field, tap_shape],
        [SMEM, SMEM] + [VMEM] * 5,
        (band_rows, tap_shift, leg_rows, spectral_filter, x, dy, tap_weight),
        scratch=[pltpu.VMEM((pair_rows, degrees), BF16), pltpu.VMEM(x.shape, BF16)]
        + [pltpu.VMEM((slots + 1, *padded), F32)] * 2,
        limit=big,
        flops=2 * pair_rows * degrees * 2 * chans,
        moved=8 * pair_rows * chans,
    )
    first_rim, second_rim, got[-1] = lax.optimization_barrier((first_rim, second_rim, got[-1]))
    first_rim = crossed(first_rim, 1)
    inner = [(i, i ^ 1) for i in range(blocks)]
    inner = [(i + 1, j + 1) for i, j in inner if max(i, j) + 1 < blocks]
    second_rim = lax.ppermute(second_rim, "space", inner)
    spectral = shape((lat_count, 2, padded_modes, chans), F32)
    keep, *sends, coeff, grad = call(
        functools.partial(gradient_kernel, blocks, slots, lat_count, local_modes),
        [shape((share, chans), F32)] + [shape((share, chans), BF16)] * 3 + [spectral] * 2,
        [SMEM, SMEM] + [VMEM] * (1 + blocks),
        (band_rows, quad_weight, back, *got),
        scratch=[
            pltpu.VMEM((pair_rows, 2 * chans), F32),
            pltpu.VMEM((degrees, 2 * chans), F32),
            pltpu.VMEM((blocks, depth + 8, 2 * slots * chans), F32),
        ],
        limit=big,
        flops=20 * degrees * pair_rows * 2 * chans,
    )
    got_sums = around(sends)
    back_parts = call(
        functools.partial(return_kernel, blocks, local_modes),
        [coded] * blocks,
        [SMEM, SMEM] + [VMEM] * 3,
        (band_rows, quad_weight, mixer, coeff, grad),
        scratch=[pltpu.VMEM(spectral.shape, F32)] * 2 + [pltpu.VMEM((depth + 8, 2 * slots * chans), F32)],
        limit=big,
    )
    tap_part = call(
        functools.partial(rim_tap_kernel, blocks),
        tap_shape,
        [SMEM, SMEM] + [VMEM] * 4,
        (band_rows, tap_shift, dy, first_rim, second_rim, tap_part),
        scratch=[pltpu.VMEM((2, *padded), F32)],
    )
    back_parts, tap_part = lax.optimization_barrier((back_parts, tap_part))
    message = shape((share + 2 * TAP_ROWS, chans), BF16)
    back_parts, tap_part = lax.optimization_barrier((back_parts, tap_part))
    own = call(quarter_kernel, message, [VMEM] * 5, (keep, *[got_sums[at] for at in (2, 1, 0)], tap_part))
    back_parts, own = lax.optimization_barrier((back_parts, own))
    returned = [back_parts[0], *reversed(crossed_all(back_parts, far).values())]
    steps = [(1 << bit, "space") for bit in range(1, blocks.bit_length() - 1)]
    steps += [(1 << bit, "ens") for bit in range(1, members.bit_length() - 1)]
    for at, (distance, axis) in enumerate(steps):
        scales = (members, members * lat_count) if at == len(steps) - 1 else (1, 1)
        own = call(
            functools.partial(add_kernel, *scales),
            message,
            [VMEM] * 2,
            (own, crossed(own, distance, axis)),
            flops=3900000000 if at == 0 else 0,
        )
    quarters = [own, *around([own] * 3)]
    rim_sum, rim_grad = call(
        functools.partial(rim_kernel, blocks),
        [shape((2, lon_count, chans), F32)] * 2,
        [SMEM, SMEM] + [VMEM] * 3,
        (band_rows, tap_shift, first_rim, second_rim, tap_weight),
        scratch=[pltpu.VMEM((2, *padded), F32)] * 2,
    )
    early_sum, early_grad = call(
        early_kernel,
        [field, field],
        [SMEM] + [VMEM] * 8,
        (band_rows, table_out, base, slope, base_grad, rim_sum, rim_grad, *returned[:2]),
    )
    quarters, early_sum = lax.optimization_barrier((quarters, early_sum))
    filter_grad, tap_grad = call(
        spread_kernel,
        [shape((2, degrees, chans), F32), shape((tap_weight.shape[0], chans), F32)],
        [VMEM] * 4,
        quarters,
        scratch=[pltpu.VMEM((4, TAP_ROWS, chans), F32)],
    )
    far_parts, filter_grad = lax.optimization_barrier((returned[2:], filter_grad))
    pieces = 4
    output, input_grad = call(
        functools.partial(finish_kernel, blocks),
        [shape(x.shape, BF16)] * 2,
        [SMEM] + [VMEM] * (2 + blocks),
        (band_rows, table_out, early_sum, early_grad, slope, *far_parts),
        scratch=[
            pltpu.VMEM(x.shape, BF16),
            pltpu.VMEM(x.shape, BF16),
            pltpu.SemaphoreType.DMA((2 * slots * pieces,)),
        ],
        flops=2 * blocks * depth * lon_count * 2 * slots * chans,
        out_specs=[HBM, HBM],
    )
    return (output[None], input_grad[None], filter_grad, tap_grad)


def solution(mesh):
    in_specs = (
        P(("groups", "ens"), "space", None, "chan"),
        P(("groups", "ens"), "space", None, "chan"),
        P("groups"),
        P(),
        P(),
        P("space", None, None),
        P(None, None, "chan"),
        P(None, "chan"),
    )
    out_specs = (
        P(("groups", "ens"), "space", None, "chan"),
        P(("groups", "ens"), "space", None, "chan"),
        P("groups", None, "chan"),
        P("groups", "chan"),
    )
    return jax.shard_map(body, mesh=mesh, in_specs=in_specs, out_specs=out_specs, check_vma=False)
```
